32 devices in a mesh: groups: 2 (over y), row: 8 (over z, core), col: 2 (over x).
Axes of the slice: x: 2, y: 2, z: 4, core: 2. Of those that a mesh axis runs over, the one named last changes fastest.
Arguments:
- pair_repr: bfloat16 [256, 128, 128], P(('groups', 'row'), 'col'), parts along dimension 0, may hold values from -6 to 6
- distance_bins: int32 [256, 128], P(('groups', 'row'), 'col'), parts along dimension 0, may hold values from 0 to 63
- chain_lengths: int32 [10], P('groups'), parts along dimension 0, may hold values from 1 to 64, 128 in all
- left_weight: bfloat16 [128, 128], replicated, may hold values from -0.5 to 0.5
- left_gate_weight: bfloat16 [128, 128], replicated, may hold values from -0.5 to 0.5
- right_weight: bfloat16 [128, 128], replicated, may hold values from -0.5 to 0.5
- right_gate_weight: bfloat16 [128, 128], replicated, may hold values from -0.5 to 0.5
- out_weight: bfloat16 [128, 128], replicated, may hold values from -0.5 to 0.5
- out_gate_weight: bfloat16 [128, 128], replicated, may hold values from -0.5 to 0.5
- dist_weight: bfloat16 [128, 64], replicated, may hold values from -1.59375 to 1.59375
Outputs:
- pair_out: bfloat16 [256, 128, 128], P(('groups', 'row'), 'col'), parts along dimension 0
- loss_value: float32 [2], P('groups'), parts along dimension 0
The draws below stay inside these ranges and needn't reach their ends.
There are 2 independent parts, one for each index of `groups`. The reference program is written for one: setup_inputs(seed, part) draws one part's arguments, and reference() takes and returns one part's arrays. A program takes and returns all parts, laid end to end along the dimension named above; an argument that names none is the same for every part. Nothing has to cross between parts.
Inputs may be any that keep to these rules, and one draw needn't show every extreme that they name: chain_lengths holds 4 chain lengths followed by the count of padding residues at the end of the complex; the entries sum to 128.
All inputs are finite; a program needn't handle non-finite values.
Results may differ from the reference program's by a relative error of at most 0.0048.
Values may be sent and summed in bfloat16 or wider, within the bound.
No kernel may reach another device: no remote copies, remote signals or barrier semaphores. Data moves between devices by JAX's collectives and lax.ppermute only.
A program may use at most 64 MiB of HBM per device.

```python
import math
import jax
import jax.numpy as jnp
import numpy as np
from jax import lax

C = 128
BINS = 64
CHAINS = 4
N = 128


def set_ends(array, rng, smallest, high):
    dims = array.shape
    index_at = [jax.random.randint(jax.random.fold_in(rng, axis), (), 0, dims[axis]) for axis in range(len(dims))]
    array = array.at[tuple(index_at)].set(smallest)
    longest = dims.index(max(dims))
    index_at[longest] = (index_at[longest] + 1) % dims[longest]
    return array.at[tuple(index_at)].set(high)


def block_levels(stream_key, extent, cuts, least, largest):
    gain = 1.0
    for axis_at, blocks in cuts:
        heights = jax.random.uniform(jax.random.fold_in(jax.random.fold_in(stream_key, 6), axis_at), (blocks,), jnp.float32, least / len(cuts), largest / len(cuts))
        gain = gain * jnp.repeat(jnp.exp(heights), extent[axis_at] // blocks).reshape((-1,) + (1,) * (len(extent) - 1 - axis_at))
    return gain


def profile(count, total, bound, skew):
    portions = [(1 << 20) // math.isqrt(rank ** skew) + 1 for rank in range(2, count + 1)]
    rest, given = total - bound - (count - 1), [1] * (count - 1)
    while rest > 0:
        candidates = [i for i in range(count - 1) if given[i] < bound]
        pool, left = sum([portions[i] for i in candidates]), rest
        for i in candidates:
            addition = min(bound - given[i], max(1, left * portions[i] // pool), rest)
            given[i] = given[i] + addition
            rest = rest - addition
    return np.array([bound] + given)


def uneven_parts(key, amount, total, most, lean):
    if amount == 2:
        one = jax.random.randint(key, (), max(1, total - most), min(most, total - 1) + 1)
        return jnp.stack([one, total - one])
    sizes = jnp.asarray(profile(amount, total, most, lean), jnp.int32)
    pairs = (amount - 1) // 2
    giver, sink = sizes[1:1 + 2 * pairs:2], sizes[2:2 + 2 * pairs:2]
    slack = jnp.minimum(giver - 1, most - sink)
    shifted = jax.random.randint(jax.random.fold_in(key, 1), (pairs,), 0, 1 << 20) % (slack + 1)
    sizes = sizes.at[1:1 + 2 * pairs:2].set(giver - shifted).at[2:2 + 2 * pairs:2].set(sink + shifted)
    return sizes[jax.random.permutation(jax.random.fold_in(key, 2), amount)]


def normal_values(key, extent, deviation, reach, cuts=(), held_as=jnp.bfloat16):
    drawn = deviation * jax.random.normal(key, extent, jnp.float32)
    if cuts:
        drawn = drawn * block_levels(key, extent, cuts, -0.22, 0.18)
    return jnp.clip(drawn, -reach, reach).astype(held_as)


def setup_inputs(seed: int = 0, part: int = 0) -> dict:
    splits = jax.random.split(jax.random.key(seed), 11)
    part_keys = jax.random.split(jax.random.fold_in(splits[10], part), 11)
    return {
        "pair_repr": normal_values(part_keys[0], (N, N, C), 1.0, 6.0, ((0, 8), (1, 2))),
        "distance_bins": set_ends(jax.random.randint(part_keys[1], (N, N), 0, BINS), jax.random.fold_in(part_keys[1], 1), 0, BINS - 1).astype(jnp.int32),
        "chain_lengths": uneven_parts(part_keys[2], CHAINS + 1, N, N // 2, 0).astype(jnp.int32),
        "left_weight": normal_values(splits[3], (C, C), C ** -0.5, 0.5),
        "left_gate_weight": normal_values(splits[4], (C, C), C ** -0.5, 0.5),
        "right_weight": normal_values(splits[5], (C, C), C ** -0.5, 0.5),
        "right_gate_weight": normal_values(splits[6], (C, C), C ** -0.5, 0.5),
        "out_weight": normal_values(splits[7], (C, C), C ** -0.5, 0.5),
        "out_gate_weight": normal_values(splits[8], (C, C), C ** -0.5, 0.5),
        "dist_weight": normal_values(splits[9], (C, BINS), 0.27, 1.59375),
    }


def layer_norm(values):
    average = lax.optimization_barrier(jnp.mean(values, axis=-1, keepdims=True))
    centred = values - average
    spread = lax.optimization_barrier(jnp.mean(centred * centred, axis=-1, keepdims=True))
    return centred * lax.rsqrt(spread + 1e-05)

def reference(pair_repr, distance_bins, chain_lengths, left_weight, left_gate_weight, right_weight, right_gate_weight, out_weight, out_gate_weight, dist_weight):
    residues = pair_repr.shape[0]
    channels = pair_repr.shape[2]
    live_count = residues - chain_lengths[CHAINS]
    live_rows = (jnp.arange(residues, dtype=jnp.int32) < live_count).astype(jnp.float32)
    pair_mask = live_rows[:, None] * live_rows[None, :]
    normed = layer_norm(pair_repr.astype(jnp.float32)).astype(jnp.bfloat16).reshape(-1, channels)

    def project(weight):
        return jnp.dot(normed, weight, preferred_element_type=jnp.float32).reshape(residues, residues, -1)
    left = (jax.nn.sigmoid(project(left_gate_weight)) * project(left_weight) * pair_mask[:, :, None]).astype(jnp.bfloat16)
    right = (jax.nn.sigmoid(project(right_gate_weight)) * project(right_weight) * pair_mask[:, :, None]).astype(jnp.bfloat16)
    left_major = left.astype(jnp.float32).transpose(2, 0, 1)
    right_major = right.astype(jnp.float32).transpose(2, 0, 1)
    tri = jnp.einsum('cik,cjk->cij', left_major, right_major, precision=lax.Precision.HIGHEST).transpose(1, 2, 0)
    tri_normed = layer_norm(tri).astype(jnp.bfloat16).reshape(-1, channels)
    out_gate = jax.nn.sigmoid(project(out_gate_weight))
    update = out_gate * jnp.dot(tri_normed, out_weight, preferred_element_type=jnp.float32).reshape(residues, residues, -1)
    pair_out = (pair_repr.astype(jnp.float32) + update).astype(jnp.bfloat16)
    logits = jnp.dot(pair_out.reshape(-1, channels), dist_weight, preferred_element_type=jnp.float32)
    log_total = jnp.log(lax.optimization_barrier(jnp.sum(jnp.exp(logits), axis=-1)))
    picked = jnp.take_along_axis(logits, distance_bins.reshape(-1, 1).astype(jnp.int32), axis=1)[:, 0]
    cross_entropy = log_total - picked
    flat_mask = pair_mask.reshape(-1)
    loss_value = jnp.sum(flat_mask * cross_entropy) / jnp.sum(flat_mask)
    return (pair_out, loss_value.reshape(1))
```

```python
import jax
import jax.numpy as jnp
from jax import lax
from jax.sharding import PartitionSpec as P

AXES = ("row", "col")


def layer_norm(values, axis):
    average = jnp.mean(values, axis=axis, keepdims=True)
    centred = values - average
    spread = jnp.mean(centred * centred, axis=axis, keepdims=True)
    return centred * lax.rsqrt(spread + 1e-05)


def on_device(
    pair_repr,
    distance_bins,
    chain_lengths,
    left_weight,
    left_gate_weight,
    right_weight,
    right_gate_weight,
    out_weight,
    out_gate_weight,
    dist_weight,
):
    tile_rows, tile_cols, channels = pair_repr.shape
    rows, cols = lax.axis_size("row"), lax.axis_size("col")
    peers = rows * cols
    share = channels // peers
    residues = tile_rows * rows
    spots = tile_rows * tile_cols
    live_count = residues - chain_lengths[chain_lengths.shape[0] - 1]
    row_place = lax.axis_index("row") * tile_rows + jnp.arange(tile_rows, dtype=jnp.int32)
    col_place = lax.axis_index("col") * tile_cols + jnp.arange(tile_cols, dtype=jnp.int32)
    live_rows = (row_place < live_count).astype(jnp.float32)
    live_cols = (col_place < live_count).astype(jnp.float32)
    flat_mask = (live_rows[:, None] * live_cols[None, :]).reshape(-1)
    normed = layer_norm(pair_repr.astype(jnp.float32), -1).astype(jnp.bfloat16)
    normed = normed.reshape(spots, channels)

    def project_turned(weight):
        return lax.dot_general(
            weight, normed, (((0,), (1,)), ((), ())), preferred_element_type=jnp.float32
        )

    def gated(gate_weight, weight):
        values = jax.nn.sigmoid(project_turned(gate_weight)) * project_turned(weight)
        return (values * flat_mask[None, :]).astype(jnp.bfloat16)

    left = gated(left_gate_weight, left_weight).reshape(peers, share, tile_rows, tile_cols)
    right = gated(right_gate_weight, right_weight).reshape(peers, share, tile_rows, tile_cols)
    both = jnp.concatenate([left, right], axis=3).reshape(peers, share * tile_rows, 2 * tile_cols)
    owned = lax.all_to_all(both, AXES, split_axis=0, concat_axis=0, tiled=True)
    owned = owned.reshape(rows, cols, share, tile_rows, 2, tile_cols)
    owned = owned.transpose(4, 2, 0, 3, 1, 5).reshape(2, share, residues, residues)
    tri = jnp.einsum(
        "cik,cjk->cij", owned[0], owned[1], preferred_element_type=jnp.float32
    ).astype(jnp.bfloat16)
    tri = tri.reshape(share, rows, tile_rows, cols, tile_cols).transpose(1, 3, 0, 2, 4)
    tri = tri.reshape(peers, share, spots)
    tri = lax.all_to_all(tri, AXES, split_axis=0, concat_axis=0, tiled=True)
    tri = tri.reshape(channels, spots).astype(jnp.float32)
    tri_normed = layer_norm(tri, 0).astype(jnp.bfloat16)
    out_gate = jax.nn.sigmoid(jnp.dot(normed, out_gate_weight, preferred_element_type=jnp.float32))
    update = out_gate * lax.dot_general(
        tri_normed, out_weight, (((0,), (0,)), ((), ())), preferred_element_type=jnp.float32
    )
    pair_out = (pair_repr.astype(jnp.float32).reshape(spots, channels) + update).astype(
        jnp.bfloat16
    )
    logits = jnp.dot(pair_out, dist_weight, preferred_element_type=jnp.float32)
    log_total = jnp.log(jnp.sum(jnp.exp(logits), axis=-1))
    bin_ids = jnp.arange(logits.shape[1], dtype=jnp.int32)
    picked = jnp.sum(
        jnp.where(bin_ids[None, :] == distance_bins.reshape(-1, 1), logits, 0.0), axis=-1
    )
    loss_sum = jnp.sum(flat_mask * (log_total - picked))
    sums = lax.all_to_all(
        jnp.full((peers, 1, 128), loss_sum), AXES, split_axis=0, concat_axis=0, tiled=True
    )
    pair_count = (live_count * live_count).astype(jnp.float32)
    loss_value = (jnp.sum(sums[:, 0, 0]) / pair_count).reshape(1)
    return (pair_out.reshape(pair_repr.shape), loss_value)


def solution(mesh):
    in_specs = (
        P(("groups", "row"), "col", None),
        P(("groups", "row"), "col"),
        P("groups"),
        P(),
        P(),
        P(),
        P(),
        P(),
        P(),
        P(),
    )
    out_specs = (P(("groups", "row"), "col", None), P("groups"))
    return jax.shard_map(
        on_device, mesh=mesh, in_specs=in_specs, out_specs=out_specs, check_vma=False
    )
```

```python
import jax
import jax.numpy as jnp
from jax import lax
from jax.sharding import PartitionSpec as P

AXES = ("row", "col")


def layer_norm(values, axis):
    average = jnp.mean(values, axis=axis, keepdims=True)
    centred = values - average
    spread = jnp.mean(centred * centred, axis=axis, keepdims=True)
    return centred * lax.rsqrt(spread + 1e-05)


def on_device(
    pair_repr,
    distance_bins,
    chain_lengths,
    left_weight,
    left_gate_weight,
    right_weight,
    right_gate_weight,
    out_weight,
    out_gate_weight,
    dist_weight,
):
    tile_rows, tile_cols, channels = pair_repr.shape
    rows, cols = lax.axis_size("row"), lax.axis_size("col")
    peers = rows * cols
    share = channels // peers
    residues = tile_rows * rows
    spots = tile_rows * tile_cols
    live_count = residues - chain_lengths[chain_lengths.shape[0] - 1]
    row_place = lax.axis_index("row") * tile_rows + jnp.arange(tile_rows, dtype=jnp.int32)
    col_place = lax.axis_index("col") * tile_cols + jnp.arange(tile_cols, dtype=jnp.int32)
    live_rows = (row_place < live_count).astype(jnp.float32)
    live_cols = (col_place < live_count).astype(jnp.float32)
    flat_mask = (live_rows[:, None] * live_cols[None, :]).reshape(-1)
    normed = layer_norm(pair_repr.astype(jnp.float32), -1).astype(jnp.bfloat16)
    normed = normed.reshape(spots, channels)

    def project_turned(weight):
        return lax.dot_general(
            weight, normed, (((0,), (1,)), ((), ())), preferred_element_type=jnp.float32
        )

    def gated(gate_weight, weight):
        values = jax.nn.sigmoid(project_turned(gate_weight)) * project_turned(weight)
        return (values * flat_mask[None, :]).astype(jnp.bfloat16)

    left = gated(left_gate_weight, left_weight).reshape(peers, share, tile_rows, tile_cols)
    right = gated(right_gate_weight, right_weight).reshape(peers, share, tile_rows, tile_cols)
    both = jnp.concatenate([left, right], axis=3).reshape(peers, share * tile_rows, 2 * tile_cols)
    owned = lax.all_to_all(both, AXES, split_axis=0, concat_axis=0, tiled=True)
    owned = owned.reshape(rows, cols, share, tile_rows, 2, tile_cols)
    owned = owned.transpose(4, 2, 0, 3, 1, 5).reshape(2, share, residues, residues)
    tri = jnp.einsum(
        "cik,cjk->cij", owned[0], owned[1], preferred_element_type=jnp.float32
    ).astype(jnp.bfloat16)
    tri = tri.reshape(share, rows, tile_rows, cols, tile_cols).transpose(1, 3, 0, 2, 4)
    tri = tri.reshape(peers, share, spots)
    tri = lax.all_to_all(tri, AXES, split_axis=0, concat_axis=0, tiled=True)
    tri = tri.reshape(channels, spots).astype(jnp.float32)
    tri_normed = layer_norm(tri, 0).astype(jnp.bfloat16)
    out_gate = jax.nn.sigmoid(jnp.dot(normed, out_gate_weight, preferred_element_type=jnp.float32))
    update = out_gate * lax.dot_general(
        tri_normed, out_weight, (((0,), (0,)), ((), ())), preferred_element_type=jnp.float32
    )
    pair_out = (pair_repr.astype(jnp.float32).reshape(spots, channels) + update).astype(
        jnp.bfloat16
    )
    logits = jnp.dot(pair_out, dist_weight, preferred_element_type=jnp.float32)
    log_total = jnp.log(jnp.sum(jnp.exp(logits), axis=-1))
    bin_ids = jnp.arange(logits.shape[1], dtype=jnp.int32)
    picked = jnp.sum(
        jnp.where(bin_ids[None, :] == distance_bins.reshape(-1, 1), logits, 0.0), axis=-1
    )
    loss_sum = jnp.sum(flat_mask * (log_total - picked))
    total = jnp.full((1, 128), loss_sum)
    for axis, size in (("col", cols), ("row", rows)):
        step = 1
        while step < size:
            total = total + lax.ppermute(total, axis, [(at, at ^ step) for at in range(size)])
            step *= 2
    pair_count = (live_count * live_count).astype(jnp.float32)
    loss_value = total[0, :1] / pair_count
    return (pair_out.reshape(pair_repr.shape), loss_value)


def solution(mesh):
    in_specs = (
        P(("groups", "row"), "col", None),
        P(("groups", "row"), "col"),
        P("groups"),
        P(),
        P(),
        P(),
        P(),
        P(),
        P(),
        P(),
    )
    out_specs = (P(("groups", "row"), "col", None), P("groups"))
    return jax.shard_map(
        on_device, mesh=mesh, in_specs=in_specs, out_specs=out_specs, check_vma=False
    )
```

```python
import jax
import jax.numpy as jnp
from jax import lax
from jax.experimental import pallas as pl
from jax.experimental.pallas import tpu as pltpu
from jax.sharding import PartitionSpec as P

AXES = ("row", "col")
OWNERS = 4
VMEM = pl.BlockSpec(memory_space=pltpu.VMEM)
SMEM = pl.BlockSpec(memory_space=pltpu.SMEM)
PARAMS = pltpu.CompilerParams(vmem_limit_bytes=24 * 1024 * 1024)


def layer_norm(values, axis):
    average = jnp.mean(values, axis=axis, keepdims=True)
    centred = values - average
    spread = jnp.mean(centred * centred, axis=axis, keepdims=True)
    return centred * lax.rsqrt(spread + 1e-05)


def sigmoid(values):
    return 0.5 * jnp.tanh(0.5 * values) + 0.5


def nt_dot(a, b):
    return lax.dot_general(a, b, (((1,), (1,)), ((), ())), preferred_element_type=jnp.float32)


def tn_dot(a, b):
    return lax.dot_general(a, b, (((0,), (0,)), ((), ())), preferred_element_type=jnp.float32)


def lanes_of(shape):
    return lax.broadcasted_iota(jnp.int32, shape, 1)


def pair_mask(lens_ref, tile_rows, tile_cols, first):
    live = tile_rows * lax.axis_size("row") - lens_ref[lens_ref.shape[0] - 1]
    lane = lanes_of((1, 2 * tile_cols))
    row = lax.axis_index("row") * tile_rows + first + (lane >= tile_cols).astype(jnp.int32)
    col = lax.axis_index("col") * tile_cols + lane % tile_cols
    return ((row < live) & (col < live)).astype(jnp.float32)


def project_kernel(lens_ref, x_ref, lw_ref, lg_ref, rw_ref, rg_ref, *refs):
    normed_ref, outs, (turned, held_left, held_right) = refs[0], refs[1:-3], refs[-3:]
    tile_rows, tile_cols, channels = x_ref.shape
    share = channels // OWNERS
    half = share // 2
    packed = OWNERS * half
    for at, w_ref in enumerate((lw_ref, lg_ref, rw_ref, rg_ref)):
        w = w_ref[...].astype(jnp.float32).T
        blocks = [
            w[o * share + g * half : o * share + (g + 1) * half] for g in (0, 1) for o in range(OWNERS)
        ]
        turned[at * channels : (at + 1) * channels] = jnp.concatenate(blocks, 0).astype(jnp.bfloat16)
    low = lanes_of((packed, 2 * tile_cols)) < tile_cols
    for first in range(0, tile_rows, 2):
        x = x_ref[first : first + 2].astype(jnp.float32).reshape(2 * tile_cols, channels)
        normed = layer_norm(x, -1).astype(jnp.bfloat16)
        normed_ref[first * tile_cols : (first + 2) * tile_cols] = normed
        flat = nt_dot(turned[...], normed)
        mask = pair_mask(lens_ref, tile_rows, tile_cols, first)
        for at, held in ((0, held_left), (2, held_right)):
            value = flat[at * channels : (at + 1) * channels]
            gate = flat[(at + 1) * channels : (at + 2) * channels]
            value = sigmoid(gate) * value * mask
            a, b = value[:packed], value[packed:]
            held[pl.ds(first, packed, stride=tile_rows), :] = jnp.where(
                low, a, pltpu.roll(b, tile_cols, 1)
            )
            held[pl.ds(first + 1, packed, stride=tile_rows), :] = jnp.where(
                low, pltpu.roll(a, tile_cols, 1), b
            )
    me = lax.axis_index("row") % OWNERS
    size = half * tile_rows
    for d in range(OWNERS):
        at = pl.multiple_of((me ^ d) * size, size)
        right = held_right[pl.ds(at, size)].astype(jnp.bfloat16)
        outs[d][:size] = held_left[pl.ds(at, size)].astype(jnp.bfloat16)
        outs[d][size:] = right
        outs[OWNERS + d][...] = right


def gate_kernel(normed_ref, w_ref, gate_ref):
    gate_ref[...] = sigmoid(jnp.dot(normed_ref[...], w_ref[...], preferred_element_type=jnp.float32))


def tri_kernel(*refs):
    near, far, outs = refs[:OWNERS], refs[OWNERS : 2 * OWNERS], refs[2 * OWNERS : -1]
    rights = refs[-1]
    size, width = far[0].shape
    half = rights.shape[0]
    tile_rows = size // half
    side = OWNERS * tile_rows
    me = lax.axis_index("row")
    owner, part, col = me % OWNERS, me // OWNERS, lax.axis_index("col")
    for d in range(OWNERS):
        for away, ref in ((0, near[d]), (1, far[d])):
            at = pl.multiple_of((part ^ away) * side + (owner ^ d) * tile_rows, tile_rows)
            start = size if away == 0 else 0
            for m in range(half):
                rights[m, pl.ds(at, tile_rows), :] = ref[
                    start + m * tile_rows : start + (m + 1) * tile_rows
                ]
    low = lanes_of((side, width)) < width // 2
    for m in range(half):
        left = jnp.concatenate([near[d][m * tile_rows : (m + 1) * tile_rows] for d in range(OWNERS)], 0)
        pieces = []
        for dx in (0, 1):
            block = rights[m, pl.ds(pl.multiple_of((col ^ dx) * side, side), side), :].astype(jnp.float32)
            pieces += [jnp.where(low, block, 0.0), jnp.where(low, 0.0, block)]
        right = jnp.concatenate(pieces, 0).astype(jnp.bfloat16)
        product = nt_dot(left, right).astype(jnp.bfloat16)
        for d in range(OWNERS):
            for dx in (0, 1):
                outs[2 * d + dx][m * tile_rows : (m + 1) * tile_rows] = product[
                    d * tile_rows : (d + 1) * tile_rows, dx * width : (dx + 1) * width
                ]


def finish_kernel(lens_ref, x_ref, gate_ref, bins_ref, ow_ref, dw_ref, *refs):
    parts, out_ref, loss_ref, (held, wide) = refs[:8], refs[8], refs[9], refs[10:]
    tile_rows, tile_cols, channels = x_ref.shape
    size, width = parts[0].shape
    half = size // tile_rows
    packed = OWNERS * half
    owner = lax.axis_index("row") % OWNERS
    total = jnp.zeros((tile_rows, width), jnp.float32)
    for d in range(OWNERS):
        block = parts[2 * d][...].astype(jnp.float32) + parts[2 * d + 1][...].astype(jnp.float32)
        held[pl.ds(pl.multiple_of((owner ^ d) * size, size), size), :] = block
        total = total + jnp.sum(block.reshape(half, tile_rows, width), 0)
    average = (total + pltpu.roll(total, tile_cols, 1)) * (1.0 / channels)
    total = jnp.zeros((tile_rows, width), jnp.float32)
    for om in range(packed):
        centred = held[om * tile_rows : (om + 1) * tile_rows] - average
        total = total + centred * centred
    spread = (total + pltpu.roll(total, tile_cols, 1)) * (1.0 / channels)
    scale = lax.rsqrt(spread + 1e-05)
    for om in range(packed):
        at = slice(om * tile_rows, (om + 1) * tile_rows)
        held[at] = (held[at] - average) * scale
    share = channels // OWNERS
    for o in range(OWNERS):
        for g in (0, 1):
            wide[o * half : (o + 1) * half, g * channels : (g + 1) * channels] = ow_ref[
                o * share + g * half : o * share + (g + 1) * half
            ]
    dist = dw_ref[...].astype(jnp.float32).T.astype(jnp.bfloat16)
    bin_ids = lax.broadcasted_iota(jnp.int32, (dist.shape[0], width), 0)
    loss = jnp.zeros((1, width), jnp.float32)
    for first in range(0, tile_rows, 2):
        updates = []
        for ii in (first, first + 1):
            turned = held[pl.ds(ii, packed, stride=tile_rows), :].astype(jnp.bfloat16)
            both = tn_dot(turned, wide[...])
            updates.append(both[:tile_cols, :channels] + both[tile_cols:, channels:])
        update = jnp.concatenate(updates, 0)
        gate = gate_ref[first * tile_cols : (first + 2) * tile_cols]
        x = x_ref[first : first + 2].astype(jnp.float32).reshape(2 * tile_cols, channels)
        pair_out = (x + gate * update).astype(jnp.bfloat16)
        out_ref[first : first + 2] = pair_out.reshape(2, tile_cols, channels)
        logits = nt_dot(dist, pair_out)
        log_total = jnp.log(jnp.sum(jnp.exp(logits), axis=0, keepdims=True))
        bins = bins_ref[first // 2 : first // 2 + 1]
        picked = jnp.sum(jnp.where(bin_ids == bins, logits, 0.0), axis=0, keepdims=True)
        loss = loss + pair_mask(lens_ref, tile_rows, tile_cols, first) * (log_total - picked)
    loss_ref[...] = jnp.broadcast_to(jnp.sum(loss, axis=1, keepdims=True), loss_ref.shape)


def loss_kernel(residues, lens_ref, *refs):
    total = refs[0][...]
    for ref in refs[1:-1]:
        total = total + ref[...]
    live = residues - lens_ref[lens_ref.shape[0] - 1]
    count = jnp.full(total.shape, live * live, jnp.int32).astype(jnp.float32)
    refs[-1][0] = (total / count)[0, 0]


def exchange(value, places, mask):
    return lax.ppermute(value, AXES, [(at, at ^ mask) for at in range(places)])


def call(kernel, outs, scratch=(), specs=None, out_specs=None, args=(), flops=0):
    return pl.pallas_call(
        kernel,
        out_shape=outs,
        in_specs=specs if specs is not None else [VMEM] * len(args),
        out_specs=out_specs if out_specs is not None else jax.tree.map(lambda _: VMEM, outs),
        scratch_shapes=list(scratch),
        compiler_params=PARAMS,
        cost_estimate=pl.CostEstimate(flops=flops, bytes_accessed=1 << 20, transcendentals=1 << 18),
    )(*args)


def by_kernels(
    pair_repr,
    distance_bins,
    chain_lengths,
    left_weight,
    left_gate_weight,
    right_weight,
    right_gate_weight,
    out_weight,
    out_gate_weight,
    dist_weight,
):
    tile_rows, tile_cols, channels = pair_repr.shape
    rows, cols = lax.axis_size("row"), lax.axis_size("col")
    places = rows * cols
    width = 2 * tile_cols
    spots = tile_rows * tile_cols
    size = channels // OWNERS // 2 * tile_rows
    bf16, f32 = jnp.bfloat16, jnp.float32
    struct = jax.ShapeDtypeStruct
    sent = call(
        project_kernel,
        [struct((spots, channels), bf16)]
        + [struct((2 * size, width), bf16)] * OWNERS
        + [struct((size, width), bf16)] * OWNERS,
        [
            pltpu.VMEM((4 * channels, channels), bf16),
            pltpu.VMEM((OWNERS * size, width), f32),
            pltpu.VMEM((OWNERS * size, width), f32),
        ],
        [SMEM] + [VMEM] * 5,
        args=(
            chain_lengths,
            pair_repr,
            left_weight,
            left_gate_weight,
            right_weight,
            right_gate_weight,
        ),
        flops=8 * spots * channels * channels,
    )
    normed, near, far = sent[0], sent[1 : 1 + OWNERS], sent[1 + OWNERS :]
    far = [exchange(value, places, (OWNERS + d) * cols) for d, value in enumerate(far)]
    near = [near[0]] + [exchange(near[d], places, d * cols) for d in range(1, OWNERS)]
    gate = call(
        gate_kernel,
        struct((spots, channels), f32),
        args=(normed, out_gate_weight),
        flops=2 * spots * channels * channels,
    )
    parts = call(
        tri_kernel,
        [struct((size, width), bf16)] * (2 * OWNERS),
        [pltpu.VMEM((size // tile_rows, rows * tile_rows, width), bf16)],
        args=(*near, *far),
        flops=2 * OWNERS * size * 2 * OWNERS * tile_rows * width,
    )
    parts = [parts[0]] + [exchange(parts[at], places, at) for at in range(1, 2 * OWNERS)]
    pair_out, loss = call(
        finish_kernel,
        [struct(pair_repr.shape, bf16), struct((8, 128), f32)],
        [
            pltpu.VMEM((OWNERS * size, width), f32),
            pltpu.VMEM((channels // 2, 2 * channels), bf16),
        ],
        [SMEM] + [VMEM] * 13,
        args=(
            chain_lengths,
            pair_repr,
            gate,
            distance_bins.reshape(tile_rows // 2, width),
            out_weight,
            dist_weight,
            *parts,
        ),
        flops=6 * spots * channels * channels,
    )
    loss = loss + exchange(loss, places, cols)
    losses = [loss] + [
        exchange(loss, places, z * 2 * cols + x)
        for z in range(rows // 2)
        for x in range(cols)
        if z or x
    ]
    loss_value = call(
        lambda *refs: loss_kernel(rows * tile_rows, *refs),
        struct((1,), f32),
        (),
        [SMEM] + [VMEM] * len(losses),
        SMEM,
        args=(chain_lengths, *losses),
    )
    return (pair_out, loss_value)


def by_all_to_all(
    pair_repr,
    distance_bins,
    chain_lengths,
    left_weight,
    left_gate_weight,
    right_weight,
    right_gate_weight,
    out_weight,
    out_gate_weight,
    dist_weight,
):
    tile_rows, tile_cols, channels = pair_repr.shape
    rows, cols = lax.axis_size("row"), lax.axis_size("col")
    peers = rows * cols
    share = channels // peers
    residues = tile_rows * rows
    spots = tile_rows * tile_cols
    live_count = residues - chain_lengths[chain_lengths.shape[0] - 1]
    row_place = lax.axis_index("row") * tile_rows + jnp.arange(tile_rows, dtype=jnp.int32)
    col_place = lax.axis_index("col") * tile_cols + jnp.arange(tile_cols, dtype=jnp.int32)
    live_rows = (row_place < live_count).astype(jnp.float32)
    live_cols = (col_place < live_count).astype(jnp.float32)
    flat_mask = (live_rows[:, None] * live_cols[None, :]).reshape(-1)
    normed = layer_norm(pair_repr.astype(jnp.float32), -1).astype(jnp.bfloat16)
    normed = normed.reshape(spots, channels)

    def project_turned(weight):
        return lax.dot_general(
            weight, normed, (((0,), (1,)), ((), ())), preferred_element_type=jnp.float32
        )

    def gated(gate_weight, weight):
        values = jax.nn.sigmoid(project_turned(gate_weight)) * project_turned(weight)
        return (values * flat_mask[None, :]).astype(jnp.bfloat16)

    left = gated(left_gate_weight, left_weight).reshape(peers, share, tile_rows, tile_cols)
    right = gated(right_gate_weight, right_weight).reshape(peers, share, tile_rows, tile_cols)
    both = jnp.concatenate([left, right], axis=3).reshape(peers, share * tile_rows, 2 * tile_cols)
    owned = lax.all_to_all(both, AXES, split_axis=0, concat_axis=0, tiled=True)
    owned = owned.reshape(rows, cols, share, tile_rows, 2, tile_cols)
    owned = owned.transpose(4, 2, 0, 3, 1, 5).reshape(2, share, residues, residues)
    tri = jnp.einsum(
        "cik,cjk->cij", owned[0], owned[1], preferred_element_type=jnp.float32
    ).astype(jnp.bfloat16)
    tri = tri.reshape(share, rows, tile_rows, cols, tile_cols).transpose(1, 3, 0, 2, 4)
    tri = tri.reshape(peers, share, spots)
    tri = lax.all_to_all(tri, AXES, split_axis=0, concat_axis=0, tiled=True)
    tri = tri.reshape(channels, spots).astype(jnp.float32)
    tri_normed = layer_norm(tri, 0).astype(jnp.bfloat16)
    out_gate = jax.nn.sigmoid(jnp.dot(normed, out_gate_weight, preferred_element_type=jnp.float32))
    update = out_gate * tn_dot(tri_normed, out_weight)
    pair_out = (pair_repr.astype(jnp.float32).reshape(spots, channels) + update).astype(
        jnp.bfloat16
    )
    logits = jnp.dot(pair_out, dist_weight, preferred_element_type=jnp.float32)
    log_total = jnp.log(jnp.sum(jnp.exp(logits), axis=-1))
    bin_ids = jnp.arange(logits.shape[1], dtype=jnp.int32)
    picked = jnp.sum(
        jnp.where(bin_ids[None, :] == distance_bins.reshape(-1, 1), logits, 0.0), axis=-1
    )
    loss_sum = jnp.sum(flat_mask * (log_total - picked))
    sums = lax.all_to_all(
        jnp.full((peers, 1, 128), loss_sum), AXES, split_axis=0, concat_axis=0, tiled=True
    )
    pair_count = (live_count * live_count).astype(jnp.float32)
    loss_value = (jnp.sum(sums[:, 0, 0]) / pair_count).reshape(1)
    return (pair_out.reshape(pair_repr.shape), loss_value)


def on_device(pair_repr, *others):
    tile_rows, tile_cols, channels = pair_repr.shape
    rows, cols = lax.axis_size("row"), lax.axis_size("col")
    fits = (
        rows == 2 * OWNERS
        and cols == 2
        and tile_rows * rows == tile_cols * cols
        and 2 * tile_cols == 128
        and tile_rows % 16 == 0
        and channels % (32 * OWNERS) == 0
    )
    return (by_kernels if fits else by_all_to_all)(pair_repr, *others)


def solution(mesh):
    in_specs = (
        P(("groups", "row"), "col", None),
        P(("groups", "row"), "col"),
        P("groups"),
        P(),
        P(),
        P(),
        P(),
        P(),
        P(),
        P(),
    )
    out_specs = (P(("groups", "row"), "col", None), P("groups"))
    return jax.shard_map(
        on_device, mesh=mesh, in_specs=in_specs, out_specs=out_specs, check_vma=False
    )
```

```python
import jax
import jax.numpy as jnp
from jax import lax
from jax.experimental import pallas as pl
from jax.experimental.pallas import tpu as pltpu
from jax.sharding import PartitionSpec as P

AXES = ("row", "col")
OWNERS = 4
VMEM = pl.BlockSpec(memory_space=pltpu.VMEM)
SMEM = pl.BlockSpec(memory_space=pltpu.SMEM)
PARAMS = pltpu.CompilerParams(vmem_limit_bytes=24 * 1024 * 1024)


def layer_norm(values, axis):
    average = jnp.mean(values, axis=axis, keepdims=True)
    centred = values - average
    spread = jnp.mean(centred * centred, axis=axis, keepdims=True)
    return centred * lax.rsqrt(spread + 1e-05)


def sigmoid(values):
    return 0.5 * jnp.tanh(0.5 * values) + 0.5


def nt_dot(a, b):
    return lax.dot_general(a, b, (((1,), (1,)), ((), ())), preferred_element_type=jnp.float32)


def tn_dot(a, b):
    return lax.dot_general(a, b, (((0,), (0,)), ((), ())), preferred_element_type=jnp.float32)


def lanes_of(shape):
    return lax.broadcasted_iota(jnp.int32, shape, 1)


def pair_mask(lens_ref, tile_rows, tile_cols, first):
    live = tile_rows * lax.axis_size("row") - lens_ref[lens_ref.shape[0] - 1]
    lane = lanes_of((1, 2 * tile_cols))
    row = lax.axis_index("row") * tile_rows + first + (lane >= tile_cols).astype(jnp.int32)
    col = lax.axis_index("col") * tile_cols + lane % tile_cols
    return ((row < live) & (col < live)).astype(jnp.float32)


def turn(w_refs, turned):
    channels = w_refs[0].shape[0]
    share = channels // OWNERS
    half = share // 2
    for at, w_ref in enumerate(w_refs):
        w = w_ref[...].astype(jnp.float32).T
        blocks = [
            w[o * share + g * half : o * share + (g + 1) * half] for g in (0, 1) for o in range(OWNERS)
        ]
        turned[at * channels : (at + 1) * channels] = jnp.concatenate(blocks, 0).astype(jnp.bfloat16)


def project(normed, turned, mask, held, first, tile_rows, tile_cols):
    channels = normed.shape[1]
    packed = channels // 2
    flat = nt_dot(turned[...], normed)
    value = sigmoid(flat[channels:]) * flat[:channels] * mask
    a, b = value[:packed], value[packed:]
    low = lanes_of((packed, 2 * tile_cols)) < tile_cols
    held[pl.ds(first, packed, stride=tile_rows), :] = jnp.where(low, a, pltpu.roll(b, tile_cols, 1))
    held[pl.ds(first + 1, packed, stride=tile_rows), :] = jnp.where(
        low, pltpu.roll(a, tile_cols, 1), b
    )


def owner_place():
    return lax.axis_index("row") // 2 % 2 * 2 + lax.axis_index("col")


def owner_block(held, d, size):
    at = pl.multiple_of((owner_place() ^ d) * size, size)
    return held[pl.ds(at, size)].astype(jnp.bfloat16)


def norm_kernel(x_ref, normed_ref):
    x = x_ref[...].astype(jnp.float32).reshape(normed_ref.shape)
    normed_ref[...] = layer_norm(x, -1).astype(jnp.bfloat16)


def project_all(lens_ref, normed_ref, w_ref, g_ref, turned, held):
    tile_rows = held.shape[0] // turned.shape[1] * 2
    tile_cols = held.shape[1] // 2
    turn((w_ref, g_ref), turned)
    for first in range(0, tile_rows, 2):
        normed = normed_ref[first * tile_cols : (first + 2) * tile_cols]
        mask = pair_mask(lens_ref, tile_rows, tile_cols, first)
        project(normed, turned, mask, held, first, tile_rows, tile_cols)


def right_kernel(lens_ref, normed_ref, w_ref, g_ref, *refs):
    outs, (turned, held) = refs[:OWNERS], refs[OWNERS:]
    project_all(lens_ref, normed_ref, w_ref, g_ref, turned, held)
    for d in range(OWNERS):
        outs[d][...] = owner_block(held, d, outs[d].shape[0])


def left_kernel(lens_ref, normed_ref, w_ref, g_ref, *refs):
    rights, outs, (turned, held) = refs[:OWNERS], refs[OWNERS : 2 * OWNERS], refs[2 * OWNERS :]
    project_all(lens_ref, normed_ref, w_ref, g_ref, turned, held)
    size = rights[0].shape[0]
    for d in range(OWNERS):
        outs[d][:size] = owner_block(held, d, size)
        outs[d][size:] = rights[d][...]


def gate_kernel(normed_ref, w_ref, gate_ref):
    gate_ref[...] = sigmoid(jnp.dot(normed_ref[...], w_ref[...], preferred_element_type=jnp.float32))


def tri_kernel(*refs):
    near, far = refs[:OWNERS], refs[OWNERS : 2 * OWNERS]
    near_over, far_over = refs[2 * OWNERS : 3 * OWNERS], refs[3 * OWNERS : 4 * OWNERS]
    outs, rights = refs[4 * OWNERS : -1], refs[-1]
    size, width = far[0].shape
    half = rights.shape[1]
    tile_rows = size // half
    side = width // 2
    me, col = lax.axis_index("row"), lax.axis_index("col")
    for d in range(OWNERS):
        for away, ref in (
            (d // 2 * 2, near[d]),
            (d // 2 * 2 + 1, near_over[d]),
            (d // 2 * 2 + 4, far[d]),
            (d // 2 * 2 + 5, far_over[d]),
        ):
            at = pl.multiple_of((me ^ away) * tile_rows, tile_rows)
            start = ref.shape[0] - size
            for m in range(half):
                rights[d % 2, m, pl.ds(at, tile_rows), :] = ref[
                    start + m * tile_rows : start + (m + 1) * tile_rows
                ]
    low = lanes_of((side, width)) < side
    for m in range(half):
        at = slice(m * tile_rows, (m + 1) * tile_rows)
        product = 0.0
        for dk in (0, 1):
            left = jnp.concatenate([near[dk][at], near[2 + dk][at]], 0)
            pieces = []
            for dx in (0, 1):
                block = rights[dk, m, pl.ds(pl.multiple_of((col ^ dx) * side, side), side), :]
                block = block.astype(jnp.float32)
                pieces += [jnp.where(low, block, 0.0), jnp.where(low, 0.0, block)]
            right = jnp.concatenate(pieces, 0).astype(jnp.bfloat16)
            product = product + nt_dot(left, right)
        product = product.astype(jnp.bfloat16)
        for dz in (0, 1):
            for dx in (0, 1):
                outs[2 * dz + dx][at] = product[
                    dz * tile_rows : (dz + 1) * tile_rows, dx * width : (dx + 1) * width
                ]


def finish_kernel(lens_ref, x_ref, gate_ref, bins_ref, ow_ref, dw_ref, *refs):
    parts, (out_ref, loss_ref, held, wide) = refs[:OWNERS], refs[OWNERS:]
    tile_rows, tile_cols, channels = x_ref.shape
    size, width = parts[0].shape
    half = size // tile_rows
    packed = OWNERS * half
    owner = owner_place()
    total = jnp.zeros((tile_rows, width), jnp.float32)
    for d in range(OWNERS):
        block = parts[d][...].astype(jnp.float32)
        held[pl.ds(pl.multiple_of((owner ^ d) * size, size), size), :] = block
        total = total + jnp.sum(block.reshape(half, tile_rows, width), 0)
    average = (total + pltpu.roll(total, tile_cols, 1)) * (1.0 / channels)
    total = jnp.zeros((tile_rows, width), jnp.float32)
    for om in range(packed):
        centred = held[om * tile_rows : (om + 1) * tile_rows] - average
        total = total + centred * centred
    spread = (total + pltpu.roll(total, tile_cols, 1)) * (1.0 / channels)
    scale = lax.rsqrt(spread + 1e-05)
    for om in range(packed):
        at = slice(om * tile_rows, (om + 1) * tile_rows)
        held[at] = (held[at] - average) * scale
    share = channels // OWNERS
    for o in range(OWNERS):
        for g in (0, 1):
            wide[o * half : (o + 1) * half, g * channels : (g + 1) * channels] = ow_ref[
                o * share + g * half : o * share + (g + 1) * half
            ]
    dist = dw_ref[...].astype(jnp.float32).T.astype(jnp.bfloat16)
    bin_ids = lax.broadcasted_iota(jnp.int32, (dist.shape[0], width), 0)
    loss = jnp.zeros((1, width), jnp.float32)
    for first in range(0, tile_rows, 2):
        updates = []
        for ii in (first, first + 1):
            turned = held[pl.ds(ii, packed, stride=tile_rows), :].astype(jnp.bfloat16)
            both = tn_dot(turned, wide[...])
            updates.append(both[:tile_cols, :channels] + both[tile_cols:, channels:])
        update = jnp.concatenate(updates, 0)
        gate = gate_ref[first * tile_cols : (first + 2) * tile_cols]
        x = x_ref[first : first + 2].astype(jnp.float32).reshape(2 * tile_cols, channels)
        pair_out = (x + gate * update).astype(jnp.bfloat16)
        out_ref[first : first + 2] = pair_out.reshape(2, tile_cols, channels)
        logits = nt_dot(dist, pair_out)
        log_total = jnp.log(jnp.sum(jnp.exp(logits), axis=0, keepdims=True))
        bins = bins_ref[first // 2 : first // 2 + 1]
        picked = jnp.sum(jnp.where(bin_ids == bins, logits, 0.0), axis=0, keepdims=True)
        loss = loss + pair_mask(lens_ref, tile_rows, tile_cols, first) * (log_total - picked)
    live = tile_rows * lax.axis_size("row") - lens_ref[lens_ref.shape[0] - 1]
    count = jnp.full((1, 1), live * live, jnp.int32).astype(jnp.float32)
    loss = jnp.sum(loss, axis=1, keepdims=True) / count
    loss_ref[...] = jnp.broadcast_to(loss, loss_ref.shape)


def exchange(value, places, mask):
    return lax.ppermute(value, AXES, [(at, at ^ mask) for at in range(places)])


def call(kernel, outs, scratch=(), specs=None, out_specs=None, args=(), flops=0):
    return pl.pallas_call(
        kernel,
        out_shape=outs,
        in_specs=specs if specs is not None else [VMEM] * len(args),
        out_specs=out_specs if out_specs is not None else jax.tree.map(lambda _: VMEM, outs),
        scratch_shapes=list(scratch),
        compiler_params=PARAMS,
        cost_estimate=pl.CostEstimate(flops=flops, bytes_accessed=1 << 20, transcendentals=1 << 18),
    )(*args)


def by_kernels(
    pair_repr,
    distance_bins,
    chain_lengths,
    left_weight,
    left_gate_weight,
    right_weight,
    right_gate_weight,
    out_weight,
    out_gate_weight,
    dist_weight,
):
    tile_rows, tile_cols, channels = pair_repr.shape
    rows, cols = lax.axis_size("row"), lax.axis_size("col")
    places = rows * cols
    width = 2 * tile_cols
    spots = tile_rows * tile_cols
    size = channels // OWNERS // 2 * tile_rows
    bf16, f32 = jnp.bfloat16, jnp.float32
    struct = jax.ShapeDtypeStruct
    turned = pltpu.VMEM((2 * channels, channels), bf16)
    held = pltpu.VMEM((OWNERS * size, width), f32)
    over_core, over_half = cols, 4 * cols
    over = [0, 1, 2 * cols, 2 * cols + 1]
    normed = call(
        norm_kernel, struct((spots, channels), bf16), args=(pair_repr,), flops=1 << 30
    )
    rights = call(
        right_kernel,
        [struct((size, width), bf16)] * OWNERS,
        [turned, held],
        [SMEM] + [VMEM] * 3,
        args=(chain_lengths, normed, right_weight, right_gate_weight),
        flops=4 * spots * channels * channels,
    )
    far = [exchange(rights[d], places, over_half + over[d]) for d in range(OWNERS)]
    near = call(
        left_kernel,
        [struct((2 * size, width), bf16)] * OWNERS,
        [turned, held],
        [SMEM] + [VMEM] * (3 + OWNERS),
        args=(chain_lengths, normed, left_weight, left_gate_weight, *rights),
        flops=4 * spots * channels * channels,
    )
    near = [near[0]] + [exchange(near[d], places, over[d]) for d in range(1, OWNERS)]
    near_over = [exchange(value, places, over_core) for value in [rights[0]] + near[1:]]
    far_over = [exchange(value, places, over_core) for value in far]
    gate = call(
        gate_kernel,
        struct((spots, channels), f32),
        args=(normed, out_gate_weight),
        flops=2 * spots * channels * channels,
    )
    parts = call(
        tri_kernel,
        [struct((size, width), bf16)] * OWNERS,
        [pltpu.VMEM((cols, size // tile_rows, rows * tile_rows, width), bf16)],
        args=(*near, *far, *near_over, *far_over),
        flops=8 * size * 2 * tile_rows * 2 * width,
    )
    parts = [parts[0]] + [exchange(parts[d], places, over[d]) for d in range(1, OWNERS)]
    pair_out, loss = call(
        finish_kernel,
        [struct(pair_repr.shape, bf16), struct((1, 128), f32)],
        [held, pltpu.VMEM((channels // 2, 2 * channels), bf16)],
        [SMEM] + [VMEM] * 9,
        args=(
            chain_lengths,
            pair_repr,
            gate,
            distance_bins.reshape(tile_rows // 2, width),
            out_weight,
            dist_weight,
            *parts,
        ),
        flops=6 * spots * channels * channels,
    )
    for mask in (over_core, over[1], over[2], over_half):
        loss = loss + exchange(loss, places, mask)
    return (pair_out, loss[0, :1])


def by_all_to_all(
    pair_repr,
    distance_bins,
    chain_lengths,
    left_weight,
    left_gate_weight,
    right_weight,
    right_gate_weight,
    out_weight,
    out_gate_weight,
    dist_weight,
):
    tile_rows, tile_cols, channels = pair_repr.shape
    rows, cols = lax.axis_size("row"), lax.axis_size("col")
    peers = rows * cols
    share = channels // peers
    residues = tile_rows * rows
    spots = tile_rows * tile_cols
    live_count = residues - chain_lengths[chain_lengths.shape[0] - 1]
    row_place = lax.axis_index("row") * tile_rows + jnp.arange(tile_rows, dtype=jnp.int32)
    col_place = lax.axis_index("col") * tile_cols + jnp.arange(tile_cols, dtype=jnp.int32)
    live_rows = (row_place < live_count).astype(jnp.float32)
    live_cols = (col_place < live_count).astype(jnp.float32)
    flat_mask = (live_rows[:, None] * live_cols[None, :]).reshape(-1)
    normed = layer_norm(pair_repr.astype(jnp.float32), -1).astype(jnp.bfloat16)
    normed = normed.reshape(spots, channels)

    def project_turned(weight):
        return lax.dot_general(
            weight, normed, (((0,), (1,)), ((), ())), preferred_element_type=jnp.float32
        )

    def gated(gate_weight, weight):
        values = jax.nn.sigmoid(project_turned(gate_weight)) * project_turned(weight)
        return (values * flat_mask[None, :]).astype(jnp.bfloat16)

    left = gated(left_gate_weight, left_weight).reshape(peers, share, tile_rows, tile_cols)
    right = gated(right_gate_weight, right_weight).reshape(peers, share, tile_rows, tile_cols)
    both = jnp.concatenate([left, right], axis=3).reshape(peers, share * tile_rows, 2 * tile_cols)
    owned = lax.all_to_all(both, AXES, split_axis=0, concat_axis=0, tiled=True)
    owned = owned.reshape(rows, cols, share, tile_rows, 2, tile_cols)
    owned = owned.transpose(4, 2, 0, 3, 1, 5).reshape(2, share, residues, residues)
    tri = jnp.einsum(
        "cik,cjk->cij", owned[0], owned[1], preferred_element_type=jnp.float32
    ).astype(jnp.bfloat16)
    tri = tri.reshape(share, rows, tile_rows, cols, tile_cols).transpose(1, 3, 0, 2, 4)
    tri = tri.reshape(peers, share, spots)
    tri = lax.all_to_all(tri, AXES, split_axis=0, concat_axis=0, tiled=True)
    tri = tri.reshape(channels, spots).astype(jnp.float32)
    tri_normed = layer_norm(tri, 0).astype(jnp.bfloat16)
    out_gate = jax.nn.sigmoid(jnp.dot(normed, out_gate_weight, preferred_element_type=jnp.float32))
    update = out_gate * tn_dot(tri_normed, out_weight)
    pair_out = (pair_repr.astype(jnp.float32).reshape(spots, channels) + update).astype(
        jnp.bfloat16
    )
    logits = jnp.dot(pair_out, dist_weight, preferred_element_type=jnp.float32)
    log_total = jnp.log(jnp.sum(jnp.exp(logits), axis=-1))
    bin_ids = jnp.arange(logits.shape[1], dtype=jnp.int32)
    picked = jnp.sum(
        jnp.where(bin_ids[None, :] == distance_bins.reshape(-1, 1), logits, 0.0), axis=-1
    )
    loss_sum = jnp.sum(flat_mask * (log_total - picked))
    sums = lax.all_to_all(
        jnp.full((peers, 1, 128), loss_sum), AXES, split_axis=0, concat_axis=0, tiled=True
    )
    pair_count = (live_count * live_count).astype(jnp.float32)
    loss_value = (jnp.sum(sums[:, 0, 0]) / pair_count).reshape(1)
    return (pair_out.reshape(pair_repr.shape), loss_value)


def on_device(pair_repr, *others):
    tile_rows, tile_cols, channels = pair_repr.shape
    rows, cols = lax.axis_size("row"), lax.axis_size("col")
    fits = (
        rows == 2 * OWNERS
        and cols == 2
        and tile_rows * rows == tile_cols * cols
        and 2 * tile_cols == 128
        and tile_rows % 16 == 0
        and channels % (32 * OWNERS) == 0
    )
    return (by_kernels if fits else by_all_to_all)(pair_repr, *others)


def solution(mesh):
    in_specs = (
        P(("groups", "row"), "col", None),
        P(("groups", "row"), "col"),
        P("groups"),
        P(),
        P(),
        P(),
        P(),
        P(),
        P(),
        P(),
    )
    out_specs = (P(("groups", "row"), "col", None), P("groups"))
    return jax.shard_map(
        on_device, mesh=mesh, in_specs=in_specs, out_specs=out_specs, check_vma=False
    )
```

```python
import jax
import jax.numpy as jnp
from jax import lax
from jax.experimental import pallas as pl
from jax.experimental.pallas import tpu as pltpu
from jax.sharding import PartitionSpec as P

AXES = ("row", "col")
OWNERS = 4
VMEM = pl.BlockSpec(memory_space=pltpu.VMEM)
SMEM = pl.BlockSpec(memory_space=pltpu.SMEM)
PARAMS = pltpu.CompilerParams(vmem_limit_bytes=24 * 1024 * 1024)


def layer_norm(values, axis):
    average = jnp.mean(values, axis=axis, keepdims=True)
    centred = values - average
    spread = jnp.mean(centred * centred, axis=axis, keepdims=True)
    return centred * lax.rsqrt(spread + 1e-05)


def sigmoid(values):
    return 0.5 * jnp.tanh(0.5 * values) + 0.5


def nt_dot(a, b):
    return lax.dot_general(a, b, (((1,), (1,)), ((), ())), preferred_element_type=jnp.float32)


def tn_dot(a, b):
    return lax.dot_general(a, b, (((0,), (0,)), ((), ())), preferred_element_type=jnp.float32)


def lanes_of(shape):
    return lax.broadcasted_iota(jnp.int32, shape, 1)


def pair_mask(lens_ref, tile_rows, tile_cols, first):
    live = tile_rows * lax.axis_size("row") - lens_ref[lens_ref.shape[0] - 1]
    lane = lanes_of((1, 2 * tile_cols))
    row = lax.axis_index("row") * tile_rows + first + (lane >= tile_cols).astype(jnp.int32)
    col = lax.axis_index("col") * tile_cols + lane % tile_cols
    return ((row < live) & (col < live)).astype(jnp.float32)


def turn(w_refs, turned):
    channels = w_refs[0].shape[0]
    share = channels // OWNERS
    half = share // 2
    for at, w_ref in enumerate(w_refs):
        w = w_ref[...].astype(jnp.float32).T
        blocks = [
            w[o * share + g * half : o * share + (g + 1) * half] for g in (0, 1) for o in range(OWNERS)
        ]
        turned[at * channels : (at + 1) * channels] = jnp.concatenate(blocks, 0).astype(jnp.bfloat16)


def project(normed, turned, held, first, tile_rows, tile_cols, mask=None):
    channels = normed.shape[1]
    packed = channels // 2
    flat = nt_dot(turned[...], normed)
    value = sigmoid(flat[channels:]) * flat[:channels]
    if mask is not None:
        value = value * mask
    a, b = value[:packed], value[packed:]
    low = lanes_of((packed, 2 * tile_cols)) < tile_cols
    held[pl.ds(first, packed, stride=tile_rows), :] = jnp.where(low, a, pltpu.roll(b, tile_cols, 1))
    held[pl.ds(first + 1, packed, stride=tile_rows), :] = jnp.where(
        low, pltpu.roll(a, tile_cols, 1), b
    )


def owner_place():
    return lax.axis_index("row") // 2 % 2 * 2 + lax.axis_index("col")


def owner_block(held, d, size):
    at = pl.multiple_of((owner_place() ^ d) * size, size)
    return held[pl.ds(at, size)].astype(jnp.bfloat16)


def norm_kernel(x_ref, normed_ref):
    x = x_ref[...].astype(jnp.float32).reshape(normed_ref.shape)
    normed_ref[...] = layer_norm(x, -1).astype(jnp.bfloat16)


def project_all(lens_ref, normed_ref, w_ref, g_ref, turned, held):
    tile_rows = held.shape[0] // turned.shape[1] * 2
    tile_cols = held.shape[1] // 2
    turn((w_ref, g_ref), turned)
    for first in range(0, tile_rows, 2):
        normed = normed_ref[first * tile_cols : (first + 2) * tile_cols]
        mask = None if lens_ref is None else pair_mask(lens_ref, tile_rows, tile_cols, first)
        project(normed, turned, held, first, tile_rows, tile_cols, mask)


def right_kernel(normed_ref, w_ref, g_ref, *refs):
    outs, (turned, held) = refs[:OWNERS], refs[OWNERS:]
    project_all(None, normed_ref, w_ref, g_ref, turned, held)
    for d in range(OWNERS):
        outs[d][...] = owner_block(held, d, outs[d].shape[0])


def left_kernel(lens_ref, normed_ref, w_ref, g_ref, *refs):
    rights, outs, (turned, held) = refs[:OWNERS], refs[OWNERS : 2 * OWNERS], refs[2 * OWNERS :]
    project_all(lens_ref, normed_ref, w_ref, g_ref, turned, held)
    size = rights[0].shape[0]
    for d in range(OWNERS):
        outs[d][:size] = owner_block(held, d, size)
        outs[d][size:] = rights[d][...]


def gate_kernel(x_ref, normed_ref, gw_ref, ow_ref, dw_ref, gate_ref, x_turned_ref, ow_turned, dw_turned):
    tile_rows, tile_cols, channels = x_ref.shape
    share = channels // OWNERS
    half = share // 2
    blocks = [
        ow_ref[o * share + g * half : o * share + (g + 1) * half].astype(jnp.float32)
        for g in (0, 1)
        for o in range(OWNERS)
    ]
    ow_turned[...] = jnp.concatenate(blocks, 0).T.astype(jnp.bfloat16)
    dw_turned[...] = dw_ref[...].astype(jnp.float32).T.astype(jnp.bfloat16)
    gate_turned = gw_ref[...].astype(jnp.float32).T.astype(jnp.bfloat16)
    for first in range(0, tile_rows, 2):
        at = slice(first * tile_cols, (first + 2) * tile_cols)
        gate_ref[:, at] = sigmoid(nt_dot(gate_turned, normed_ref[at]))
        x = x_ref[first : first + 2].astype(jnp.float32).reshape(2 * tile_cols, channels)
        x_turned_ref[:, at] = x.T


def tri_kernel(lens_ref, *refs):
    near, far = refs[:OWNERS], refs[OWNERS : 2 * OWNERS]
    near_over, far_over = refs[2 * OWNERS : 3 * OWNERS], refs[3 * OWNERS : 4 * OWNERS]
    outs, rights = refs[4 * OWNERS : -1], refs[-1]
    size, width = far[0].shape
    half = rights.shape[1]
    tile_rows = size // half
    side = width // 2
    me, col = lax.axis_index("row"), lax.axis_index("col")
    pieces = []
    for d in range(OWNERS):
        away = d // 2 * 2
        pieces += [(d % 2, away, near[d]), (d % 2, away + 4, far[d])]
        pieces += [(d % 2, away + 1, near_over[d]), (d % 2, away + 5, far_over[d])]
    for dk, away, ref in pieces:
        start = ref.shape[0] - size
        at = pl.multiple_of((me ^ away) * tile_rows, tile_rows)
        for m in range(half):
            rights[dk, m, pl.ds(at, tile_rows), :] = ref[
                start + m * tile_rows : start + (m + 1) * tile_rows
            ]
    live = lens_ref.shape[0] - 1
    live = tile_rows * lax.axis_size("row") - lens_ref[live]
    lane = lanes_of((side, width))
    place = lax.broadcasted_iota(jnp.int32, (side, width), 0)
    keep = [place + (col ^ dx) * side < live for dx in (0, 1)]
    picks = [((lane < side) & keep[dx], (lane >= side) & keep[dx]) for dx in (0, 1)]
    for m in range(half):
        at = slice(m * tile_rows, (m + 1) * tile_rows)
        product = 0.0
        for dk in (0, 1):
            left = jnp.concatenate([near[dk][at], near[2 + dk][at]], 0)
            pieces = []
            for dx in (0, 1):
                block = rights[dk, m, pl.ds(pl.multiple_of((col ^ dx) * side, side), side), :]
                block = block.astype(jnp.float32)
                pieces += [jnp.where(pick, block, 0.0) for pick in picks[dx]]
            right = jnp.concatenate(pieces, 0).astype(jnp.bfloat16)
            product = product + nt_dot(left, right)
        product = product.astype(jnp.bfloat16)
        for dz in (0, 1):
            for dx in (0, 1):
                outs[2 * dz + dx][at] = product[
                    dz * tile_rows : (dz + 1) * tile_rows, dx * width : (dx + 1) * width
                ]


def finish_kernel(lens_ref, x_ref, gate_ref, bins_ref, ow_ref, dw_ref, *refs):
    parts, (out_ref, loss_ref, held) = refs[:OWNERS], refs[OWNERS:]
    channels = x_ref.shape[0]
    size, width = parts[0].shape
    half = channels // 2 // OWNERS
    tile_rows, tile_cols = size // half, width // 2
    packed = OWNERS * half
    owner = owner_place()
    total = jnp.zeros((tile_rows, width), jnp.float32)
    for d in range(OWNERS):
        block = parts[d][...].astype(jnp.float32)
        held[pl.ds(pl.multiple_of((owner ^ d) * size, size), size), :] = block
        total = total + jnp.sum(block.reshape(half, tile_rows, width), 0)
    average = (total + pltpu.roll(total, tile_cols, 1)) * (1.0 / channels)
    total = jnp.zeros((tile_rows, width), jnp.float32)
    for om in range(packed):
        centred = held[om * tile_rows : (om + 1) * tile_rows] - average
        total = total + centred * centred
    spread = (total + pltpu.roll(total, tile_cols, 1)) * (1.0 / channels)
    scale = lax.rsqrt(spread + 1e-05)
    low = lanes_of((packed, width)) < tile_cols
    bin_ids = lax.broadcasted_iota(jnp.int32, (dw_ref.shape[0], width), 0)
    loss = jnp.zeros((1, width), jnp.float32)
    for first in range(0, tile_rows, 2):
        a, b = [
            (held[pl.ds(ii, packed, stride=tile_rows), :] - average[ii : ii + 1]) * scale[ii : ii + 1]
            for ii in (first, first + 1)
        ]
        normed = jnp.concatenate(
            [
                jnp.where(low, a, pltpu.roll(b, tile_cols, 1)),
                jnp.where(low, pltpu.roll(a, tile_cols, 1), b),
            ],
            0,
        ).astype(jnp.bfloat16)
        update = jnp.dot(ow_ref[...], normed, preferred_element_type=jnp.float32)
        at = slice(first * tile_cols, (first + 2) * tile_cols)
        pair_out = (x_ref[:, at] + gate_ref[:, at] * update).astype(jnp.bfloat16)
        out_ref[:, at] = pair_out
        logits = jnp.dot(dw_ref[...], pair_out, preferred_element_type=jnp.float32)
        log_total = jnp.log(jnp.sum(jnp.exp(logits), axis=0, keepdims=True))
        bins = bins_ref[first // 2 : first // 2 + 1]
        picked = jnp.sum(jnp.where(bin_ids == bins, logits, 0.0), axis=0, keepdims=True)
        loss = loss + pair_mask(lens_ref, tile_rows, tile_cols, first) * (log_total - picked)
    live = tile_rows * lax.axis_size("row") - lens_ref[lens_ref.shape[0] - 1]
    count = jnp.full((1, 1), live * live, jnp.int32).astype(jnp.float32)
    loss = jnp.sum(loss, axis=1, keepdims=True) / count
    loss_ref[...] = jnp.broadcast_to(loss[None], loss_ref.shape)


def turn_back_kernel(turned_ref, out_ref):
    tile_rows, tile_cols, channels = out_ref.shape
    for first in range(0, tile_rows, 2):
        block = turned_ref[:, first * tile_cols : (first + 2) * tile_cols].astype(jnp.float32).T
        out_ref[first : first + 2] = block.astype(jnp.bfloat16).reshape(2, tile_cols, channels)


def exchange(value, places, mask):
    return lax.ppermute(value, AXES, [(at, at ^ mask) for at in range(places)])


def call(kernel, outs, scratch=(), specs=None, out_specs=None, args=(), flops=0):
    return pl.pallas_call(
        kernel,
        out_shape=outs,
        in_specs=specs if specs is not None else [VMEM] * len(args),
        out_specs=out_specs if out_specs is not None else jax.tree.map(lambda _: VMEM, outs),
        scratch_shapes=list(scratch),
        compiler_params=PARAMS,
        cost_estimate=pl.CostEstimate(flops=flops, bytes_accessed=1 << 20, transcendentals=1 << 18),
    )(*args)


def by_kernels(
    pair_repr,
    distance_bins,
    chain_lengths,
    left_weight,
    left_gate_weight,
    right_weight,
    right_gate_weight,
    out_weight,
    out_gate_weight,
    dist_weight,
):
    tile_rows, tile_cols, channels = pair_repr.shape
    rows, cols = lax.axis_size("row"), lax.axis_size("col")
    places = rows * cols
    width = 2 * tile_cols
    spots = tile_rows * tile_cols
    size = channels // OWNERS // 2 * tile_rows
    bf16, f32 = jnp.bfloat16, jnp.float32
    struct = jax.ShapeDtypeStruct
    turned = pltpu.VMEM((2 * channels, channels), bf16)
    held = pltpu.VMEM((OWNERS * size, width), f32)
    over_core, over_half = cols, 4 * cols
    over = [0, 1, 2 * cols, 2 * cols + 1]
    normed = call(
        norm_kernel, struct((spots, channels), bf16), args=(pair_repr,), flops=1 << 30
    )
    rights = call(
        right_kernel,
        [struct((size, width), bf16)] * OWNERS,
        [turned, held],
        args=(normed, right_weight, right_gate_weight),
        flops=4 * spots * channels * channels,
    )
    far = [exchange(rights[d], places, over_half + over[d]) for d in range(OWNERS)]
    near = call(
        left_kernel,
        [struct((2 * size, width), bf16)] * OWNERS,
        [turned, held],
        [SMEM] + [VMEM] * (3 + OWNERS),
        args=(chain_lengths, normed, left_weight, left_gate_weight, *rights),
        flops=4 * spots * channels * channels,
    )
    near = [near[0]] + [exchange(near[d], places, over[d]) for d in range(1, OWNERS)]
    near_over = [exchange(value, places, over_core) for value in [rights[0]] + near[1:]]
    far_over = [exchange(value, places, over_core) for value in far]
    parts = call(
        tri_kernel,
        [struct((size, width), bf16)] * OWNERS,
        [pltpu.VMEM((cols, size // tile_rows, rows * tile_rows, width), bf16)],
        [SMEM] + [VMEM] * (4 * OWNERS),
        args=(chain_lengths, *near, *far, *near_over, *far_over),
        flops=8 * size * 2 * tile_rows * 2 * width,
    )
    parts = [parts[0]] + [exchange(parts[d], places, over[d]) for d in range(1, OWNERS)]
    gate, x_turned, out_turned, dist_turned = call(
        gate_kernel,
        [
            struct((channels, spots), f32),
            struct((channels, spots), f32),
            struct((channels, channels), bf16),
            struct(dist_weight.shape[::-1], bf16),
        ],
        args=(pair_repr, normed, out_gate_weight, out_weight, dist_weight),
        flops=2 * spots * channels * channels,
    )
    pair_out, loss = call(
        finish_kernel,
        [struct((channels, spots), bf16), struct((places // 2, 8, 128), f32)],
        [held],
        [SMEM] + [VMEM] * 9,
        args=(
            chain_lengths,
            x_turned,
            gate,
            distance_bins.reshape(tile_rows // 2, width),
            out_turned,
            dist_turned,
            *parts,
        ),
        flops=6 * spots * channels * channels,
    )
    pair_out = call(turn_back_kernel, struct(pair_repr.shape, bf16), args=(pair_out,), flops=1 << 26)
    loss = loss + exchange(loss, places, over_core)
    chips = [
        [(place * 2 + core) * cols + col for place in range(rows // 2) for col in range(cols)]
        for core in (0, 1)
    ]
    loss = lax.all_to_all(loss, AXES, 0, 0, axis_index_groups=chips, tiled=True)
    return (pair_out, jnp.sum(loss, axis=0)[0, :1])


def by_all_to_all(
    pair_repr,
    distance_bins,
    chain_lengths,
    left_weight,
    left_gate_weight,
    right_weight,
    right_gate_weight,
    out_weight,
    out_gate_weight,
    dist_weight,
):
    tile_rows, tile_cols, channels = pair_repr.shape
    rows, cols = lax.axis_size("row"), lax.axis_size("col")
    peers = rows * cols
    share = channels // peers
    residues = tile_rows * rows
    spots = tile_rows * tile_cols
    live_count = residues - chain_lengths[chain_lengths.shape[0] - 1]
    row_place = lax.axis_index("row") * tile_rows + jnp.arange(tile_rows, dtype=jnp.int32)
    col_place = lax.axis_index("col") * tile_cols + jnp.arange(tile_cols, dtype=jnp.int32)
    live_rows = (row_place < live_count).astype(jnp.float32)
    live_cols = (col_place < live_count).astype(jnp.float32)
    flat_mask = (live_rows[:, None] * live_cols[None, :]).reshape(-1)
    normed = layer_norm(pair_repr.astype(jnp.float32), -1).astype(jnp.bfloat16)
    normed = normed.reshape(spots, channels)

    def project_turned(weight):
        return lax.dot_general(
            weight, normed, (((0,), (1,)), ((), ())), preferred_element_type=jnp.float32
        )

    def gated(gate_weight, weight):
        values = jax.nn.sigmoid(project_turned(gate_weight)) * project_turned(weight)
        return (values * flat_mask[None, :]).astype(jnp.bfloat16)

    left = gated(left_gate_weight, left_weight).reshape(peers, share, tile_rows, tile_cols)
    right = gated(right_gate_weight, right_weight).reshape(peers, share, tile_rows, tile_cols)
    both = jnp.concatenate([left, right], axis=3).reshape(peers, share * tile_rows, 2 * tile_cols)
    owned = lax.all_to_all(both, AXES, split_axis=0, concat_axis=0, tiled=True)
    owned = owned.reshape(rows, cols, share, tile_rows, 2, tile_cols)
    owned = owned.transpose(4, 2, 0, 3, 1, 5).reshape(2, share, residues, residues)
    tri = jnp.einsum(
        "cik,cjk->cij", owned[0], owned[1], preferred_element_type=jnp.float32
    ).astype(jnp.bfloat16)
    tri = tri.reshape(share, rows, tile_rows, cols, tile_cols).transpose(1, 3, 0, 2, 4)
    tri = tri.reshape(peers, share, spots)
    tri = lax.all_to_all(tri, AXES, split_axis=0, concat_axis=0, tiled=True)
    tri = tri.reshape(channels, spots).astype(jnp.float32)
    tri_normed = layer_norm(tri, 0).astype(jnp.bfloat16)
    out_gate = jax.nn.sigmoid(jnp.dot(normed, out_gate_weight, preferred_element_type=jnp.float32))
    update = out_gate * tn_dot(tri_normed, out_weight)
    pair_out = (pair_repr.astype(jnp.float32).reshape(spots, channels) + update).astype(
        jnp.bfloat16
    )
    logits = jnp.dot(pair_out, dist_weight, preferred_element_type=jnp.float32)
    log_total = jnp.log(jnp.sum(jnp.exp(logits), axis=-1))
    bin_ids = jnp.arange(logits.shape[1], dtype=jnp.int32)
    picked = jnp.sum(
        jnp.where(bin_ids[None, :] == distance_bins.reshape(-1, 1), logits, 0.0), axis=-1
    )
    loss_sum = jnp.sum(flat_mask * (log_total - picked))
    sums = lax.all_to_all(
        jnp.full((peers, 1, 128), loss_sum), AXES, split_axis=0, concat_axis=0, tiled=True
    )
    pair_count = (live_count * live_count).astype(jnp.float32)
    loss_value = (jnp.sum(sums[:, 0, 0]) / pair_count).reshape(1)
    return (pair_out.reshape(pair_repr.shape), loss_value)


def on_device(pair_repr, *others):
    tile_rows, tile_cols, channels = pair_repr.shape
    rows, cols = lax.axis_size("row"), lax.axis_size("col")
    fits = (
        rows == 2 * OWNERS
        and cols == 2
        and tile_rows * rows == tile_cols * cols
        and 2 * tile_cols == 128
        and tile_rows % 16 == 0
        and channels % (32 * OWNERS) == 0
    )
    return (by_kernels if fits else by_all_to_all)(pair_repr, *others)


def solution(mesh):
    in_specs = (
        P(("groups", "row"), "col", None),
        P(("groups", "row"), "col"),
        P("groups"),
        P(),
        P(),
        P(),
        P(),
        P(),
        P(),
        P(),
    )
    out_specs = (P(("groups", "row"), "col", None), P("groups"))
    return jax.shard_map(
        on_device, mesh=mesh, in_specs=in_specs, out_specs=out_specs, check_vma=False
    )
```

```python
import jax
import jax.numpy as jnp
from jax import lax
from jax.experimental import pallas as pl
from jax.experimental.pallas import tpu as pltpu
from jax.sharding import PartitionSpec as P

AXES = ("row", "col")
OWNERS = 4
VMEM = pl.BlockSpec(memory_space=pltpu.VMEM)
SMEM = pl.BlockSpec(memory_space=pltpu.SMEM)
PARAMS = pltpu.CompilerParams(vmem_limit_bytes=24 * 1024 * 1024)


def layer_norm(values, axis):
    average = jnp.mean(values, axis=axis, keepdims=True)
    centred = values - average
    spread = jnp.mean(centred * centred, axis=axis, keepdims=True)
    return centred * lax.rsqrt(spread + 1e-05)


def sigmoid(values):
    return 0.5 * jnp.tanh(0.5 * values) + 0.5


def nt_dot(a, b):
    return lax.dot_general(a, b, (((1,), (1,)), ((), ())), preferred_element_type=jnp.float32)


def tn_dot(a, b):
    return lax.dot_general(a, b, (((0,), (0,)), ((), ())), preferred_element_type=jnp.float32)


def lanes_of(shape):
    return lax.broadcasted_iota(jnp.int32, shape, 1)


def make_masks(lens_ref, tile_rows, tile_cols):
    live = tile_rows * lax.axis_size("row") - lens_ref[lens_ref.shape[0] - 1]
    lane = lanes_of((1, 2 * tile_cols))
    upper = (lane >= tile_cols).astype(jnp.int32)
    place = lane - tile_cols * upper
    row, col = lax.axis_index("row") * tile_rows, lax.axis_index("col")
    keeps = [(place + (col ^ dx) * tile_cols < live).astype(jnp.float32) for dx in (0, 1)]
    pairs = [
        (row + first + upper < live).astype(jnp.float32) * keeps[0]
        for first in range(0, tile_rows, 2)
    ]
    count = jnp.full(lane.shape, live * live, jnp.int32).astype(jnp.float32)
    return pairs, keeps, 1.0 / count


def turn(w_refs, turned):
    channels = w_refs[0].shape[0]
    share = channels // OWNERS
    half = share // 2
    for at, w_ref in enumerate(w_refs):
        w = w_ref[...].astype(jnp.float32).T
        blocks = [
            w[o * share + g * half : o * share + (g + 1) * half] for g in (0, 1) for o in range(OWNERS)
        ]
        turned[at * channels : (at + 1) * channels] = jnp.concatenate(blocks, 0).astype(jnp.bfloat16)


def project(normed_ref, w_ref, g_ref, turned, held, masks=None):
    channels = normed_ref.shape[1]
    packed = channels // 2
    tile_rows, tile_cols = held.shape[0] // packed, held.shape[1] // 2
    turn((w_ref, g_ref), turned)
    low = lanes_of((packed, 2 * tile_cols)) < tile_cols
    for first in range(0, tile_rows, 2):
        flat = nt_dot(turned[...], normed_ref[first * tile_cols : (first + 2) * tile_cols])
        value = sigmoid(flat[channels:]) * flat[:channels]
        if masks is not None:
            value = value * masks[first // 2]
        a, b = value[:packed], value[packed:]
        held[pl.ds(first, packed, stride=tile_rows), :] = jnp.where(
            low, a, pltpu.roll(b, tile_cols, 1)
        )
        held[pl.ds(first + 1, packed, stride=tile_rows), :] = jnp.where(
            low, pltpu.roll(a, tile_cols, 1), b
        )


def owner_place():
    return lax.axis_index("row") % OWNERS


def owner_block(held, d, size):
    at = pl.multiple_of((owner_place() ^ d) * size, size)
    return held[pl.ds(at, size)].astype(jnp.bfloat16)


def norm_kernel(x_ref, normed_ref):
    x = x_ref[...].astype(jnp.float32).reshape(normed_ref.shape)
    normed_ref[...] = layer_norm(x, -1).astype(jnp.bfloat16)


def right_kernel(normed_ref, w_ref, g_ref, stay_ref, move_ref, turned, held):
    project(normed_ref, w_ref, g_ref, turned, held)
    size = stay_ref.shape[0] // 2
    for d, ref in enumerate((stay_ref, stay_ref, move_ref, move_ref)):
        ref[d % 2 * size : (d % 2 + 1) * size] = owner_block(held, d, size)


def left_kernel(lens_ref, normed_ref, w_ref, g_ref, *refs):
    (stay_ref, move_ref), outs, (masks_ref, turned, held) = refs[:2], refs[2:-3], refs[-3:]
    tile_rows = held.shape[0] // normed_ref.shape[1] * 2
    pairs, keeps, share = make_masks(lens_ref, tile_rows, held.shape[1] // 2)
    project(normed_ref, w_ref, g_ref, turned, held, pairs)
    masks_ref[...] = jnp.concatenate(
        pairs + keeps + [share] * (masks_ref.shape[0] - len(pairs) - len(keeps)), 0
    )
    size = stay_ref.shape[0] // 2
    for d, ref in enumerate(outs):
        right_ref = (stay_ref, move_ref)[d // 2]
        ref[:size] = owner_block(held, d, size)
        ref[size:] = right_ref[d % 2 * size : (d % 2 + 1) * size]


def gate_kernel(x_ref, normed_ref, gw_ref, ow_ref, dw_ref, gate_ref, x_turned_ref, ow_turned, dw_turned):
    tile_rows, tile_cols, channels = x_ref.shape
    share = channels // OWNERS
    half = share // 2
    blocks = [
        ow_ref[o * share + g * half : o * share + (g + 1) * half].astype(jnp.float32)
        for g in (0, 1)
        for o in range(OWNERS)
    ]
    ow_turned[...] = jnp.concatenate(blocks, 0).T.astype(jnp.bfloat16)
    dw_turned[...] = dw_ref[...].astype(jnp.float32).T.astype(jnp.bfloat16)
    gate_turned = gw_ref[...].astype(jnp.float32).T.astype(jnp.bfloat16)
    for first in range(0, tile_rows, 2):
        at = slice(first * tile_cols, (first + 2) * tile_cols)
        gate_ref[:, at] = sigmoid(nt_dot(gate_turned, normed_ref[at]))
        x = x_ref[first : first + 2].astype(jnp.float32).reshape(2 * tile_cols, channels)
        x_turned_ref[:, at] = x.T


def tri_kernel(masks_ref, own, core, near, near_over, far, far_over, cross, cross_over, *refs):
    outs, rights = refs[:-1], refs[-1]
    half, _, width = rights.shape
    size = own.shape[0] // 2
    tile_rows = size // half
    side = OWNERS * tile_rows
    me, col = lax.axis_index("row"), lax.axis_index("col")
    lefts = (own, core, near, near_over)
    pieces = (
        (0, own, size),
        (1, core, size),
        (2, near, size),
        (3, near_over, size),
        (4, far, 0),
        (5, far_over, size),
        (6, cross, 0),
        (7, cross_over, size),
    )
    for away, ref, start in pieces:
        at = pl.multiple_of((me ^ away) * tile_rows, tile_rows)
        for m in range(half):
            rights[m, pl.ds(at, tile_rows), :] = ref[
                start + m * tile_rows : start + (m + 1) * tile_rows
            ]
    low = lanes_of((side, width)) < width // 2
    first = masks_ref.shape[0] // 2
    keep = jnp.concatenate([masks_ref[first : first + 1], masks_ref[first + 1 : first + 2]], 1)
    for m in range(half):
        left = jnp.concatenate(
            [ref[m * tile_rows : (m + 1) * tile_rows] for ref in lefts], 0
        )
        pieces = []
        for dx in (0, 1):
            block = rights[m, pl.ds(pl.multiple_of((col ^ dx) * side, side), side), :]
            block = block.astype(jnp.float32)
            pieces += [jnp.where(low, block, 0.0), jnp.where(low, 0.0, block)]
        right = jnp.concatenate(pieces, 0).astype(jnp.bfloat16)
        product = (nt_dot(left, right) * keep).astype(jnp.bfloat16)
        for d in range(OWNERS):
            for dx in (0, 1):
                at = d % 2 * size + m * tile_rows
                outs[d // 2 * 2 + dx][at : at + tile_rows] = product[
                    d * tile_rows : (d + 1) * tile_rows, dx * width : (dx + 1) * width
                ]


def finish_kernel(masks_ref, x_ref, gate_ref, bins_ref, ow_ref, dw_ref, *refs):
    parts, overs = refs[:OWNERS], refs[OWNERS : 2 * OWNERS]
    out_ref, loss_ref, held = refs[2 * OWNERS :]
    channels = x_ref.shape[0]
    size, width = parts[0].shape[0] // 2, parts[0].shape[1]
    half = channels // 2 // OWNERS
    tile_rows, tile_cols = size // half, width // 2
    packed = OWNERS * half
    owner = owner_place()
    total = jnp.zeros((tile_rows, width), jnp.float32)
    for d in range(OWNERS):
        refs, at = ((parts, 0), (overs, size))[d % 2]
        a, b = [refs[d // 2 * 2 + dx][at : at + size].astype(jnp.float32) for dx in (0, 1)]
        block = a + b
        held[pl.ds(pl.multiple_of((owner ^ d) * size, size), size), :] = block
        total = total + jnp.sum(block.reshape(half, tile_rows, width), 0)
    average = (total + pltpu.roll(total, tile_cols, 1)) * (1.0 / channels)
    total = jnp.zeros((tile_rows, width), jnp.float32)
    for om in range(packed):
        centred = held[om * tile_rows : (om + 1) * tile_rows] - average
        total = total + centred * centred
    spread = (total + pltpu.roll(total, tile_cols, 1)) * (1.0 / channels)
    scale = lax.rsqrt(spread + 1e-05)
    low = lanes_of((packed, width)) < tile_cols
    bin_ids = lax.broadcasted_iota(jnp.int32, (dw_ref.shape[0], width), 0)
    loss = jnp.zeros((1, width), jnp.float32)
    for first in range(0, tile_rows, 2):
        a, b = [
            (held[pl.ds(ii, packed, stride=tile_rows), :] - average[ii : ii + 1]) * scale[ii : ii + 1]
            for ii in (first, first + 1)
        ]
        normed = jnp.concatenate(
            [
                jnp.where(low, a, pltpu.roll(b, tile_cols, 1)),
                jnp.where(low, pltpu.roll(a, tile_cols, 1), b),
            ],
            0,
        ).astype(jnp.bfloat16)
        update = jnp.dot(ow_ref[...], normed, preferred_element_type=jnp.float32)
        at = slice(first * tile_cols, (first + 2) * tile_cols)
        pair_out = (x_ref[:, at] + gate_ref[:, at] * update).astype(jnp.bfloat16)
        out_ref[:, at] = pair_out
        logits = jnp.dot(dw_ref[...], pair_out, preferred_element_type=jnp.float32)
        log_total = jnp.log(jnp.sum(jnp.exp(logits), axis=0, keepdims=True))
        bins = bins_ref[first // 2 : first // 2 + 1]
        picked = jnp.sum(jnp.where(bin_ids == bins, logits, 0.0), axis=0, keepdims=True)
        loss = loss + masks_ref[first // 2 : first // 2 + 1] * (log_total - picked)
    last = masks_ref.shape[0] - 1
    loss = jnp.sum(loss * masks_ref[last : last + 1], axis=1, keepdims=True)
    loss_ref[...] = jnp.broadcast_to(loss[None], loss_ref.shape)


def turn_back_kernel(turned_ref, out_ref):
    tile_rows, tile_cols, channels = out_ref.shape
    for first in range(0, tile_rows, 2):
        block = turned_ref[:, first * tile_cols : (first + 2) * tile_cols].astype(jnp.float32).T
        out_ref[first : first + 2] = block.astype(jnp.bfloat16).reshape(2, tile_cols, channels)


def exchange(value, places, mask):
    return lax.ppermute(value, AXES, [(at, at ^ mask) for at in range(places)])


def call(kernel, outs, scratch=(), specs=None, out_specs=None, args=(), flops=0):
    return pl.pallas_call(
        kernel,
        out_shape=outs,
        in_specs=specs if specs is not None else [VMEM] * len(args),
        out_specs=out_specs if out_specs is not None else jax.tree.map(lambda _: VMEM, outs),
        scratch_shapes=list(scratch),
        compiler_params=PARAMS,
        cost_estimate=pl.CostEstimate(flops=flops, bytes_accessed=1 << 20, transcendentals=1 << 18),
    )(*args)


def by_kernels(
    pair_repr,
    distance_bins,
    chain_lengths,
    left_weight,
    left_gate_weight,
    right_weight,
    right_gate_weight,
    out_weight,
    out_gate_weight,
    dist_weight,
):
    tile_rows, tile_cols, channels = pair_repr.shape
    rows, cols = lax.axis_size("row"), lax.axis_size("col")
    places = rows * cols
    width = 2 * tile_cols
    spots = tile_rows * tile_cols
    size = channels // OWNERS // 2 * tile_rows
    bf16, f32 = jnp.bfloat16, jnp.float32
    struct = jax.ShapeDtypeStruct
    turned = pltpu.VMEM((2 * channels, channels), bf16)
    held = pltpu.VMEM((OWNERS * size, width), f32)
    over_x, over_core, over_z, over_half = 1, cols, 2 * cols, OWNERS * cols
    normed = call(
        norm_kernel, struct((spots, channels), bf16), args=(pair_repr,), flops=1 << 30
    )
    stay, move = call(
        right_kernel,
        [struct((2 * size, width), bf16)] * 2,
        [turned, held],
        args=(normed, right_weight, right_gate_weight),
        flops=4 * spots * channels * channels,
    )
    cross = exchange(move, places, over_half + over_z)
    far = exchange(stay, places, over_half)
    own, core, near, near_over, masks = call(
        left_kernel,
        [struct((2 * size, width), bf16)] * OWNERS + [struct((tile_rows, width), f32)],
        [turned, held],
        [SMEM] + [VMEM] * 5,
        args=(chain_lengths, normed, left_weight, left_gate_weight, stay, move),
        flops=4 * spots * channels * channels,
    )
    near_over = exchange(near_over, places, over_z + over_core)
    near = exchange(near, places, over_z)
    core, far_over, cross_over = [
        exchange(value, places, over_core) for value in (core, far, cross)
    ]
    parts = call(
        tri_kernel,
        [struct((2 * size, width), bf16)] * OWNERS,
        [pltpu.VMEM((size // tile_rows, rows * tile_rows, width), bf16)],
        args=(masks, own, core, near, near_over, far, far_over, cross, cross_over),
        flops=8 * size * 2 * tile_rows * 2 * width,
    )
    parts = [parts[0]] + [
        exchange(parts[d], places, d // 2 * over_z + d % 2 * over_x) for d in range(1, OWNERS)
    ]
    parts += [exchange(value, places, over_core) for value in parts]
    gate, x_turned, out_turned, dist_turned = call(
        gate_kernel,
        [
            struct((channels, spots), f32),
            struct((channels, spots), f32),
            struct((channels, channels), bf16),
            struct(dist_weight.shape[::-1], bf16),
        ],
        args=(pair_repr, normed, out_gate_weight, out_weight, dist_weight),
        flops=2 * spots * channels * channels,
    )
    pair_out, loss = call(
        finish_kernel,
        [struct((channels, spots), bf16), struct((places, 8, 128), f32)],
        [held],
        args=(
            masks,
            x_turned,
            gate,
            distance_bins.reshape(tile_rows // 2, width),
            out_turned,
            dist_turned,
            *parts,
        ),
        flops=6 * spots * channels * channels,
    )
    pair_out = call(turn_back_kernel, struct(pair_repr.shape, bf16), args=(pair_out,), flops=1 << 26)
    loss = lax.all_to_all(loss, AXES, 0, 0, tiled=True)
    return (pair_out, jnp.sum(loss, axis=0)[0, :1])


def by_all_to_all(
    pair_repr,
    distance_bins,
    chain_lengths,
    left_weight,
    left_gate_weight,
    right_weight,
    right_gate_weight,
    out_weight,
    out_gate_weight,
    dist_weight,
):
    tile_rows, tile_cols, channels = pair_repr.shape
    rows, cols = lax.axis_size("row"), lax.axis_size("col")
    peers = rows * cols
    share = channels // peers
    residues = tile_rows * rows
    spots = tile_rows * tile_cols
    live_count = residues - chain_lengths[chain_lengths.shape[0] - 1]
    row_place = lax.axis_index("row") * tile_rows + jnp.arange(tile_rows, dtype=jnp.int32)
    col_place = lax.axis_index("col") * tile_cols + jnp.arange(tile_cols, dtype=jnp.int32)
    live_rows = (row_place < live_count).astype(jnp.float32)
    live_cols = (col_place < live_count).astype(jnp.float32)
    flat_mask = (live_rows[:, None] * live_cols[None, :]).reshape(-1)
    normed = layer_norm(pair_repr.astype(jnp.float32), -1).astype(jnp.bfloat16)
    normed = normed.reshape(spots, channels)

    def project_turned(weight):
        return lax.dot_general(
            weight, normed, (((0,), (1,)), ((), ())), preferred_element_type=jnp.float32
        )

    def gated(gate_weight, weight):
        values = jax.nn.sigmoid(project_turned(gate_weight)) * project_turned(weight)
        return (values * flat_mask[None, :]).astype(jnp.bfloat16)

    left = gated(left_gate_weight, left_weight).reshape(peers, share, tile_rows, tile_cols)
    right = gated(right_gate_weight, right_weight).reshape(peers, share, tile_rows, tile_cols)
    both = jnp.concatenate([left, right], axis=3).reshape(peers, share * tile_rows, 2 * tile_cols)
    owned = lax.all_to_all(both, AXES, split_axis=0, concat_axis=0, tiled=True)
    owned = owned.reshape(rows, cols, share, tile_rows, 2, tile_cols)
    owned = owned.transpose(4, 2, 0, 3, 1, 5).reshape(2, share, residues, residues)
    tri = jnp.einsum(
        "cik,cjk->cij", owned[0], owned[1], preferred_element_type=jnp.float32
    ).astype(jnp.bfloat16)
    tri = tri.reshape(share, rows, tile_rows, cols, tile_cols).transpose(1, 3, 0, 2, 4)
    tri = tri.reshape(peers, share, spots)
    tri = lax.all_to_all(tri, AXES, split_axis=0, concat_axis=0, tiled=True)
    tri = tri.reshape(channels, spots).astype(jnp.float32)
    tri_normed = layer_norm(tri, 0).astype(jnp.bfloat16)
    out_gate = jax.nn.sigmoid(jnp.dot(normed, out_gate_weight, preferred_element_type=jnp.float32))
    update = out_gate * tn_dot(tri_normed, out_weight)
    pair_out = (pair_repr.astype(jnp.float32).reshape(spots, channels) + update).astype(
        jnp.bfloat16
    )
    logits = jnp.dot(pair_out, dist_weight, preferred_element_type=jnp.float32)
    log_total = jnp.log(jnp.sum(jnp.exp(logits), axis=-1))
    bin_ids = jnp.arange(logits.shape[1], dtype=jnp.int32)
    picked = jnp.sum(
        jnp.where(bin_ids[None, :] == distance_bins.reshape(-1, 1), logits, 0.0), axis=-1
    )
    loss_sum = jnp.sum(flat_mask * (log_total - picked))
    sums = lax.all_to_all(
        jnp.full((peers, 1, 128), loss_sum), AXES, split_axis=0, concat_axis=0, tiled=True
    )
    pair_count = (live_count * live_count).astype(jnp.float32)
    loss_value = (jnp.sum(sums[:, 0, 0]) / pair_count).reshape(1)
    return (pair_out.reshape(pair_repr.shape), loss_value)


def on_device(pair_repr, *others):
    tile_rows, tile_cols, channels = pair_repr.shape
    rows, cols = lax.axis_size("row"), lax.axis_size("col")
    fits = (
        rows == 2 * OWNERS
        and cols == 2
        and tile_rows * rows == tile_cols * cols
        and 2 * tile_cols == 128
        and tile_rows == 16
        and channels % (32 * OWNERS) == 0
    )
    return (by_kernels if fits else by_all_to_all)(pair_repr, *others)


def solution(mesh):
    in_specs = (
        P(("groups", "row"), "col", None),
        P(("groups", "row"), "col"),
        P("groups"),
        P(),
        P(),
        P(),
        P(),
        P(),
        P(),
        P(),
    )
    out_specs = (P(("groups", "row"), "col", None), P("groups"))
    return jax.shard_map(
        on_device, mesh=mesh, in_specs=in_specs, out_specs=out_specs, check_vma=False
    )
```

```python
import jax
import jax.numpy as jnp
from jax import lax
from jax.experimental import pallas as pl
from jax.experimental.pallas import tpu as pltpu
from jax.sharding import PartitionSpec as P

AXES = ("row", "col")
OWNERS = 4
VMEM = pl.BlockSpec(memory_space=pltpu.VMEM)
SMEM = pl.BlockSpec(memory_space=pltpu.SMEM)
PARAMS = pltpu.CompilerParams(vmem_limit_bytes=24 * 1024 * 1024)


def layer_norm(values, axis):
    average = jnp.mean(values, axis=axis, keepdims=True)
    centred = values - average
    spread = jnp.mean(centred * centred, axis=axis, keepdims=True)
    return centred * lax.rsqrt(spread + 1e-05)


def sigmoid(values):
    return 0.5 * jnp.tanh(0.5 * values) + 0.5


def nt_dot(a, b):
    return lax.dot_general(a, b, (((1,), (1,)), ((), ())), preferred_element_type=jnp.float32)


def tn_dot(a, b):
    return lax.dot_general(a, b, (((0,), (0,)), ((), ())), preferred_element_type=jnp.float32)


def lanes_of(shape):
    return lax.broadcasted_iota(jnp.int32, shape, 1)


def make_masks(lens_ref, tile_rows, tile_cols):
    live = tile_rows * lax.axis_size("row") - lens_ref[lens_ref.shape[0] - 1]
    lane = lanes_of((1, 2 * tile_cols))
    upper = (lane >= tile_cols).astype(jnp.int32)
    place = lane - tile_cols * upper
    row, col = lax.axis_index("row") * tile_rows, lax.axis_index("col")
    keeps = [(place + (col ^ dx) * tile_cols < live).astype(jnp.float32) for dx in (0, 1)]
    pairs = [
        (row + first + upper < live).astype(jnp.float32) * keeps[0]
        for first in range(0, tile_rows, 2)
    ]
    count = jnp.full(lane.shape, live * live, jnp.int32).astype(jnp.float32)
    return pairs, keeps, 1.0 / count


def turn(w_refs, turned):
    channels = w_refs[0].shape[0]
    share = channels // OWNERS
    half = share // 2
    for at, w_ref in enumerate(w_refs):
        w = w_ref[...].astype(jnp.float32).T
        blocks = [
            w[o * share + g * half : o * share + (g + 1) * half] for g in (0, 1) for o in range(OWNERS)
        ]
        turned[at * channels : (at + 1) * channels] = jnp.concatenate(blocks, 0).astype(jnp.bfloat16)


def project(normed_ref, w_ref, g_ref, turned, held, masks=None):
    channels = normed_ref.shape[1]
    packed = channels // 2
    tile_rows, tile_cols = held.shape[0] // packed, held.shape[1] // 2
    turn((w_ref, g_ref), turned)
    low = lanes_of((packed, 2 * tile_cols)) < tile_cols
    for first in range(0, tile_rows, 2):
        flat = nt_dot(turned[...], normed_ref[first * tile_cols : (first + 2) * tile_cols])
        value = sigmoid(flat[channels:]) * flat[:channels]
        if masks is not None:
            value = value * masks[first // 2]
        a, b = value[:packed], value[packed:]
        held[pl.ds(first, packed, stride=tile_rows), :] = jnp.where(
            low, a, pltpu.roll(b, tile_cols, 1)
        )
        held[pl.ds(first + 1, packed, stride=tile_rows), :] = jnp.where(
            low, pltpu.roll(a, tile_cols, 1), b
        )


def owner_place():
    return lax.axis_index("row") // 2 % 2 * 2 + lax.axis_index("col")


def owner_block(held, d, size):
    at = pl.multiple_of((owner_place() ^ d) * size, size)
    return held[pl.ds(at, size)].astype(jnp.bfloat16)


def norm_kernel(x_ref, normed_ref):
    x = x_ref[...].astype(jnp.float32).reshape(normed_ref.shape)
    normed_ref[...] = layer_norm(x, -1).astype(jnp.bfloat16)


def right_kernel(normed_ref, w_ref, g_ref, all_ref, *refs):
    outs, (turned, held) = refs[:OWNERS], refs[OWNERS:]
    project(normed_ref, w_ref, g_ref, turned, held)
    for d, ref in enumerate(outs):
        ref[...] = owner_block(held, d, ref.shape[0])
    all_ref[...] = held[...].astype(jnp.bfloat16)


def left_kernel(lens_ref, normed_ref, w_ref, g_ref, all_ref, near_ref, masks_ref, turned, held):
    tile_rows = held.shape[0] // normed_ref.shape[1] * 2
    pairs, keeps, share = make_masks(lens_ref, tile_rows, held.shape[1] // 2)
    project(normed_ref, w_ref, g_ref, turned, held, pairs)
    masks_ref[...] = jnp.concatenate(
        pairs + keeps + [share] * (masks_ref.shape[0] - len(pairs) - len(keeps)), 0
    )
    size = near_ref.shape[1] // 2
    for o in range(OWNERS):
        near_ref[o, :size] = held[o * size : (o + 1) * size].astype(jnp.bfloat16)
        near_ref[o, size:] = all_ref[o * size : (o + 1) * size]


def gate_kernel(x_ref, normed_ref, gw_ref, ow_ref, dw_ref, gate_ref, x_turned_ref, ow_turned, dw_turned):
    tile_rows, tile_cols, channels = x_ref.shape
    share = channels // OWNERS
    half = share // 2
    blocks = [
        ow_ref[o * share + g * half : o * share + (g + 1) * half].astype(jnp.float32)
        for g in (0, 1)
        for o in range(OWNERS)
    ]
    ow_turned[...] = jnp.concatenate(blocks, 0).T.astype(jnp.bfloat16)
    dw_turned[...] = dw_ref[...].astype(jnp.float32).T.astype(jnp.bfloat16)
    gate_turned = gw_ref[...].astype(jnp.float32).T.astype(jnp.bfloat16)
    for first in range(0, tile_rows, 2):
        at = slice(first * tile_cols, (first + 2) * tile_cols)
        gate_ref[:, at] = sigmoid(nt_dot(gate_turned, normed_ref[at]))
        x = x_ref[first : first + 2].astype(jnp.float32).reshape(2 * tile_cols, channels)
        x_turned_ref[:, at] = x.T


def tri_kernel(masks_ref, near_ref, near_over_ref, *refs):
    far, far_over = refs[:OWNERS], refs[OWNERS : 2 * OWNERS]
    outs, rights = refs[2 * OWNERS : -1], refs[-1]
    size, width = far[0].shape
    half = rights.shape[1]
    tile_rows = size // half
    side = width // 2
    me, col, owner = lax.axis_index("row"), lax.axis_index("col"), owner_place()
    for d in range(OWNERS):
        away = d // 2 * 2
        for step, load in (
            (0, lambda at: near_ref[owner ^ d, size + at : size + at + tile_rows]),
            (1, lambda at: near_over_ref[owner ^ d, size + at : size + at + tile_rows]),
            (4, lambda at: far[d][at : at + tile_rows]),
            (5, lambda at: far_over[d][at : at + tile_rows]),
        ):
            place = pl.multiple_of((me ^ (away + step)) * tile_rows, tile_rows)
            for m in range(half):
                rights[d % 2, m, pl.ds(place, tile_rows), :] = load(m * tile_rows)
    low = lanes_of((side, width)) < side
    first = masks_ref.shape[0] // 2
    keep = jnp.concatenate([masks_ref[first : first + 1], masks_ref[first + 1 : first + 2]], 1)
    for m in range(half):
        at = slice(m * tile_rows, (m + 1) * tile_rows)
        product = 0.0
        for dk in (0, 1):
            left = jnp.concatenate([near_ref[owner ^ dk, at], near_ref[owner ^ (2 + dk), at]], 0)
            pieces = []
            for dx in (0, 1):
                block = rights[dk, m, pl.ds(pl.multiple_of((col ^ dx) * side, side), side), :]
                block = block.astype(jnp.float32)
                pieces += [jnp.where(low, block, 0.0), jnp.where(low, 0.0, block)]
            right = jnp.concatenate(pieces, 0).astype(jnp.bfloat16)
            product = product + nt_dot(left, right)
        product = (product * keep).astype(jnp.bfloat16)
        for dz in (0, 1):
            for dx in (0, 1):
                outs[2 * dz + dx][at] = product[
                    dz * tile_rows : (dz + 1) * tile_rows, dx * width : (dx + 1) * width
                ]


def finish_kernel(masks_ref, x_ref, gate_ref, bins_ref, ow_ref, dw_ref, *refs):
    parts, (out_ref, loss_ref, held) = refs[:OWNERS], refs[OWNERS:]
    channels = x_ref.shape[0]
    size, width = parts[0].shape
    half = channels // 2 // OWNERS
    tile_rows, tile_cols = size // half, width // 2
    packed = OWNERS * half
    owner = owner_place()
    total = jnp.zeros((tile_rows, width), jnp.float32)
    for d in range(OWNERS):
        block = parts[d][...].astype(jnp.float32)
        held[pl.ds(pl.multiple_of((owner ^ d) * size, size), size), :] = block
        total = total + jnp.sum(block.reshape(half, tile_rows, width), 0)
    average = (total + pltpu.roll(total, tile_cols, 1)) * (1.0 / channels)
    total = jnp.zeros((tile_rows, width), jnp.float32)
    for om in range(packed):
        centred = held[om * tile_rows : (om + 1) * tile_rows] - average
        total = total + centred * centred
    spread = (total + pltpu.roll(total, tile_cols, 1)) * (1.0 / channels)
    scale = lax.rsqrt(spread + 1e-05)
    low = lanes_of((packed, width)) < tile_cols
    bin_ids = lax.broadcasted_iota(jnp.int32, (dw_ref.shape[0], width), 0)
    loss = jnp.zeros((1, width), jnp.float32)
    for first in range(0, tile_rows, 2):
        a, b = [
            (held[pl.ds(ii, packed, stride=tile_rows), :] - average[ii : ii + 1]) * scale[ii : ii + 1]
            for ii in (first, first + 1)
        ]
        normed = jnp.concatenate(
            [
                jnp.where(low, a, pltpu.roll(b, tile_cols, 1)),
                jnp.where(low, pltpu.roll(a, tile_cols, 1), b),
            ],
            0,
        ).astype(jnp.bfloat16)
        update = jnp.dot(ow_ref[...], normed, preferred_element_type=jnp.float32)
        at = slice(first * tile_cols, (first + 2) * tile_cols)
        pair_out = (x_ref[:, at] + gate_ref[:, at] * update).astype(jnp.bfloat16)
        out_ref[:, at] = pair_out
        logits = jnp.dot(dw_ref[...], pair_out, preferred_element_type=jnp.float32)
        log_total = jnp.log(jnp.sum(jnp.exp(logits), axis=0, keepdims=True))
        bins = bins_ref[first // 2 : first // 2 + 1]
        picked = jnp.sum(jnp.where(bin_ids == bins, logits, 0.0), axis=0, keepdims=True)
        loss = loss + masks_ref[first // 2 : first // 2 + 1] * (log_total - picked)
    last = masks_ref.shape[0] - 1
    loss = jnp.sum(loss * masks_ref[last : last + 1], axis=1, keepdims=True)
    loss_ref[...] = jnp.broadcast_to(loss[None], loss_ref.shape)


def turn_back_kernel(turned_ref, out_ref):
    tile_rows, tile_cols, channels = out_ref.shape
    for first in range(0, tile_rows, 2):
        block = turned_ref[:, first * tile_cols : (first + 2) * tile_cols].astype(jnp.float32).T
        out_ref[first : first + 2] = block.astype(jnp.bfloat16).reshape(2, tile_cols, channels)


def exchange(value, places, mask):
    return lax.ppermute(value, AXES, [(at, at ^ mask) for at in range(places)])


def call(kernel, outs, scratch=(), specs=None, out_specs=None, args=(), flops=0):
    return pl.pallas_call(
        kernel,
        out_shape=outs,
        in_specs=specs if specs is not None else [VMEM] * len(args),
        out_specs=out_specs if out_specs is not None else jax.tree.map(lambda _: VMEM, outs),
        scratch_shapes=list(scratch),
        compiler_params=PARAMS,
        cost_estimate=pl.CostEstimate(flops=flops, bytes_accessed=1 << 20, transcendentals=1 << 18),
    )(*args)


def by_kernels(
    pair_repr,
    distance_bins,
    chain_lengths,
    left_weight,
    left_gate_weight,
    right_weight,
    right_gate_weight,
    out_weight,
    out_gate_weight,
    dist_weight,
):
    tile_rows, tile_cols, channels = pair_repr.shape
    rows, cols = lax.axis_size("row"), lax.axis_size("col")
    places = rows * cols
    width = 2 * tile_cols
    spots = tile_rows * tile_cols
    size = channels // OWNERS // 2 * tile_rows
    bf16, f32 = jnp.bfloat16, jnp.float32
    struct = jax.ShapeDtypeStruct
    turned = pltpu.VMEM((2 * channels, channels), bf16)
    held = pltpu.VMEM((OWNERS * size, width), f32)
    over_x, over_core, over_z, over_half = 1, cols, 2 * cols, OWNERS * cols
    normed = call(
        norm_kernel, struct((spots, channels), bf16), args=(pair_repr,), flops=1 << 30
    )
    whole, *rights = call(
        right_kernel,
        [struct((OWNERS * size, width), bf16)] + [struct((size, width), bf16)] * OWNERS,
        [turned, held],
        args=(normed, right_weight, right_gate_weight),
        flops=4 * spots * channels * channels,
    )
    over = [d // 2 * over_z + d % 2 * over_x for d in range(OWNERS)]
    far = [exchange(rights[d], places, over_half + over[d]) for d in range(OWNERS)]
    near, masks = call(
        left_kernel,
        [struct((OWNERS, 2 * size, width), bf16), struct((tile_rows, width), f32)],
        [turned, held],
        [SMEM] + [VMEM] * 4,
        args=(chain_lengths, normed, left_weight, left_gate_weight, whole),
        flops=4 * spots * channels * channels,
    )
    sides = [
        [part * over_half + z * over_z + core * over_core + x for z in (0, 1) for x in (0, 1)]
        for part in (0, 1)
        for core in (0, 1)
    ]
    near = lax.all_to_all(near, AXES, 0, 0, axis_index_groups=sides, tiled=True)
    near_over = exchange(near, places, over_core)
    far_over = [exchange(value, places, over_core) for value in far]
    parts = call(
        tri_kernel,
        [struct((size, width), bf16)] * OWNERS,
        [pltpu.VMEM((cols, size // tile_rows, rows * tile_rows, width), bf16)],
        args=(masks, near, near_over, *far, *far_over),
        flops=8 * size * 2 * tile_rows * 2 * width,
    )
    parts = [parts[0]] + [exchange(parts[d], places, over[d]) for d in range(1, OWNERS)]
    gate, x_turned, out_turned, dist_turned = call(
        gate_kernel,
        [
            struct((channels, spots), f32),
            struct((channels, spots), f32),
            struct((channels, channels), bf16),
            struct(dist_weight.shape[::-1], bf16),
        ],
        args=(pair_repr, normed, out_gate_weight, out_weight, dist_weight),
        flops=2 * spots * channels * channels,
    )
    pair_out, loss = call(
        finish_kernel,
        [struct((channels, spots), bf16), struct((places, 8, 128), f32)],
        [held],
        args=(
            masks,
            x_turned,
            gate,
            distance_bins.reshape(tile_rows // 2, width),
            out_turned,
            dist_turned,
            *parts,
        ),
        flops=6 * spots * channels * channels,
    )
    pair_out = call(turn_back_kernel, struct(pair_repr.shape, bf16), args=(pair_out,), flops=1 << 26)
    loss = lax.all_to_all(loss, AXES, 0, 0, tiled=True)
    return (pair_out, jnp.sum(loss, axis=0)[0, :1])


def by_all_to_all(
    pair_repr,
    distance_bins,
    chain_lengths,
    left_weight,
    left_gate_weight,
    right_weight,
    right_gate_weight,
    out_weight,
    out_gate_weight,
    dist_weight,
):
    tile_rows, tile_cols, channels = pair_repr.shape
    rows, cols = lax.axis_size("row"), lax.axis_size("col")
    peers = rows * cols
    share = channels // peers
    residues = tile_rows * rows
    spots = tile_rows * tile_cols
    live_count = residues - chain_lengths[chain_lengths.shape[0] - 1]
    row_place = lax.axis_index("row") * tile_rows + jnp.arange(tile_rows, dtype=jnp.int32)
    col_place = lax.axis_index("col") * tile_cols + jnp.arange(tile_cols, dtype=jnp.int32)
    live_rows = (row_place < live_count).astype(jnp.float32)
    live_cols = (col_place < live_count).astype(jnp.float32)
    flat_mask = (live_rows[:, None] * live_cols[None, :]).reshape(-1)
    normed = layer_norm(pair_repr.astype(jnp.float32), -1).astype(jnp.bfloat16)
    normed = normed.reshape(spots, channels)

    def project_turned(weight):
        return lax.dot_general(
            weight, normed, (((0,), (1,)), ((), ())), preferred_element_type=jnp.float32
        )

    def gated(gate_weight, weight):
        values = jax.nn.sigmoid(project_turned(gate_weight)) * project_turned(weight)
        return (values * flat_mask[None, :]).astype(jnp.bfloat16)

    left = gated(left_gate_weight, left_weight).reshape(peers, share, tile_rows, tile_cols)
    right = gated(right_gate_weight, right_weight).reshape(peers, share, tile_rows, tile_cols)
    both = jnp.concatenate([left, right], axis=3).reshape(peers, share * tile_rows, 2 * tile_cols)
    owned = lax.all_to_all(both, AXES, split_axis=0, concat_axis=0, tiled=True)
    owned = owned.reshape(rows, cols, share, tile_rows, 2, tile_cols)
    owned = owned.transpose(4, 2, 0, 3, 1, 5).reshape(2, share, residues, residues)
    tri = jnp.einsum(
        "cik,cjk->cij", owned[0], owned[1], preferred_element_type=jnp.float32
    ).astype(jnp.bfloat16)
    tri = tri.reshape(share, rows, tile_rows, cols, tile_cols).transpose(1, 3, 0, 2, 4)
    tri = tri.reshape(peers, share, spots)
    tri = lax.all_to_all(tri, AXES, split_axis=0, concat_axis=0, tiled=True)
    tri = tri.reshape(channels, spots).astype(jnp.float32)
    tri_normed = layer_norm(tri, 0).astype(jnp.bfloat16)
    out_gate = jax.nn.sigmoid(jnp.dot(normed, out_gate_weight, preferred_element_type=jnp.float32))
    update = out_gate * tn_dot(tri_normed, out_weight)
    pair_out = (pair_repr.astype(jnp.float32).reshape(spots, channels) + update).astype(
        jnp.bfloat16
    )
    logits = jnp.dot(pair_out, dist_weight, preferred_element_type=jnp.float32)
    log_total = jnp.log(jnp.sum(jnp.exp(logits), axis=-1))
    bin_ids = jnp.arange(logits.shape[1], dtype=jnp.int32)
    picked = jnp.sum(
        jnp.where(bin_ids[None, :] == distance_bins.reshape(-1, 1), logits, 0.0), axis=-1
    )
    loss_sum = jnp.sum(flat_mask * (log_total - picked))
    sums = lax.all_to_all(
        jnp.full((peers, 1, 128), loss_sum), AXES, split_axis=0, concat_axis=0, tiled=True
    )
    pair_count = (live_count * live_count).astype(jnp.float32)
    loss_value = (jnp.sum(sums[:, 0, 0]) / pair_count).reshape(1)
    return (pair_out.reshape(pair_repr.shape), loss_value)


def on_device(pair_repr, *others):
    tile_rows, tile_cols, channels = pair_repr.shape
    rows, cols = lax.axis_size("row"), lax.axis_size("col")
    fits = (
        rows == 2 * OWNERS
        and cols == 2
        and tile_rows * rows == tile_cols * cols
        and 2 * tile_cols == 128
        and tile_rows == 16
        and channels % (32 * OWNERS) == 0
    )
    return (by_kernels if fits else by_all_to_all)(pair_repr, *others)


def solution(mesh):
    in_specs = (
        P(("groups", "row"), "col", None),
        P(("groups", "row"), "col"),
        P("groups"),
        P(),
        P(),
        P(),
        P(),
        P(),
        P(),
        P(),
    )
    out_specs = (P(("groups", "row"), "col", None), P("groups"))
    return jax.shard_map(
        on_device, mesh=mesh, in_specs=in_specs, out_specs=out_specs, check_vma=False
    )
```

```python
import jax
import jax.numpy as jnp
from jax import lax
from jax.experimental import pallas as pl
from jax.experimental.pallas import tpu as pltpu
from jax.sharding import PartitionSpec as P

AXES = ("row", "col")
OWNERS = 4
VMEM = pl.BlockSpec(memory_space=pltpu.VMEM)
SMEM = pl.BlockSpec(memory_space=pltpu.SMEM)
PARAMS = pltpu.CompilerParams(vmem_limit_bytes=24 * 1024 * 1024)


def layer_norm(values, axis):
    average = jnp.mean(values, axis=axis, keepdims=True)
    centred = values - average
    spread = jnp.mean(centred * centred, axis=axis, keepdims=True)
    return centred * lax.rsqrt(spread + 1e-05)


def sigmoid(values):
    return 0.5 * jnp.tanh(0.5 * values) + 0.5


def nt_dot(a, b):
    return lax.dot_general(a, b, (((1,), (1,)), ((), ())), preferred_element_type=jnp.float32)


def tn_dot(a, b):
    return lax.dot_general(a, b, (((0,), (0,)), ((), ())), preferred_element_type=jnp.float32)


def lanes_of(shape):
    return lax.broadcasted_iota(jnp.int32, shape, 1)


def make_masks(lens_ref, tile_rows, tile_cols):
    live = tile_rows * lax.axis_size("row") - lens_ref[lens_ref.shape[0] - 1]
    lane = lanes_of((1, 2 * tile_cols))
    upper = (lane >= tile_cols).astype(jnp.int32)
    place = lane - tile_cols * upper
    row, col = lax.axis_index("row") * tile_rows, lax.axis_index("col")
    keeps = [(place + (col ^ dx) * tile_cols < live).astype(jnp.float32) for dx in (0, 1)]
    pairs = [
        (row + first + upper < live).astype(jnp.float32) * keeps[0]
        for first in range(0, tile_rows, 2)
    ]
    count = jnp.full(lane.shape, live * live, jnp.int32).astype(jnp.float32)
    return pairs, keeps, 1.0 / count


def turn(w_refs, turned):
    channels = w_refs[0].shape[0]
    share = channels // OWNERS
    half = share // 2
    for at, w_ref in enumerate(w_refs):
        w = w_ref[...].astype(jnp.float32).T
        blocks = [
            w[o * share + g * half : o * share + (g + 1) * half] for g in (0, 1) for o in range(OWNERS)
        ]
        turned[at * channels : (at + 1) * channels] = jnp.concatenate(blocks, 0).astype(jnp.bfloat16)


def project(normed_ref, w_ref, g_ref, turned, held, masks=None):
    channels = normed_ref.shape[1]
    packed = channels // 2
    tile_rows, tile_cols = held.shape[0] // packed, held.shape[1] // 2
    turn((w_ref, g_ref), turned)
    low = lanes_of((packed, 2 * tile_cols)) < tile_cols
    for first in range(0, tile_rows, 2):
        flat = nt_dot(turned[...], normed_ref[first * tile_cols : (first + 2) * tile_cols])
        value = sigmoid(flat[channels:]) * flat[:channels]
        if masks is not None:
            value = value * masks[first // 2]
        a, b = value[:packed], value[packed:]
        held[pl.ds(first, packed, stride=tile_rows), :] = jnp.where(
            low, a, pltpu.roll(b, tile_cols, 1)
        )
        held[pl.ds(first + 1, packed, stride=tile_rows), :] = jnp.where(
            low, pltpu.roll(a, tile_cols, 1), b
        )


def owner_place():
    return lax.axis_index("row") // 2 % 2 * 2 + lax.axis_index("col")


def owner_block(held, d, size):
    at = pl.multiple_of((owner_place() ^ d) * size, size)
    return held[pl.ds(at, size)].astype(jnp.bfloat16)


def norm_kernel(x_ref, normed_ref):
    x = x_ref[...].astype(jnp.float32).reshape(normed_ref.shape)
    normed_ref[...] = layer_norm(x, -1).astype(jnp.bfloat16)


def right_kernel(normed_ref, w_ref, g_ref, *refs):
    outs, (turned, held) = refs[:OWNERS], refs[OWNERS:]
    project(normed_ref, w_ref, g_ref, turned, held)
    for d, ref in enumerate(outs):
        ref[...] = owner_block(held, d, ref.shape[0])


def left_kernel(lens_ref, normed_ref, w_ref, g_ref, *refs):
    rights, outs = refs[:OWNERS], refs[OWNERS : 2 * OWNERS]
    masks_ref, turned, held = refs[2 * OWNERS :]
    tile_rows = held.shape[0] // normed_ref.shape[1] * 2
    pairs, keeps, share = make_masks(lens_ref, tile_rows, held.shape[1] // 2)
    project(normed_ref, w_ref, g_ref, turned, held, pairs)
    masks_ref[...] = jnp.concatenate(
        pairs + keeps + [share] * (masks_ref.shape[0] - len(pairs) - len(keeps)), 0
    )
    size = rights[0].shape[0]
    for d, ref in enumerate(outs):
        ref[:size] = owner_block(held, d, size)
        ref[size:] = rights[d][...]


def pack_kernel(*refs):
    size = refs[0].shape[0]
    for at, ref in enumerate(refs[:-1]):
        refs[-1][at * size : (at + 1) * size] = ref[...]


def gate_kernel(x_ref, normed_ref, gw_ref, ow_ref, dw_ref, gate_ref, x_turned_ref, ow_turned, dw_turned):
    tile_rows, tile_cols, channels = x_ref.shape
    share = channels // OWNERS
    half = share // 2
    blocks = [
        ow_ref[o * share + g * half : o * share + (g + 1) * half].astype(jnp.float32)
        for g in (0, 1)
        for o in range(OWNERS)
    ]
    ow_turned[...] = jnp.concatenate(blocks, 0).T.astype(jnp.bfloat16)
    dw_turned[...] = dw_ref[...].astype(jnp.float32).T.astype(jnp.bfloat16)
    gate_turned = gw_ref[...].astype(jnp.float32).T.astype(jnp.bfloat16)
    for first in range(0, tile_rows, 2):
        at = slice(first * tile_cols, (first + 2) * tile_cols)
        gate_ref[:, at] = sigmoid(nt_dot(gate_turned, normed_ref[at]))
        x = x_ref[first : first + 2].astype(jnp.float32).reshape(2 * tile_cols, channels)
        x_turned_ref[:, at] = x.T


def tri_kernel(masks_ref, far_over, *refs):
    near, far, near_over = [refs[at * OWNERS : (at + 1) * OWNERS] for at in range(3)]
    outs, rights = refs[3 * OWNERS : -1], refs[-1]
    size, width = far[0].shape
    half = rights.shape[1]
    tile_rows = size // half
    side = width // 2
    me, col = lax.axis_index("row"), lax.axis_index("col")
    for d in range(OWNERS):
        for step, ref, start in (
            (0, near[d], size),
            (1, near_over[d], near_over[d].shape[0] - size),
            (4, far[d], 0),
            (5, far_over, d * size),
        ):
            place = pl.multiple_of((me ^ (d // 2 * 2 + step)) * tile_rows, tile_rows)
            for m in range(half):
                at = start + m * tile_rows
                rights[d % 2, m, pl.ds(place, tile_rows), :] = ref[at : at + tile_rows]
    low = lanes_of((side, width)) < side
    first = masks_ref.shape[0] // 2
    keep = jnp.concatenate([masks_ref[first : first + 1], masks_ref[first + 1 : first + 2]], 1)
    for m in range(half):
        at = slice(m * tile_rows, (m + 1) * tile_rows)
        product = 0.0
        for dk in (0, 1):
            left = jnp.concatenate([near[dk][at], near[2 + dk][at]], 0)
            pieces = []
            for dx in (0, 1):
                block = rights[dk, m, pl.ds(pl.multiple_of((col ^ dx) * side, side), side), :]
                block = block.astype(jnp.float32)
                pieces += [jnp.where(low, block, 0.0), jnp.where(low, 0.0, block)]
            right = jnp.concatenate(pieces, 0).astype(jnp.bfloat16)
            product = product + nt_dot(left, right)
        product = (product * keep).astype(jnp.bfloat16)
        for dz in (0, 1):
            for dx in (0, 1):
                outs[2 * dz + dx][at] = product[
                    dz * tile_rows : (dz + 1) * tile_rows, dx * width : (dx + 1) * width
                ]


def finish_kernel(masks_ref, x_ref, gate_ref, bins_ref, ow_ref, dw_ref, *refs):
    parts, (out_ref, loss_ref, held) = refs[:OWNERS], refs[OWNERS:]
    channels = x_ref.shape[0]
    size, width = parts[0].shape
    half = channels // 2 // OWNERS
    tile_rows, tile_cols = size // half, width // 2
    packed = OWNERS * half
    owner = owner_place()
    total = jnp.zeros((tile_rows, width), jnp.float32)
    for d in range(OWNERS):
        block = parts[d][...].astype(jnp.float32)
        held[pl.ds(pl.multiple_of((owner ^ d) * size, size), size), :] = block
        total = total + jnp.sum(block.reshape(half, tile_rows, width), 0)
    average = (total + pltpu.roll(total, tile_cols, 1)) * (1.0 / channels)
    total = jnp.zeros((tile_rows, width), jnp.float32)
    for om in range(packed):
        centred = held[om * tile_rows : (om + 1) * tile_rows] - average
        total = total + centred * centred
    spread = (total + pltpu.roll(total, tile_cols, 1)) * (1.0 / channels)
    scale = lax.rsqrt(spread + 1e-05)
    low = lanes_of((packed, width)) < tile_cols
    bin_ids = lax.broadcasted_iota(jnp.int32, (dw_ref.shape[0], width), 0)
    loss = jnp.zeros((1, width), jnp.float32)
    for first in range(0, tile_rows, 2):
        a, b = [
            (held[pl.ds(ii, packed, stride=tile_rows), :] - average[ii : ii + 1]) * scale[ii : ii + 1]
            for ii in (first, first + 1)
        ]
        normed = jnp.concatenate(
            [
                jnp.where(low, a, pltpu.roll(b, tile_cols, 1)),
                jnp.where(low, pltpu.roll(a, tile_cols, 1), b),
            ],
            0,
        ).astype(jnp.bfloat16)
        update = jnp.dot(ow_ref[...], normed, preferred_element_type=jnp.float32)
        at = slice(first * tile_cols, (first + 2) * tile_cols)
        pair_out = (x_ref[:, at] + gate_ref[:, at] * update).astype(jnp.bfloat16)
        out_ref[:, at] = pair_out
        logits = jnp.dot(dw_ref[...], pair_out, preferred_element_type=jnp.float32)
        log_total = jnp.log(jnp.sum(jnp.exp(logits), axis=0, keepdims=True))
        bins = bins_ref[first // 2 : first // 2 + 1]
        picked = jnp.sum(jnp.where(bin_ids == bins, logits, 0.0), axis=0, keepdims=True)
        loss = loss + masks_ref[first // 2 : first // 2 + 1] * (log_total - picked)
    last = masks_ref.shape[0] - 1
    loss = jnp.sum(loss * masks_ref[last : last + 1], axis=1, keepdims=True)
    loss_ref[...] = jnp.broadcast_to(loss[None], loss_ref.shape)


def turn_back_kernel(turned_ref, out_ref):
    tile_rows, tile_cols, channels = out_ref.shape
    for first in range(0, tile_rows, 2):
        block = turned_ref[:, first * tile_cols : (first + 2) * tile_cols].astype(jnp.float32).T
        out_ref[first : first + 2] = block.astype(jnp.bfloat16).reshape(2, tile_cols, channels)


def exchange(value, places, mask):
    return lax.ppermute(value, AXES, [(at, at ^ mask) for at in range(places)])


def call(kernel, outs, scratch=(), specs=None, out_specs=None, args=(), flops=0):
    return pl.pallas_call(
        kernel,
        out_shape=outs,
        in_specs=specs if specs is not None else [VMEM] * len(args),
        out_specs=out_specs if out_specs is not None else jax.tree.map(lambda _: VMEM, outs),
        scratch_shapes=list(scratch),
        compiler_params=PARAMS,
        cost_estimate=pl.CostEstimate(flops=flops, bytes_accessed=1 << 20, transcendentals=1 << 18),
    )(*args)


def by_kernels(
    pair_repr,
    distance_bins,
    chain_lengths,
    left_weight,
    left_gate_weight,
    right_weight,
    right_gate_weight,
    out_weight,
    out_gate_weight,
    dist_weight,
):
    tile_rows, tile_cols, channels = pair_repr.shape
    rows, cols = lax.axis_size("row"), lax.axis_size("col")
    places = rows * cols
    width = 2 * tile_cols
    spots = tile_rows * tile_cols
    size = channels // OWNERS // 2 * tile_rows
    bf16, f32 = jnp.bfloat16, jnp.float32
    struct = jax.ShapeDtypeStruct
    turned = pltpu.VMEM((2 * channels, channels), bf16)
    held = pltpu.VMEM((OWNERS * size, width), f32)
    over_x, over_core, over_z, over_half = 1, cols, 2 * cols, OWNERS * cols
    normed = call(
        norm_kernel, struct((spots, channels), bf16), args=(pair_repr,), flops=1 << 30
    )
    rights = call(
        right_kernel,
        [struct((size, width), bf16)] * OWNERS,
        [turned, held],
        args=(normed, right_weight, right_gate_weight),
        flops=4 * spots * channels * channels,
    )
    over = [d // 2 * over_z + d % 2 * over_x for d in range(OWNERS)]
    far = [exchange(rights[d], places, over_half + over[d]) for d in range(OWNERS)]
    *near, masks = call(
        left_kernel,
        [struct((2 * size, width), bf16)] * OWNERS + [struct((tile_rows, width), f32)],
        [turned, held],
        [SMEM] + [VMEM] * (3 + OWNERS),
        args=(chain_lengths, normed, left_weight, left_gate_weight, *rights),
        flops=4 * spots * channels * channels,
    )
    near = [near[0]] + [exchange(near[d], places, over[d]) for d in range(1, OWNERS)]
    near_over = [exchange(value, places, over_core) for value in (rights[0], *near[1:])]
    far_over = call(pack_kernel, struct((OWNERS * size, width), bf16), args=far)
    far_over = exchange(far_over, places, over_core)
    parts = call(
        tri_kernel,
        [struct((size, width), bf16)] * OWNERS,
        [pltpu.VMEM((cols, size // tile_rows, rows * tile_rows, width), bf16)],
        args=(masks, far_over, *near, *far, *near_over),
        flops=8 * size * 2 * tile_rows * 2 * width,
    )
    parts = [parts[0]] + [exchange(parts[d], places, over[d]) for d in range(1, OWNERS)]
    gate, x_turned, out_turned, dist_turned = call(
        gate_kernel,
        [
            struct((channels, spots), f32),
            struct((channels, spots), f32),
            struct((channels, channels), bf16),
            struct(dist_weight.shape[::-1], bf16),
        ],
        args=(pair_repr, normed, out_gate_weight, out_weight, dist_weight),
        flops=2 * spots * channels * channels,
    )
    pair_out, loss = call(
        finish_kernel,
        [struct((channels, spots), bf16), struct((places, 8, 128), f32)],
        [held],
        args=(
            masks,
            x_turned,
            gate,
            distance_bins.reshape(tile_rows // 2, width),
            out_turned,
            dist_turned,
            *parts,
        ),
        flops=6 * spots * channels * channels,
    )
    pair_out = call(turn_back_kernel, struct(pair_repr.shape, bf16), args=(pair_out,), flops=1 << 26)
    loss = lax.all_to_all(loss, AXES, 0, 0, tiled=True)
    return (pair_out, jnp.sum(loss, axis=0)[0, :1])


def by_all_to_all(
    pair_repr,
    distance_bins,
    chain_lengths,
    left_weight,
    left_gate_weight,
    right_weight,
    right_gate_weight,
    out_weight,
    out_gate_weight,
    dist_weight,
):
    tile_rows, tile_cols, channels = pair_repr.shape
    rows, cols = lax.axis_size("row"), lax.axis_size("col")
    peers = rows * cols
    share = channels // peers
    residues = tile_rows * rows
    spots = tile_rows * tile_cols
    live_count = residues - chain_lengths[chain_lengths.shape[0] - 1]
    row_place = lax.axis_index("row") * tile_rows + jnp.arange(tile_rows, dtype=jnp.int32)
    col_place = lax.axis_index("col") * tile_cols + jnp.arange(tile_cols, dtype=jnp.int32)
    live_rows = (row_place < live_count).astype(jnp.float32)
    live_cols = (col_place < live_count).astype(jnp.float32)
    flat_mask = (live_rows[:, None] * live_cols[None, :]).reshape(-1)
    normed = layer_norm(pair_repr.astype(jnp.float32), -1).astype(jnp.bfloat16)
    normed = normed.reshape(spots, channels)

    def project_turned(weight):
        return lax.dot_general(
            weight, normed, (((0,), (1,)), ((), ())), preferred_element_type=jnp.float32
        )

    def gated(gate_weight, weight):
        values = jax.nn.sigmoid(project_turned(gate_weight)) * project_turned(weight)
        return (values * flat_mask[None, :]).astype(jnp.bfloat16)

    left = gated(left_gate_weight, left_weight).reshape(peers, share, tile_rows, tile_cols)
    right = gated(right_gate_weight, right_weight).reshape(peers, share, tile_rows, tile_cols)
    both = jnp.concatenate([left, right], axis=3).reshape(peers, share * tile_rows, 2 * tile_cols)
    owned = lax.all_to_all(both, AXES, split_axis=0, concat_axis=0, tiled=True)
    owned = owned.reshape(rows, cols, share, tile_rows, 2, tile_cols)
    owned = owned.transpose(4, 2, 0, 3, 1, 5).reshape(2, share, residues, residues)
    tri = jnp.einsum(
        "cik,cjk->cij", owned[0], owned[1], preferred_element_type=jnp.float32
    ).astype(jnp.bfloat16)
    tri = tri.reshape(share, rows, tile_rows, cols, tile_cols).transpose(1, 3, 0, 2, 4)
    tri = tri.reshape(peers, share, spots)
    tri = lax.all_to_all(tri, AXES, split_axis=0, concat_axis=0, tiled=True)
    tri = tri.reshape(channels, spots).astype(jnp.float32)
    tri_normed = layer_norm(tri, 0).astype(jnp.bfloat16)
    out_gate = jax.nn.sigmoid(jnp.dot(normed, out_gate_weight, preferred_element_type=jnp.float32))
    update = out_gate * tn_dot(tri_normed, out_weight)
    pair_out = (pair_repr.astype(jnp.float32).reshape(spots, channels) + update).astype(
        jnp.bfloat16
    )
    logits = jnp.dot(pair_out, dist_weight, preferred_element_type=jnp.float32)
    log_total = jnp.log(jnp.sum(jnp.exp(logits), axis=-1))
    bin_ids = jnp.arange(logits.shape[1], dtype=jnp.int32)
    picked = jnp.sum(
        jnp.where(bin_ids[None, :] == distance_bins.reshape(-1, 1), logits, 0.0), axis=-1
    )
    loss_sum = jnp.sum(flat_mask * (log_total - picked))
    sums = lax.all_to_all(
        jnp.full((peers, 1, 128), loss_sum), AXES, split_axis=0, concat_axis=0, tiled=True
    )
    pair_count = (live_count * live_count).astype(jnp.float32)
    loss_value = (jnp.sum(sums[:, 0, 0]) / pair_count).reshape(1)
    return (pair_out.reshape(pair_repr.shape), loss_value)


def on_device(pair_repr, *others):
    tile_rows, tile_cols, channels = pair_repr.shape
    rows, cols = lax.axis_size("row"), lax.axis_size("col")
    fits = (
        rows == 2 * OWNERS
        and cols == 2
        and tile_rows * rows == tile_cols * cols
        and 2 * tile_cols == 128
        and tile_rows == 16
        and channels % (32 * OWNERS) == 0
    )
    return (by_kernels if fits else by_all_to_all)(pair_repr, *others)


def solution(mesh):
    in_specs = (
        P(("groups", "row"), "col", None),
        P(("groups", "row"), "col"),
        P("groups"),
        P(),
        P(),
        P(),
        P(),
        P(),
        P(),
        P(),
    )
    out_specs = (P(("groups", "row"), "col", None), P("groups"))
    return jax.shard_map(
        on_device, mesh=mesh, in_specs=in_specs, out_specs=out_specs, check_vma=False
    )
```

```python
import functools

import jax
import jax.numpy as jnp
from jax import lax
from jax.experimental import pallas as pl
from jax.experimental.pallas import tpu as pltpu
from jax.sharding import PartitionSpec as P

AXES = ("row", "col")
OWNERS = 4
VMEM = pl.BlockSpec(memory_space=pltpu.VMEM)
SMEM = pl.BlockSpec(memory_space=pltpu.SMEM)
PARAMS = pltpu.CompilerParams(vmem_limit_bytes=24 * 1024 * 1024)


def layer_norm(values, axis):
    average = jnp.mean(values, axis=axis, keepdims=True)
    centred = values - average
    spread = jnp.mean(centred * centred, axis=axis, keepdims=True)
    return centred * lax.rsqrt(spread + 1e-05)


def sigmoid(values):
    return 0.5 * jnp.tanh(0.5 * values) + 0.5


def nt_dot(a, b):
    return lax.dot_general(a, b, (((1,), (1,)), ((), ())), preferred_element_type=jnp.float32)


def tn_dot(a, b):
    return lax.dot_general(a, b, (((0,), (0,)), ((), ())), preferred_element_type=jnp.float32)


def lanes_of(shape):
    return lax.broadcasted_iota(jnp.int32, shape, 1)


def mask_kernel(lens_ref, masks_ref):
    width = masks_ref.shape[1]
    tile_cols = width // 2
    tile_rows = tile_cols * lax.axis_size("col") // lax.axis_size("row")
    live = tile_rows * lax.axis_size("row") - lens_ref[lens_ref.shape[0] - 1]
    lane = lanes_of((1, width))
    upper = (lane >= tile_cols).astype(jnp.int32)
    place = lane - tile_cols * upper
    row, col = lax.axis_index("row"), lax.axis_index("col")
    keeps = [(place + (col ^ dx) * tile_cols < live).astype(jnp.float32) for dx in (0, 1)]
    lines = [
        ((row ^ d) * tile_rows + first + upper < live).astype(jnp.float32) * keeps[0]
        for d in range(OWNERS)
        for first in range(0, tile_rows, 2)
    ]
    lines += keeps
    count = jnp.full(lane.shape, live * live, jnp.int32).astype(jnp.float32)
    lines += [1.0 / count] * (masks_ref.shape[0] - len(lines))
    masks_ref[...] = jnp.concatenate(lines, 0)


def turn(w_refs, turned):
    channels = w_refs[0].shape[0]
    share = channels // OWNERS
    half = share // 2
    for at, w_ref in enumerate(w_refs):
        w = w_ref[...].astype(jnp.float32).T
        blocks = [
            w[o * share + g * half : o * share + (g + 1) * half] for g in (0, 1) for o in range(OWNERS)
        ]
        turned[at * channels : (at + 1) * channels] = jnp.concatenate(blocks, 0).astype(jnp.bfloat16)


def store_rows(held, first, stride, value, tile_cols):
    packed = value.shape[0] // 2
    a, b = value[:packed], value[packed:]
    low = lanes_of(a.shape) < tile_cols
    held[pl.ds(first, packed, stride=stride), :] = jnp.where(low, a, pltpu.roll(b, tile_cols, 1))
    held[pl.ds(first + 1, packed, stride=stride), :] = jnp.where(low, pltpu.roll(a, tile_cols, 1), b)


def owner_place():
    return lax.axis_index("row") % OWNERS


def owner_block(held, d, size):
    at = pl.multiple_of((owner_place() ^ d) * size, size)
    return held[pl.ds(at, size)].astype(jnp.bfloat16)


def norm_kernel(x_ref, normed_ref):
    x = x_ref[...].astype(jnp.float32).reshape(normed_ref.shape)
    normed_ref[...] = layer_norm(x, -1).astype(jnp.bfloat16)


def right_kernel(normed_ref, w_ref, g_ref, stay_ref, move_ref, turned, held):
    channels = normed_ref.shape[1]
    width = held.shape[1]
    turn((w_ref, g_ref), turned)
    for at in range(normed_ref.shape[0] // width):
        flat = nt_dot(turned[...], normed_ref[at * width : (at + 1) * width])
        value = sigmoid(flat[channels:]) * flat[:channels]
        store_rows(held, 2 * at, 2 * held.shape[0] // channels, value, width // 2)
    size = stay_ref.shape[0] // 2
    for d, ref in enumerate((stay_ref, stay_ref, move_ref, move_ref)):
        ref[d % 2 * size : (d % 2 + 1) * size] = owner_block(held, d, size)


def side_kernel(base, masks_ref, a_ref, b_ref, *refs):
    weights, (left_ref, right_ref, turned, mine, held_left, held_right) = refs[:4], refs[4:]
    tile_rows, tile_cols, channels = a_ref.shape
    size = held_left.shape[0]
    half = size // tile_rows
    turn(weights, turned)
    owner = owner_place()
    for at in range(8):
        start = pl.multiple_of(at * (channels // 2) + owner * half, half)
        mine[at * half : (at + 1) * half] = turned[pl.ds(start, half), :]
    for tile, x_ref in enumerate((a_ref, b_ref)):
        for first in range(0, tile_rows, 2):
            x = x_ref[first : first + 2].astype(jnp.float32).reshape(2 * tile_cols, channels)
            flat = nt_dot(mine[...], layer_norm(x, -1).astype(jnp.bfloat16))
            lv, lg, rv, rg = [flat[at * 2 * half : (at + 1) * 2 * half] for at in range(4)]
            line = ((base + tile) * tile_rows + first) // 2
            left = sigmoid(lg) * lv * masks_ref[line : line + 1]
            store_rows(held_left, first, tile_rows, left, tile_cols)
            store_rows(held_right, first, tile_rows, sigmoid(rg) * rv, tile_cols)
        left_ref[tile * size : (tile + 1) * size] = held_left[...].astype(jnp.bfloat16)
        right_ref[tile * size : (tile + 1) * size] = held_right[...].astype(jnp.bfloat16)


def pass_kernel(value_ref, ready_ref, out_ref):
    del ready_ref
    out_ref[...] = value_ref[...]


def pack_kernel(far_ref, cross_ref, ready_ref, out_ref):
    del ready_ref
    size = out_ref.shape[0] // 2
    out_ref[:size] = far_ref[size:]
    out_ref[size:] = cross_ref[size:]


def gate_kernel(x_ref, normed_ref, gw_ref, ow_ref, dw_ref, gate_ref, x_turned_ref, ow_turned, dw_turned):
    tile_rows, tile_cols, channels = x_ref.shape
    share = channels // OWNERS
    half = share // 2
    blocks = [
        ow_ref[o * share + g * half : o * share + (g + 1) * half].astype(jnp.float32)
        for g in (0, 1)
        for o in range(OWNERS)
    ]
    ow_turned[...] = jnp.concatenate(blocks, 0).T.astype(jnp.bfloat16)
    dw_turned[...] = dw_ref[...].astype(jnp.float32).T.astype(jnp.bfloat16)
    gate_turned = gw_ref[...].astype(jnp.float32).T.astype(jnp.bfloat16)
    for first in range(0, tile_rows, 2):
        at = slice(first * tile_cols, (first + 2) * tile_cols)
        gate_ref[:, at] = sigmoid(nt_dot(gate_turned, normed_ref[at]))
        x = x_ref[first : first + 2].astype(jnp.float32).reshape(2 * tile_cols, channels)
        x_turned_ref[:, at] = x.T


def tri_kernel(
    masks_ref, left, right, left_near, right_near, far, cross, both_over, *refs
):
    outs, rights = refs[:-1], refs[-1]
    half, _, width = rights.shape
    size = far.shape[0] // 2
    tile_rows = size // half
    side = OWNERS * tile_rows
    me, col = lax.axis_index("row"), lax.axis_index("col")
    lefts = ((left, 0), (left, size), (left_near, 0), (left_near, size))
    pieces = (
        (0, right, 0),
        (1, right, size),
        (2, right_near, 0),
        (3, right_near, size),
        (4, far, 0),
        (5, both_over, 0),
        (6, cross, 0),
        (7, both_over, size),
    )
    for away, ref, start in pieces:
        at = pl.multiple_of((me ^ away) * tile_rows, tile_rows)
        for m in range(half):
            rights[m, pl.ds(at, tile_rows), :] = ref[
                start + m * tile_rows : start + (m + 1) * tile_rows
            ]
    low = lanes_of((side, width)) < width // 2
    first = OWNERS * tile_rows // 2
    keep = jnp.concatenate([masks_ref[first : first + 1], masks_ref[first + 1 : first + 2]], 1)
    for m in range(half):
        rows = jnp.concatenate(
            [ref[at + m * tile_rows : at + (m + 1) * tile_rows] for ref, at in lefts], 0
        )
        pieces = []
        for dx in (0, 1):
            block = rights[m, pl.ds(pl.multiple_of((col ^ dx) * side, side), side), :]
            block = block.astype(jnp.float32)
            pieces += [jnp.where(low, block, 0.0), jnp.where(low, 0.0, block)]
        columns = jnp.concatenate(pieces, 0).astype(jnp.bfloat16)
        product = (nt_dot(rows, columns) * keep).astype(jnp.bfloat16)
        for d in range(OWNERS):
            for dx in (0, 1):
                at = d % 2 * size + m * tile_rows
                outs[d // 2 * 2 + dx][at : at + tile_rows] = product[
                    d * tile_rows : (d + 1) * tile_rows, dx * width : (dx + 1) * width
                ]


def finish_kernel(masks_ref, x_ref, gate_ref, bins_ref, ow_ref, dw_ref, *refs):
    parts, overs = refs[:OWNERS], refs[OWNERS : 2 * OWNERS]
    out_ref, loss_ref, held = refs[2 * OWNERS :]
    channels = x_ref.shape[0]
    size, width = parts[0].shape[0] // 2, parts[0].shape[1]
    half = channels // 2 // OWNERS
    tile_rows, tile_cols = size // half, width // 2
    packed = OWNERS * half
    owner = owner_place()
    total = jnp.zeros((tile_rows, width), jnp.float32)
    for d in range(OWNERS):
        refs, at = ((parts, 0), (overs, size))[d % 2]
        a, b = [refs[d // 2 * 2 + dx][at : at + size].astype(jnp.float32) for dx in (0, 1)]
        block = a + b
        held[pl.ds(pl.multiple_of((owner ^ d) * size, size), size), :] = block
        total = total + jnp.sum(block.reshape(half, tile_rows, width), 0)
    average = (total + pltpu.roll(total, tile_cols, 1)) * (1.0 / channels)
    total = jnp.zeros((tile_rows, width), jnp.float32)
    for om in range(packed):
        centred = held[om * tile_rows : (om + 1) * tile_rows] - average
        total = total + centred * centred
    spread = (total + pltpu.roll(total, tile_cols, 1)) * (1.0 / channels)
    scale = lax.rsqrt(spread + 1e-05)
    low = lanes_of((packed, width)) < tile_cols
    bin_ids = lax.broadcasted_iota(jnp.int32, (dw_ref.shape[0], width), 0)
    loss = jnp.zeros((1, width), jnp.float32)
    for first in range(0, tile_rows, 2):
        a, b = [
            (held[pl.ds(ii, packed, stride=tile_rows), :] - average[ii : ii + 1]) * scale[ii : ii + 1]
            for ii in (first, first + 1)
        ]
        normed = jnp.concatenate(
            [
                jnp.where(low, a, pltpu.roll(b, tile_cols, 1)),
                jnp.where(low, pltpu.roll(a, tile_cols, 1), b),
            ],
            0,
        ).astype(jnp.bfloat16)
        update = jnp.dot(ow_ref[...], normed, preferred_element_type=jnp.float32)
        at = slice(first * tile_cols, (first + 2) * tile_cols)
        pair_out = (x_ref[:, at] + gate_ref[:, at] * update).astype(jnp.bfloat16)
        out_ref[:, at] = pair_out
        logits = jnp.dot(dw_ref[...], pair_out, preferred_element_type=jnp.float32)
        log_total = jnp.log(jnp.sum(jnp.exp(logits), axis=0, keepdims=True))
        bins = bins_ref[first // 2 : first // 2 + 1]
        picked = jnp.sum(jnp.where(bin_ids == bins, logits, 0.0), axis=0, keepdims=True)
        loss = loss + masks_ref[first // 2 : first // 2 + 1] * (log_total - picked)
    last = masks_ref.shape[0] - 1
    loss = jnp.sum(loss * masks_ref[last : last + 1], axis=1, keepdims=True)
    loss_ref[...] = jnp.broadcast_to(loss[None], loss_ref.shape)


def turn_back_kernel(turned_ref, out_ref):
    tile_rows, tile_cols, channels = out_ref.shape
    for first in range(0, tile_rows, 2):
        block = turned_ref[:, first * tile_cols : (first + 2) * tile_cols].astype(jnp.float32).T
        out_ref[first : first + 2] = block.astype(jnp.bfloat16).reshape(2, tile_cols, channels)


def exchange(value, places, mask):
    return lax.ppermute(value, AXES, [(at, at ^ mask) for at in range(places)])


def call(kernel, outs, scratch=(), specs=None, out_specs=None, args=(), flops=0):
    return pl.pallas_call(
        kernel,
        out_shape=outs,
        in_specs=specs if specs is not None else [VMEM] * len(args),
        out_specs=out_specs if out_specs is not None else jax.tree.map(lambda _: VMEM, outs),
        scratch_shapes=list(scratch),
        compiler_params=PARAMS,
        cost_estimate=pl.CostEstimate(flops=flops, bytes_accessed=1 << 20, transcendentals=1 << 18),
    )(*args)


def by_kernels(
    pair_repr,
    distance_bins,
    chain_lengths,
    left_weight,
    left_gate_weight,
    right_weight,
    right_gate_weight,
    out_weight,
    out_gate_weight,
    dist_weight,
):
    tile_rows, tile_cols, channels = pair_repr.shape
    rows, cols = lax.axis_size("row"), lax.axis_size("col")
    places = rows * cols
    width = 2 * tile_cols
    spots = tile_rows * tile_cols
    size = channels // OWNERS // 2 * tile_rows
    bf16, f32 = jnp.bfloat16, jnp.float32
    struct = jax.ShapeDtypeStruct
    turned = pltpu.VMEM((2 * channels, channels), bf16)
    held = pltpu.VMEM((OWNERS * size, width), f32)
    over_x, over_core, over_z, over_half = 1, cols, 2 * cols, OWNERS * cols
    near = exchange(pair_repr, places, over_z)
    core = exchange(pair_repr, places, over_core)
    normed = call(
        norm_kernel, struct((spots, channels), bf16), args=(pair_repr,), flops=1 << 30
    )
    stay, move = call(
        right_kernel,
        [struct((2 * size, width), bf16)] * 2,
        [turned, held],
        args=(normed, right_weight, right_gate_weight),
        flops=4 * spots * channels * channels,
    )
    cross = exchange(move, places, over_half + over_z)
    far = exchange(stay, places, over_half)
    near_over = call(
        pass_kernel,
        struct(pair_repr.shape, bf16),
        specs=[VMEM, pl.BlockSpec(memory_space=pl.ANY)],
        args=(near, stay),
    )
    near_over = exchange(near_over, places, over_core)
    masks = call(
        mask_kernel,
        struct((OWNERS * tile_rows // 2 + 8, width), f32),
        specs=[SMEM],
        args=(chain_lengths,),
    )
    sides = [
        call(
            functools.partial(side_kernel, base),
            [struct((2 * size, width), bf16)] * 2,
            [
                pltpu.VMEM((4 * channels, channels), bf16),
                pltpu.VMEM((channels, channels), bf16),
                pltpu.VMEM((size, width), f32),
                pltpu.VMEM((size, width), f32),
            ],
            args=(
                masks,
                *tiles,
                left_weight,
                left_gate_weight,
                right_weight,
                right_gate_weight,
            ),
            flops=4 * spots * channels * channels,
        )
        for base, tiles in ((0, (pair_repr, core)), (2, (near, near_over)))
    ]
    both_over = call(
        pack_kernel,
        struct((2 * size, width), bf16),
        specs=[VMEM, VMEM, pl.BlockSpec(memory_space=pl.ANY)],
        args=(far, cross, sides[1][1]),
    )
    both_over = exchange(both_over, places, over_core)
    parts = call(
        tri_kernel,
        [struct((2 * size, width), bf16)] * OWNERS,
        [pltpu.VMEM((size // tile_rows, rows * tile_rows, width), bf16)],
        args=(masks, *sides[0], *sides[1], far, cross, both_over),
        flops=8 * size * 2 * tile_rows * 2 * width,
    )
    parts = [parts[0]] + [
        exchange(parts[d], places, d // 2 * over_z + d % 2 * over_x) for d in range(1, OWNERS)
    ]
    parts += [exchange(value, places, over_core) for value in parts]
    gate, x_turned, out_turned, dist_turned = call(
        gate_kernel,
        [
            struct((channels, spots), f32),
            struct((channels, spots), f32),
            struct((channels, channels), bf16),
            struct(dist_weight.shape[::-1], bf16),
        ],
        args=(pair_repr, normed, out_gate_weight, out_weight, dist_weight),
        flops=2 * spots * channels * channels,
    )
    pair_out, loss = call(
        finish_kernel,
        [struct((channels, spots), bf16), struct((places, 8, 128), f32)],
        [held],
        args=(
            masks,
            x_turned,
            gate,
            distance_bins.reshape(tile_rows // 2, width),
            out_turned,
            dist_turned,
            *parts,
        ),
        flops=6 * spots * channels * channels,
    )
    pair_out = call(turn_back_kernel, struct(pair_repr.shape, bf16), args=(pair_out,), flops=1 << 26)
    loss = lax.all_to_all(loss, AXES, 0, 0, tiled=True)
    return (pair_out, jnp.sum(loss, axis=0)[0, :1])


def by_all_to_all(
    pair_repr,
    distance_bins,
    chain_lengths,
    left_weight,
    left_gate_weight,
    right_weight,
    right_gate_weight,
    out_weight,
    out_gate_weight,
    dist_weight,
):
    tile_rows, tile_cols, channels = pair_repr.shape
    rows, cols = lax.axis_size("row"), lax.axis_size("col")
    peers = rows * cols
    share = channels // peers
    residues = tile_rows * rows
    spots = tile_rows * tile_cols
    live_count = residues - chain_lengths[chain_lengths.shape[0] - 1]
    row_place = lax.axis_index("row") * tile_rows + jnp.arange(tile_rows, dtype=jnp.int32)
    col_place = lax.axis_index("col") * tile_cols + jnp.arange(tile_cols, dtype=jnp.int32)
    live_rows = (row_place < live_count).astype(jnp.float32)
    live_cols = (col_place < live_count).astype(jnp.float32)
    flat_mask = (live_rows[:, None] * live_cols[None, :]).reshape(-1)
    normed = layer_norm(pair_repr.astype(jnp.float32), -1).astype(jnp.bfloat16)
    normed = normed.reshape(spots, channels)

    def project_turned(weight):
        return lax.dot_general(
            weight, normed, (((0,), (1,)), ((), ())), preferred_element_type=jnp.float32
        )

    def gated(gate_weight, weight):
        values = jax.nn.sigmoid(project_turned(gate_weight)) * project_turned(weight)
        return (values * flat_mask[None, :]).astype(jnp.bfloat16)

    left = gated(left_gate_weight, left_weight).reshape(peers, share, tile_rows, tile_cols)
    right = gated(right_gate_weight, right_weight).reshape(peers, share, tile_rows, tile_cols)
    both = jnp.concatenate([left, right], axis=3).reshape(peers, share * tile_rows, 2 * tile_cols)
    owned = lax.all_to_all(both, AXES, split_axis=0, concat_axis=0, tiled=True)
    owned = owned.reshape(rows, cols, share, tile_rows, 2, tile_cols)
    owned = owned.transpose(4, 2, 0, 3, 1, 5).reshape(2, share, residues, residues)
    tri = jnp.einsum(
        "cik,cjk->cij", owned[0], owned[1], preferred_element_type=jnp.float32
    ).astype(jnp.bfloat16)
    tri = tri.reshape(share, rows, tile_rows, cols, tile_cols).transpose(1, 3, 0, 2, 4)
    tri = tri.reshape(peers, share, spots)
    tri = lax.all_to_all(tri, AXES, split_axis=0, concat_axis=0, tiled=True)
    tri = tri.reshape(channels, spots).astype(jnp.float32)
    tri_normed = layer_norm(tri, 0).astype(jnp.bfloat16)
    out_gate = jax.nn.sigmoid(jnp.dot(normed, out_gate_weight, preferred_element_type=jnp.float32))
    update = out_gate * tn_dot(tri_normed, out_weight)
    pair_out = (pair_repr.astype(jnp.float32).reshape(spots, channels) + update).astype(
        jnp.bfloat16
    )
    logits = jnp.dot(pair_out, dist_weight, preferred_element_type=jnp.float32)
    log_total = jnp.log(jnp.sum(jnp.exp(logits), axis=-1))
    bin_ids = jnp.arange(logits.shape[1], dtype=jnp.int32)
    picked = jnp.sum(
        jnp.where(bin_ids[None, :] == distance_bins.reshape(-1, 1), logits, 0.0), axis=-1
    )
    loss_sum = jnp.sum(flat_mask * (log_total - picked))
    sums = lax.all_to_all(
        jnp.full((peers, 1, 128), loss_sum), AXES, split_axis=0, concat_axis=0, tiled=True
    )
    pair_count = (live_count * live_count).astype(jnp.float32)
    loss_value = (jnp.sum(sums[:, 0, 0]) / pair_count).reshape(1)
    return (pair_out.reshape(pair_repr.shape), loss_value)


def on_device(pair_repr, *others):
    tile_rows, tile_cols, channels = pair_repr.shape
    rows, cols = lax.axis_size("row"), lax.axis_size("col")
    fits = (
        rows == 2 * OWNERS
        and cols == 2
        and tile_rows * rows == tile_cols * cols
        and 2 * tile_cols == 128
        and tile_rows == 16
        and channels == 32 * OWNERS
    )
    return (by_kernels if fits else by_all_to_all)(pair_repr, *others)


def solution(mesh):
    in_specs = (
        P(("groups", "row"), "col", None),
        P(("groups", "row"), "col"),
        P("groups"),
        P(),
        P(),
        P(),
        P(),
        P(),
        P(),
        P(),
    )
    out_specs = (P(("groups", "row"), "col", None), P("groups"))
    return jax.shard_map(
        on_device, mesh=mesh, in_specs=in_specs, out_specs=out_specs, check_vma=False
    )
```

```python
import jax
import jax.numpy as jnp
from jax import lax
from jax.experimental import pallas as pl
from jax.experimental.pallas import tpu as pltpu
from jax.sharding import PartitionSpec as P

AXES = ("row", "col")
OWNERS = 4
VMEM = pl.BlockSpec(memory_space=pltpu.VMEM)
SMEM = pl.BlockSpec(memory_space=pltpu.SMEM)
PARAMS = pltpu.CompilerParams(vmem_limit_bytes=24 * 1024 * 1024)


def layer_norm(values, axis):
    average = jnp.mean(values, axis=axis, keepdims=True)
    centred = values - average
    spread = jnp.mean(centred * centred, axis=axis, keepdims=True)
    return centred * lax.rsqrt(spread + 1e-05)


def sigmoid(values):
    return 0.5 * jnp.tanh(0.5 * values) + 0.5


def nt_dot(a, b):
    return lax.dot_general(a, b, (((1,), (1,)), ((), ())), preferred_element_type=jnp.float32)


def tn_dot(a, b):
    return lax.dot_general(a, b, (((0,), (0,)), ((), ())), preferred_element_type=jnp.float32)


def lanes_of(shape):
    return lax.broadcasted_iota(jnp.int32, shape, 1)


def make_masks(lens_ref, tile_rows, tile_cols):
    live = tile_rows * lax.axis_size("row") - lens_ref[lens_ref.shape[0] - 1]
    lane = lanes_of((1, 2 * tile_cols))
    upper = (lane >= tile_cols).astype(jnp.int32)
    place = lane - tile_cols * upper
    row, col = lax.axis_index("row"), lax.axis_index("col")
    keeps = [(place + (col ^ dx) * tile_cols < live).astype(jnp.float32) for dx in (0, 1)]
    pairs = [
        ((row ^ d) * tile_rows + first + upper < live).astype(jnp.float32) * keeps[0]
        for d in (0, OWNERS // 2)
        for first in range(0, tile_rows, 2)
    ]
    count = jnp.full(lane.shape, live * live, jnp.int32).astype(jnp.float32)
    return pairs, keeps, 1.0 / count


def turn(w_refs, turned):
    channels = w_refs[0].shape[0]
    share = channels // OWNERS
    half = share // 2
    for at, w_ref in enumerate(w_refs):
        w = w_ref[...].astype(jnp.float32).T
        blocks = [
            w[o * share + g * half : o * share + (g + 1) * half] for g in (0, 1) for o in range(OWNERS)
        ]
        turned[at * channels : (at + 1) * channels] = jnp.concatenate(blocks, 0).astype(jnp.bfloat16)


def store_rows(held, first, value, tile_cols):
    packed = value.shape[0] // 2
    stride = held.shape[0] // packed
    a, b = value[:packed], value[packed:]
    low = lanes_of(a.shape) < tile_cols
    held[pl.ds(first, packed, stride=stride), :] = jnp.where(low, a, pltpu.roll(b, tile_cols, 1))
    held[pl.ds(first + 1, packed, stride=stride), :] = jnp.where(low, pltpu.roll(a, tile_cols, 1), b)


def chip_rows(turned, mine):
    size = mine.shape[0] // (turned.shape[0] // mine.shape[1]) // 2
    pair = owner_place() // 2
    for at in range(mine.shape[0] // size):
        start = pl.multiple_of(at * (mine.shape[1] // 2) + pair * size, size)
        mine[at * size : (at + 1) * size] = turned[pl.ds(start, size), :]


def owner_place():
    return lax.axis_index("row") % OWNERS


def owner_block(held, d, size):
    at = pl.multiple_of((owner_place() ^ d) * size, size)
    return held[pl.ds(at, size)].astype(jnp.bfloat16)


def core_block(held, d, size):
    at = pl.multiple_of((owner_place() % 2 ^ d) * size, size)
    return held[pl.ds(at, size)].astype(jnp.bfloat16)


def norm_kernel(x_ref, normed_ref):
    x = x_ref[...].astype(jnp.float32).reshape(normed_ref.shape)
    normed_ref[...] = layer_norm(x, -1).astype(jnp.bfloat16)


def right_kernel(normed_ref, w_ref, g_ref, stay_ref, move_ref, turned, held):
    channels = normed_ref.shape[1]
    width = held.shape[1]
    turn((w_ref, g_ref), turned)
    for at in range(normed_ref.shape[0] // width):
        flat = nt_dot(turned[...], normed_ref[at * width : (at + 1) * width])
        store_rows(held, 2 * at, sigmoid(flat[channels:]) * flat[:channels], width // 2)
    size = stay_ref.shape[0] // 2
    for d, ref in enumerate((stay_ref, stay_ref, move_ref, move_ref)):
        ref[d % 2 * size : (d % 2 + 1) * size] = owner_block(held, d, size)


def left_kernel(lens_ref, normed_ref, w_ref, g_ref, stay_ref, own_ref, core_ref, masks_ref, *refs):
    turned, mine, held = refs
    width = held.shape[1]
    half = mine.shape[0] // 2
    pairs, keeps, share = make_masks(lens_ref, 2 * normed_ref.shape[0] // width, width // 2)
    masks_ref[...] = jnp.concatenate(
        pairs + keeps + [share] * (masks_ref.shape[0] - len(pairs) - len(keeps)), 0
    )
    turn((w_ref, g_ref), turned)
    chip_rows(turned, mine)
    for at in range(normed_ref.shape[0] // width):
        flat = nt_dot(mine[...], normed_ref[at * width : (at + 1) * width])
        store_rows(held, 2 * at, sigmoid(flat[half:]) * flat[:half] * pairs[at], width // 2)
    size = stay_ref.shape[0] // 2
    for d, ref in enumerate((own_ref, core_ref)):
        ref[:size] = core_block(held, d, size)
        ref[size:] = stay_ref[d * size : (d + 1) * size]


def near_kernel(masks_ref, x_ref, lw_ref, lg_ref, rw_ref, rg_ref, near_ref, over_ref, *refs):
    turned, mine, held_left, held_right = refs
    tile_rows, tile_cols, channels = x_ref.shape
    share = mine.shape[0] // 4
    turn((lw_ref, lg_ref, rw_ref, rg_ref), turned)
    chip_rows(turned, mine)
    for first in range(0, tile_rows, 2):
        x = x_ref[first : first + 2].astype(jnp.float32).reshape(2 * tile_cols, channels)
        flat = nt_dot(mine[...], layer_norm(x, -1).astype(jnp.bfloat16))
        lv, lg, rv, rg = [flat[at * share : (at + 1) * share] for at in range(4)]
        line = (tile_rows + first) // 2
        store_rows(held_left, first, sigmoid(lg) * lv * masks_ref[line : line + 1], tile_cols)
        store_rows(held_right, first, sigmoid(rg) * rv, tile_cols)
    size = near_ref.shape[0] // 2
    for d, ref in enumerate((near_ref, over_ref)):
        ref[:size] = core_block(held_left, d, size)
        ref[size:] = core_block(held_right, d, size)


def pack_kernel(far_ref, cross_ref, ready_ref, out_ref):
    del ready_ref
    size = out_ref.shape[0] // 2
    out_ref[:size] = far_ref[size:]
    out_ref[size:] = cross_ref[size:]


def gate_kernel(x_ref, normed_ref, gw_ref, ow_ref, dw_ref, gate_ref, x_turned_ref, ow_turned, dw_turned):
    tile_rows, tile_cols, channels = x_ref.shape
    share = channels // OWNERS
    half = share // 2
    blocks = [
        ow_ref[o * share + g * half : o * share + (g + 1) * half].astype(jnp.float32)
        for g in (0, 1)
        for o in range(OWNERS)
    ]
    ow_turned[...] = jnp.concatenate(blocks, 0).T.astype(jnp.bfloat16)
    dw_turned[...] = dw_ref[...].astype(jnp.float32).T.astype(jnp.bfloat16)
    gate_turned = gw_ref[...].astype(jnp.float32).T.astype(jnp.bfloat16)
    for first in range(0, tile_rows, 2):
        at = slice(first * tile_cols, (first + 2) * tile_cols)
        gate_ref[:, at] = sigmoid(nt_dot(gate_turned, normed_ref[at]))
        x = x_ref[first : first + 2].astype(jnp.float32).reshape(2 * tile_cols, channels)
        x_turned_ref[:, at] = x.T


def tri_kernel(masks_ref, own, core, near, near_over, far, cross, both_over, *refs):
    outs, rights = refs[:-1], refs[-1]
    half, _, width = rights.shape
    size = own.shape[0] // 2
    tile_rows = size // half
    side = OWNERS * tile_rows
    me, col = lax.axis_index("row"), lax.axis_index("col")
    lefts = (own, core, near, near_over)
    pieces = (
        (0, own, size),
        (1, core, size),
        (2, near, size),
        (3, near_over, size),
        (4, far, 0),
        (5, both_over, 0),
        (6, cross, 0),
        (7, both_over, size),
    )
    for away, ref, start in pieces:
        at = pl.multiple_of((me ^ away) * tile_rows, tile_rows)
        for m in range(half):
            rights[m, pl.ds(at, tile_rows), :] = ref[
                start + m * tile_rows : start + (m + 1) * tile_rows
            ]
    low = lanes_of((side, width)) < width // 2
    first = masks_ref.shape[0] - tile_rows // 2
    keep = jnp.concatenate([masks_ref[first : first + 1], masks_ref[first + 1 : first + 2]], 1)
    for m in range(half):
        left = jnp.concatenate(
            [ref[m * tile_rows : (m + 1) * tile_rows] for ref in lefts], 0
        )
        pieces = []
        for dx in (0, 1):
            block = rights[m, pl.ds(pl.multiple_of((col ^ dx) * side, side), side), :]
            block = block.astype(jnp.float32)
            pieces += [jnp.where(low, block, 0.0), jnp.where(low, 0.0, block)]
        right = jnp.concatenate(pieces, 0).astype(jnp.bfloat16)
        product = (nt_dot(left, right) * keep).astype(jnp.bfloat16)
        for d in range(OWNERS):
            for dx in (0, 1):
                at = d % 2 * size + m * tile_rows
                outs[d // 2 * 2 + dx][at : at + tile_rows] = product[
                    d * tile_rows : (d + 1) * tile_rows, dx * width : (dx + 1) * width
                ]


def finish_kernel(masks_ref, x_ref, gate_ref, bins_ref, ow_ref, dw_ref, *refs):
    parts, overs = refs[:OWNERS], refs[OWNERS : 2 * OWNERS]
    out_ref, loss_ref, held = refs[2 * OWNERS :]
    channels = x_ref.shape[0]
    size, width = parts[0].shape[0] // 2, parts[0].shape[1]
    half = channels // 2 // OWNERS
    tile_rows, tile_cols = size // half, width // 2
    packed = OWNERS * half
    owner = owner_place()
    total = jnp.zeros((tile_rows, width), jnp.float32)
    for d in range(OWNERS):
        refs, at = ((parts, 0), (overs, size))[d % 2]
        a, b = [refs[d // 2 * 2 + dx][at : at + size].astype(jnp.float32) for dx in (0, 1)]
        block = a + b
        held[pl.ds(pl.multiple_of((owner ^ d) * size, size), size), :] = block
        total = total + jnp.sum(block.reshape(half, tile_rows, width), 0)
    average = (total + pltpu.roll(total, tile_cols, 1)) * (1.0 / channels)
    total = jnp.zeros((tile_rows, width), jnp.float32)
    for om in range(packed):
        centred = held[om * tile_rows : (om + 1) * tile_rows] - average
        total = total + centred * centred
    spread = (total + pltpu.roll(total, tile_cols, 1)) * (1.0 / channels)
    scale = lax.rsqrt(spread + 1e-05)
    low = lanes_of((packed, width)) < tile_cols
    bin_ids = lax.broadcasted_iota(jnp.int32, (dw_ref.shape[0], width), 0)
    loss = jnp.zeros((1, width), jnp.float32)
    for first in range(0, tile_rows, 2):
        a, b = [
            (held[pl.ds(ii, packed, stride=tile_rows), :] - average[ii : ii + 1]) * scale[ii : ii + 1]
            for ii in (first, first + 1)
        ]
        normed = jnp.concatenate(
            [
                jnp.where(low, a, pltpu.roll(b, tile_cols, 1)),
                jnp.where(low, pltpu.roll(a, tile_cols, 1), b),
            ],
            0,
        ).astype(jnp.bfloat16)
        update = jnp.dot(ow_ref[...], normed, preferred_element_type=jnp.float32)
        at = slice(first * tile_cols, (first + 2) * tile_cols)
        pair_out = (x_ref[:, at] + gate_ref[:, at] * update).astype(jnp.bfloat16)
        out_ref[:, at] = pair_out
        logits = jnp.dot(dw_ref[...], pair_out, preferred_element_type=jnp.float32)
        log_total = jnp.log(jnp.sum(jnp.exp(logits), axis=0, keepdims=True))
        bins = bins_ref[first // 2 : first // 2 + 1]
        picked = jnp.sum(jnp.where(bin_ids == bins, logits, 0.0), axis=0, keepdims=True)
        loss = loss + masks_ref[first // 2 : first // 2 + 1] * (log_total - picked)
    last = masks_ref.shape[0] - 1
    loss = jnp.sum(loss * masks_ref[last : last + 1], axis=1, keepdims=True)
    loss_ref[...] = jnp.broadcast_to(loss[None], loss_ref.shape)


def turn_back_kernel(turned_ref, out_ref):
    tile_rows, tile_cols, channels = out_ref.shape
    for first in range(0, tile_rows, 2):
        block = turned_ref[:, first * tile_cols : (first + 2) * tile_cols].astype(jnp.float32).T
        out_ref[first : first + 2] = block.astype(jnp.bfloat16).reshape(2, tile_cols, channels)


def exchange(value, places, mask):
    return lax.ppermute(value, AXES, [(at, at ^ mask) for at in range(places)])


def call(kernel, outs, scratch=(), specs=None, out_specs=None, args=(), flops=0):
    return pl.pallas_call(
        kernel,
        out_shape=outs,
        in_specs=specs if specs is not None else [VMEM] * len(args),
        out_specs=out_specs if out_specs is not None else jax.tree.map(lambda _: VMEM, outs),
        scratch_shapes=list(scratch),
        compiler_params=PARAMS,
        cost_estimate=pl.CostEstimate(flops=flops, bytes_accessed=1 << 20, transcendentals=1 << 18),
    )(*args)


def by_kernels(
    pair_repr,
    distance_bins,
    chain_lengths,
    left_weight,
    left_gate_weight,
    right_weight,
    right_gate_weight,
    out_weight,
    out_gate_weight,
    dist_weight,
):
    tile_rows, tile_cols, channels = pair_repr.shape
    rows, cols = lax.axis_size("row"), lax.axis_size("col")
    places = rows * cols
    width = 2 * tile_cols
    spots = tile_rows * tile_cols
    size = channels // OWNERS // 2 * tile_rows
    bf16, f32 = jnp.bfloat16, jnp.float32
    struct = jax.ShapeDtypeStruct
    turned = pltpu.VMEM((2 * channels, channels), bf16)
    held = pltpu.VMEM((OWNERS * size, width), f32)
    over_x, over_core, over_z, over_half = 1, cols, 2 * cols, OWNERS * cols
    near = exchange(pair_repr, places, over_z)
    normed = call(
        norm_kernel, struct((spots, channels), bf16), args=(pair_repr,), flops=1 << 30
    )
    stay, move = call(
        right_kernel,
        [struct((2 * size, width), bf16)] * 2,
        [turned, held],
        args=(normed, right_weight, right_gate_weight),
        flops=4 * spots * channels * channels,
    )
    cross = exchange(move, places, over_half + over_z)
    far = exchange(stay, places, over_half)
    block = struct((2 * size, width), bf16)
    own, core, masks = call(
        left_kernel,
        [block, block, struct((3 * tile_rows // 2, width), f32)],
        [turned, pltpu.VMEM((channels, channels), bf16), pltpu.VMEM((2 * size, width), f32)],
        [SMEM] + [VMEM] * 4,
        args=(chain_lengths, normed, left_weight, left_gate_weight, stay),
        flops=2 * spots * channels * channels,
    )
    near, near_over = call(
        near_kernel,
        [block, block],
        [
            pltpu.VMEM((4 * channels, channels), bf16),
            pltpu.VMEM((2 * channels, channels), bf16),
            pltpu.VMEM((2 * size, width), f32),
            pltpu.VMEM((2 * size, width), f32),
        ],
        args=(masks, near, left_weight, left_gate_weight, right_weight, right_gate_weight),
        flops=4 * spots * channels * channels,
    )
    near_over = exchange(near_over, places, over_core)
    core = exchange(core, places, over_core)
    both_over = call(
        pack_kernel,
        block,
        specs=[VMEM, VMEM, pl.BlockSpec(memory_space=pl.ANY)],
        args=(far, cross, near_over),
    )
    both_over = exchange(both_over, places, over_core)
    parts = call(
        tri_kernel,
        [struct((2 * size, width), bf16)] * OWNERS,
        [pltpu.VMEM((size // tile_rows, rows * tile_rows, width), bf16)],
        args=(masks, own, core, near, near_over, far, cross, both_over),
        flops=8 * size * 2 * tile_rows * 2 * width,
    )
    parts = [parts[0]] + [
        exchange(parts[d], places, d // 2 * over_z + d % 2 * over_x) for d in range(1, OWNERS)
    ]
    parts += [exchange(value, places, over_core) for value in parts]
    gate, x_turned, out_turned, dist_turned = call(
        gate_kernel,
        [
            struct((channels, spots), f32),
            struct((channels, spots), f32),
            struct((channels, channels), bf16),
            struct(dist_weight.shape[::-1], bf16),
        ],
        args=(pair_repr, normed, out_gate_weight, out_weight, dist_weight),
        flops=2 * spots * channels * channels,
    )
    pair_out, loss = call(
        finish_kernel,
        [struct((channels, spots), bf16), struct((places, 8, 128), f32)],
        [held],
        args=(
            masks,
            x_turned,
            gate,
            distance_bins.reshape(tile_rows // 2, width),
            out_turned,
            dist_turned,
            *parts,
        ),
        flops=6 * spots * channels * channels,
    )
    pair_out = call(turn_back_kernel, struct(pair_repr.shape, bf16), args=(pair_out,), flops=1 << 26)
    loss = lax.all_to_all(loss, AXES, 0, 0, tiled=True)
    return (pair_out, jnp.sum(loss, axis=0)[0, :1])


def by_all_to_all(
    pair_repr,
    distance_bins,
    chain_lengths,
    left_weight,
    left_gate_weight,
    right_weight,
    right_gate_weight,
    out_weight,
    out_gate_weight,
    dist_weight,
):
    tile_rows, tile_cols, channels = pair_repr.shape
    rows, cols = lax.axis_size("row"), lax.axis_size("col")
    peers = rows * cols
    share = channels // peers
    residues = tile_rows * rows
    spots = tile_rows * tile_cols
    live_count = residues - chain_lengths[chain_lengths.shape[0] - 1]
    row_place = lax.axis_index("row") * tile_rows + jnp.arange(tile_rows, dtype=jnp.int32)
    col_place = lax.axis_index("col") * tile_cols + jnp.arange(tile_cols, dtype=jnp.int32)
    live_rows = (row_place < live_count).astype(jnp.float32)
    live_cols = (col_place < live_count).astype(jnp.float32)
    flat_mask = (live_rows[:, None] * live_cols[None, :]).reshape(-1)
    normed = layer_norm(pair_repr.astype(jnp.float32), -1).astype(jnp.bfloat16)
    normed = normed.reshape(spots, channels)

    def project_turned(weight):
        return lax.dot_general(
            weight, normed, (((0,), (1,)), ((), ())), preferred_element_type=jnp.float32
        )

    def gated(gate_weight, weight):
        values = jax.nn.sigmoid(project_turned(gate_weight)) * project_turned(weight)
        return (values * flat_mask[None, :]).astype(jnp.bfloat16)

    left = gated(left_gate_weight, left_weight).reshape(peers, share, tile_rows, tile_cols)
    right = gated(right_gate_weight, right_weight).reshape(peers, share, tile_rows, tile_cols)
    both = jnp.concatenate([left, right], axis=3).reshape(peers, share * tile_rows, 2 * tile_cols)
    owned = lax.all_to_all(both, AXES, split_axis=0, concat_axis=0, tiled=True)
    owned = owned.reshape(rows, cols, share, tile_rows, 2, tile_cols)
    owned = owned.transpose(4, 2, 0, 3, 1, 5).reshape(2, share, residues, residues)
    tri = jnp.einsum(
        "cik,cjk->cij", owned[0], owned[1], preferred_element_type=jnp.float32
    ).astype(jnp.bfloat16)
    tri = tri.reshape(share, rows, tile_rows, cols, tile_cols).transpose(1, 3, 0, 2, 4)
    tri = tri.reshape(peers, share, spots)
    tri = lax.all_to_all(tri, AXES, split_axis=0, concat_axis=0, tiled=True)
    tri = tri.reshape(channels, spots).astype(jnp.float32)
    tri_normed = layer_norm(tri, 0).astype(jnp.bfloat16)
    out_gate = jax.nn.sigmoid(jnp.dot(normed, out_gate_weight, preferred_element_type=jnp.float32))
    update = out_gate * tn_dot(tri_normed, out_weight)
    pair_out = (pair_repr.astype(jnp.float32).reshape(spots, channels) + update).astype(
        jnp.bfloat16
    )
    logits = jnp.dot(pair_out, dist_weight, preferred_element_type=jnp.float32)
    log_total = jnp.log(jnp.sum(jnp.exp(logits), axis=-1))
    bin_ids = jnp.arange(logits.shape[1], dtype=jnp.int32)
    picked = jnp.sum(
        jnp.where(bin_ids[None, :] == distance_bins.reshape(-1, 1), logits, 0.0), axis=-1
    )
    loss_sum = jnp.sum(flat_mask * (log_total - picked))
    sums = lax.all_to_all(
        jnp.full((peers, 1, 128), loss_sum), AXES, split_axis=0, concat_axis=0, tiled=True
    )
    pair_count = (live_count * live_count).astype(jnp.float32)
    loss_value = (jnp.sum(sums[:, 0, 0]) / pair_count).reshape(1)
    return (pair_out.reshape(pair_repr.shape), loss_value)


def on_device(pair_repr, *others):
    tile_rows, tile_cols, channels = pair_repr.shape
    rows, cols = lax.axis_size("row"), lax.axis_size("col")
    fits = (
        rows == 2 * OWNERS
        and cols == 2
        and tile_rows * rows == tile_cols * cols
        and 2 * tile_cols == 128
        and tile_rows == 16
        and channels == 32 * OWNERS
    )
    return (by_kernels if fits else by_all_to_all)(pair_repr, *others)


def solution(mesh):
    in_specs = (
        P(("groups", "row"), "col", None),
        P(("groups", "row"), "col"),
        P("groups"),
        P(),
        P(),
        P(),
        P(),
        P(),
        P(),
        P(),
    )
    out_specs = (P(("groups", "row"), "col", None), P("groups"))
    return jax.shard_map(
        on_device, mesh=mesh, in_specs=in_specs, out_specs=out_specs, check_vma=False
    )
```

```python
import jax
import jax.numpy as jnp
from jax import lax
from jax.experimental import pallas as pl
from jax.experimental.pallas import tpu as pltpu
from jax.sharding import PartitionSpec as P

AXES = ("row", "col")
OWNERS = 4
DIAGONAL_FIRST = (3, 1, 2, 0)
VMEM = pl.BlockSpec(memory_space=pltpu.VMEM)
SMEM = pl.BlockSpec(memory_space=pltpu.SMEM)
PARAMS = pltpu.CompilerParams(vmem_limit_bytes=24 * 1024 * 1024)


def layer_norm(values, axis):
    average = jnp.mean(values, axis=axis, keepdims=True)
    centred = values - average
    spread = jnp.mean(centred * centred, axis=axis, keepdims=True)
    return centred * lax.rsqrt(spread + 1e-05)


def sigmoid(values):
    return 0.5 * jnp.tanh(0.5 * values) + 0.5


def nt_dot(a, b):
    return lax.dot_general(a, b, (((1,), (1,)), ((), ())), preferred_element_type=jnp.float32)


def tn_dot(a, b):
    return lax.dot_general(a, b, (((0,), (0,)), ((), ())), preferred_element_type=jnp.float32)


def lanes_of(shape):
    return lax.broadcasted_iota(jnp.int32, shape, 1)


def make_masks(lens_ref, tile_rows, tile_cols):
    live = tile_rows * lax.axis_size("row") - lens_ref[lens_ref.shape[0] - 1]
    lane = lanes_of((1, 2 * tile_cols))
    upper = (lane >= tile_cols).astype(jnp.int32)
    place = lane - tile_cols * upper
    row, col = lax.axis_index("row"), lax.axis_index("col")
    keeps = [(place + (col ^ dx) * tile_cols < live).astype(jnp.float32) for dx in (0, 1)]
    pairs = [
        ((row ^ d) * tile_rows + first + upper < live).astype(jnp.float32) * keeps[0]
        for d in (0, OWNERS // 2)
        for first in range(0, tile_rows, 2)
    ]
    count = jnp.full(lane.shape, live * live, jnp.int32).astype(jnp.float32)
    return pairs, keeps, 1.0 / count


def turn(w_refs, turned):
    channels = w_refs[0].shape[0]
    share = channels // OWNERS
    half = share // 2
    for at, w_ref in enumerate(w_refs):
        w = w_ref[...].astype(jnp.float32).T
        blocks = [
            w[o * share + g * half : o * share + (g + 1) * half] for g in (0, 1) for o in range(OWNERS)
        ]
        turned[at * channels : (at + 1) * channels] = jnp.concatenate(blocks, 0).astype(jnp.bfloat16)


def store_rows(held, first, value, tile_cols):
    packed = value.shape[0] // 2
    stride = held.shape[0] // packed
    a, b = value[:packed], value[packed:]
    low = lanes_of(a.shape) < tile_cols
    held[pl.ds(first, packed, stride=stride), :] = jnp.where(low, a, pltpu.roll(b, tile_cols, 1))
    held[pl.ds(first + 1, packed, stride=stride), :] = jnp.where(low, pltpu.roll(a, tile_cols, 1), b)


def chip_rows(turned, mine):
    size = mine.shape[0] // (turned.shape[0] // mine.shape[1]) // 2
    pair = owner_place() // 2
    for at in range(mine.shape[0] // size):
        start = pl.multiple_of(at * (mine.shape[1] // 2) + pair * size, size)
        mine[at * size : (at + 1) * size] = turned[pl.ds(start, size), :]


def owner_place():
    return lax.axis_index("row") % OWNERS


def owner_block(held, d, size):
    at = pl.multiple_of((owner_place() ^ d) * size, size)
    return held[pl.ds(at, size)].astype(jnp.bfloat16)


def core_block(held, d, size):
    at = pl.multiple_of((owner_place() % 2 ^ d) * size, size)
    return held[pl.ds(at, size)].astype(jnp.bfloat16)


def norm_kernel(x_ref, normed_ref):
    x = x_ref[...].astype(jnp.float32).reshape(normed_ref.shape)
    normed_ref[...] = layer_norm(x, -1).astype(jnp.bfloat16)


def right_kernel(normed_ref, w_ref, g_ref, stay_ref, move_ref, turned, held):
    channels = normed_ref.shape[1]
    width = held.shape[1]
    turn((w_ref, g_ref), turned)
    for at in range(normed_ref.shape[0] // width):
        flat = nt_dot(turned[...], normed_ref[at * width : (at + 1) * width])
        store_rows(held, 2 * at, sigmoid(flat[channels:]) * flat[:channels], width // 2)
    size = stay_ref.shape[0] // 2
    for d, ref in enumerate((stay_ref, stay_ref, move_ref, move_ref)):
        ref[d % 2 * size : (d % 2 + 1) * size] = owner_block(held, d, size)


def left_kernel(lens_ref, normed_ref, w_ref, g_ref, stay_ref, own_ref, core_ref, masks_ref, *refs):
    turned, mine, held = refs
    width = held.shape[1]
    half = mine.shape[0] // 2
    pairs, keeps, share = make_masks(lens_ref, 2 * normed_ref.shape[0] // width, width // 2)
    masks_ref[...] = jnp.concatenate(
        pairs + keeps + [share] * (masks_ref.shape[0] - len(pairs) - len(keeps)), 0
    )
    turn((w_ref, g_ref), turned)
    chip_rows(turned, mine)
    for at in range(normed_ref.shape[0] // width):
        flat = nt_dot(mine[...], normed_ref[at * width : (at + 1) * width])
        store_rows(held, 2 * at, sigmoid(flat[half:]) * flat[:half] * pairs[at], width // 2)
    size = stay_ref.shape[0] // 2
    for d, ref in enumerate((own_ref, core_ref)):
        ref[:size] = core_block(held, d, size)
        ref[size:] = stay_ref[d * size : (d + 1) * size]


def near_kernel(masks_ref, x_ref, lw_ref, lg_ref, rw_ref, rg_ref, near_ref, over_ref, *refs):
    turned, mine, held_left, held_right = refs
    tile_rows, tile_cols, channels = x_ref.shape
    share = mine.shape[0] // 4
    turn((lw_ref, lg_ref, rw_ref, rg_ref), turned)
    chip_rows(turned, mine)
    for first in range(0, tile_rows, 2):
        x = x_ref[first : first + 2].astype(jnp.float32).reshape(2 * tile_cols, channels)
        flat = nt_dot(mine[...], layer_norm(x, -1).astype(jnp.bfloat16))
        lv, lg, rv, rg = [flat[at * share : (at + 1) * share] for at in range(4)]
        line = (tile_rows + first) // 2
        store_rows(held_left, first, sigmoid(lg) * lv * masks_ref[line : line + 1], tile_cols)
        store_rows(held_right, first, sigmoid(rg) * rv, tile_cols)
    size = near_ref.shape[0] // 2
    for d, ref in enumerate((near_ref, over_ref)):
        ref[:size] = core_block(held_left, d, size)
        ref[size:] = core_block(held_right, d, size)


def pack_kernel(far_ref, cross_ref, ready_ref, out_ref):
    del ready_ref
    size = out_ref.shape[0] // 2
    out_ref[:size] = far_ref[size:]
    out_ref[size:] = cross_ref[size:]


def gate_kernel(x_ref, normed_ref, gw_ref, ow_ref, dw_ref, gate_ref, x_turned_ref, ow_turned, dw_turned):
    tile_rows, tile_cols, channels = x_ref.shape
    share = channels // OWNERS
    half = share // 2
    blocks = [
        ow_ref[o * share + g * half : o * share + (g + 1) * half].astype(jnp.float32)
        for g in (0, 1)
        for o in range(OWNERS)
    ]
    ow_turned[...] = jnp.concatenate(blocks, 0).T.astype(jnp.bfloat16)
    dw_turned[...] = dw_ref[...].astype(jnp.float32).T.astype(jnp.bfloat16)
    gate_turned = gw_ref[...].astype(jnp.float32).T.astype(jnp.bfloat16)
    for first in range(0, tile_rows, 2):
        at = slice(first * tile_cols, (first + 2) * tile_cols)
        gate_ref[:, at] = sigmoid(nt_dot(gate_turned, normed_ref[at]))
        x = x_ref[first : first + 2].astype(jnp.float32).reshape(2 * tile_cols, channels)
        x_turned_ref[:, at] = x.T


def tri_kernel(masks_ref, own, core, near, near_over, far, cross, both_over, *refs):
    outs, rights = refs[:-1], refs[-1]
    half, _, width = rights.shape
    size = own.shape[0] // 2
    tile_rows = size // half
    side = OWNERS * tile_rows
    me, col = lax.axis_index("row"), lax.axis_index("col")
    lefts = (own, core, near, near_over)
    pieces = (
        (0, own, size),
        (1, core, size),
        (2, near, size),
        (3, near_over, size),
        (4, far, 0),
        (5, both_over, 0),
        (6, cross, 0),
        (7, both_over, size),
    )
    for away, ref, start in pieces:
        at = pl.multiple_of((me ^ away) * tile_rows, tile_rows)
        for m in range(half):
            rights[m, pl.ds(at, tile_rows), :] = ref[
                start + m * tile_rows : start + (m + 1) * tile_rows
            ]
    low = lanes_of((side, width)) < width // 2
    first = masks_ref.shape[0] - tile_rows // 2
    keep = jnp.concatenate([masks_ref[first : first + 1], masks_ref[first + 1 : first + 2]], 1)
    for m in range(half):
        left = jnp.concatenate(
            [ref[m * tile_rows : (m + 1) * tile_rows] for ref in lefts], 0
        )
        pieces = []
        for dx in (0, 1):
            block = rights[m, pl.ds(pl.multiple_of((col ^ dx) * side, side), side), :]
            block = block.astype(jnp.float32)
            pieces += [jnp.where(low, block, 0.0), jnp.where(low, 0.0, block)]
        right = jnp.concatenate(pieces, 0).astype(jnp.bfloat16)
        product = (nt_dot(left, right) * keep).astype(jnp.bfloat16)
        for d in range(OWNERS):
            for dx in (0, 1):
                at = d % 2 * size + m * tile_rows
                outs[d // 2 * 2 + dx][at : at + tile_rows] = product[
                    d * tile_rows : (d + 1) * tile_rows, dx * width : (dx + 1) * width
                ]


def finish_kernel(masks_ref, x_ref, gate_ref, bins_ref, ow_ref, dw_ref, *refs):
    parts, overs = [
        [refs[first + DIAGONAL_FIRST.index(d)] for d in range(OWNERS)] for first in (0, OWNERS)
    ]
    out_ref, loss_ref, held = refs[2 * OWNERS :]
    channels = x_ref.shape[0]
    size, width = parts[0].shape[0] // 2, parts[0].shape[1]
    half = channels // 2 // OWNERS
    tile_rows, tile_cols = size // half, width // 2
    packed = OWNERS * half
    owner = owner_place()
    total = jnp.zeros((tile_rows, width), jnp.float32)
    for d in range(OWNERS):
        refs, at = ((parts, 0), (overs, size))[d % 2]
        a, b = [refs[d // 2 * 2 + dx][at : at + size].astype(jnp.float32) for dx in (0, 1)]
        block = a + b
        held[pl.ds(pl.multiple_of((owner ^ d) * size, size), size), :] = block
        total = total + jnp.sum(block.reshape(half, tile_rows, width), 0)
    average = (total + pltpu.roll(total, tile_cols, 1)) * (1.0 / channels)
    total = jnp.zeros((tile_rows, width), jnp.float32)
    for om in range(packed):
        centred = held[om * tile_rows : (om + 1) * tile_rows] - average
        total = total + centred * centred
    spread = (total + pltpu.roll(total, tile_cols, 1)) * (1.0 / channels)
    scale = lax.rsqrt(spread + 1e-05)
    low = lanes_of((packed, width)) < tile_cols
    bin_ids = lax.broadcasted_iota(jnp.int32, (dw_ref.shape[0], width), 0)
    loss = jnp.zeros((1, width), jnp.float32)
    for first in range(0, tile_rows, 2):
        a, b = [
            (held[pl.ds(ii, packed, stride=tile_rows), :] - average[ii : ii + 1]) * scale[ii : ii + 1]
            for ii in (first, first + 1)
        ]
        normed = jnp.concatenate(
            [
                jnp.where(low, a, pltpu.roll(b, tile_cols, 1)),
                jnp.where(low, pltpu.roll(a, tile_cols, 1), b),
            ],
            0,
        ).astype(jnp.bfloat16)
        update = jnp.dot(ow_ref[...], normed, preferred_element_type=jnp.float32)
        at = slice(first * tile_cols, (first + 2) * tile_cols)
        pair_out = (x_ref[:, at] + gate_ref[:, at] * update).astype(jnp.bfloat16)
        out_ref[:, at] = pair_out
        logits = jnp.dot(dw_ref[...], pair_out, preferred_element_type=jnp.float32)
        log_total = jnp.log(jnp.sum(jnp.exp(logits), axis=0, keepdims=True))
        bins = bins_ref[first // 2 : first // 2 + 1]
        picked = jnp.sum(jnp.where(bin_ids == bins, logits, 0.0), axis=0, keepdims=True)
        loss = loss + masks_ref[first // 2 : first // 2 + 1] * (log_total - picked)
    last = masks_ref.shape[0] - 1
    loss = jnp.sum(loss * masks_ref[last : last + 1], axis=1, keepdims=True)
    loss_ref[...] = jnp.broadcast_to(loss[None], loss_ref.shape)


def turn_back_kernel(turned_ref, out_ref):
    tile_rows, tile_cols, channels = out_ref.shape
    for first in range(0, tile_rows, 2):
        block = turned_ref[:, first * tile_cols : (first + 2) * tile_cols].astype(jnp.float32).T
        out_ref[first : first + 2] = block.astype(jnp.bfloat16).reshape(2, tile_cols, channels)


def exchange(value, places, mask):
    return lax.ppermute(value, AXES, [(at, at ^ mask) for at in range(places)])


def call(kernel, outs, scratch=(), specs=None, out_specs=None, args=(), flops=0):
    return pl.pallas_call(
        kernel,
        out_shape=outs,
        in_specs=specs if specs is not None else [VMEM] * len(args),
        out_specs=out_specs if out_specs is not None else jax.tree.map(lambda _: VMEM, outs),
        scratch_shapes=list(scratch),
        compiler_params=PARAMS,
        cost_estimate=pl.CostEstimate(flops=flops, bytes_accessed=1 << 20, transcendentals=1 << 18),
    )(*args)


def by_kernels(
    pair_repr,
    distance_bins,
    chain_lengths,
    left_weight,
    left_gate_weight,
    right_weight,
    right_gate_weight,
    out_weight,
    out_gate_weight,
    dist_weight,
):
    tile_rows, tile_cols, channels = pair_repr.shape
    rows, cols = lax.axis_size("row"), lax.axis_size("col")
    places = rows * cols
    width = 2 * tile_cols
    spots = tile_rows * tile_cols
    size = channels // OWNERS // 2 * tile_rows
    bf16, f32 = jnp.bfloat16, jnp.float32
    struct = jax.ShapeDtypeStruct
    turned = pltpu.VMEM((2 * channels, channels), bf16)
    held = pltpu.VMEM((OWNERS * size, width), f32)
    over_x, over_core, over_z, over_half = 1, cols, 2 * cols, OWNERS * cols
    near = exchange(pair_repr, places, over_z)
    normed = call(
        norm_kernel, struct((spots, channels), bf16), args=(pair_repr,), flops=1 << 30
    )
    stay, move = call(
        right_kernel,
        [struct((2 * size, width), bf16)] * 2,
        [turned, held],
        args=(normed, right_weight, right_gate_weight),
        flops=4 * spots * channels * channels,
    )
    cross = exchange(move, places, over_half + over_z)
    far = exchange(stay, places, over_half)
    block = struct((2 * size, width), bf16)
    own, core, masks = call(
        left_kernel,
        [block, block, struct((3 * tile_rows // 2, width), f32)],
        [turned, pltpu.VMEM((channels, channels), bf16), pltpu.VMEM((2 * size, width), f32)],
        [SMEM] + [VMEM] * 4,
        args=(chain_lengths, normed, left_weight, left_gate_weight, stay),
        flops=2 * spots * channels * channels,
    )
    near, near_over = call(
        near_kernel,
        [block, block],
        [
            pltpu.VMEM((4 * channels, channels), bf16),
            pltpu.VMEM((2 * channels, channels), bf16),
            pltpu.VMEM((2 * size, width), f32),
            pltpu.VMEM((2 * size, width), f32),
        ],
        args=(masks, near, left_weight, left_gate_weight, right_weight, right_gate_weight),
        flops=4 * spots * channels * channels,
    )
    near_over = exchange(near_over, places, over_core)
    core = exchange(core, places, over_core)
    both_over = call(
        pack_kernel,
        block,
        specs=[VMEM, VMEM, pl.BlockSpec(memory_space=pl.ANY)],
        args=(far, cross, near_over),
    )
    both_over = exchange(both_over, places, over_core)
    parts = call(
        tri_kernel,
        [struct((2 * size, width), bf16)] * OWNERS,
        [pltpu.VMEM((size // tile_rows, rows * tile_rows, width), bf16)],
        args=(masks, own, core, near, near_over, far, cross, both_over),
        flops=8 * size * 2 * tile_rows * 2 * width,
    )
    parts = [
        exchange(parts[d], places, d // 2 * over_z + d % 2 * over_x) if d else parts[0] for d in DIAGONAL_FIRST
    ]
    parts += [exchange(value, places, over_core) for value in parts]
    gate, x_turned, out_turned, dist_turned = call(
        gate_kernel,
        [
            struct((channels, spots), f32),
            struct((channels, spots), f32),
            struct((channels, channels), bf16),
            struct(dist_weight.shape[::-1], bf16),
        ],
        args=(pair_repr, normed, out_gate_weight, out_weight, dist_weight),
        flops=2 * spots * channels * channels,
    )
    pair_out, loss = call(
        finish_kernel,
        [struct((channels, spots), bf16), struct((places, 8, 128), f32)],
        [held],
        args=(
            masks,
            x_turned,
            gate,
            distance_bins.reshape(tile_rows // 2, width),
            out_turned,
            dist_turned,
            *parts,
        ),
        flops=6 * spots * channels * channels,
    )
    pair_out = call(turn_back_kernel, struct(pair_repr.shape, bf16), args=(pair_out,), flops=1 << 26)
    loss = lax.all_to_all(loss, AXES, 0, 0, tiled=True)
    return (pair_out, jnp.sum(loss, axis=0)[0, :1])


def by_all_to_all(
    pair_repr,
    distance_bins,
    chain_lengths,
    left_weight,
    left_gate_weight,
    right_weight,
    right_gate_weight,
    out_weight,
    out_gate_weight,
    dist_weight,
):
    tile_rows, tile_cols, channels = pair_repr.shape
    rows, cols = lax.axis_size("row"), lax.axis_size("col")
    peers = rows * cols
    share = channels // peers
    residues = tile_rows * rows
    spots = tile_rows * tile_cols
    live_count = residues - chain_lengths[chain_lengths.shape[0] - 1]
    row_place = lax.axis_index("row") * tile_rows + jnp.arange(tile_rows, dtype=jnp.int32)
    col_place = lax.axis_index("col") * tile_cols + jnp.arange(tile_cols, dtype=jnp.int32)
    live_rows = (row_place < live_count).astype(jnp.float32)
    live_cols = (col_place < live_count).astype(jnp.float32)
    flat_mask = (live_rows[:, None] * live_cols[None, :]).reshape(-1)
    normed = layer_norm(pair_repr.astype(jnp.float32), -1).astype(jnp.bfloat16)
    normed = normed.reshape(spots, channels)

    def project_turned(weight):
        return lax.dot_general(
            weight, normed, (((0,), (1,)), ((), ())), preferred_element_type=jnp.float32
        )

    def gated(gate_weight, weight):
        values = jax.nn.sigmoid(project_turned(gate_weight)) * project_turned(weight)
        return (values * flat_mask[None, :]).astype(jnp.bfloat16)

    left = gated(left_gate_weight, left_weight).reshape(peers, share, tile_rows, tile_cols)
    right = gated(right_gate_weight, right_weight).reshape(peers, share, tile_rows, tile_cols)
    both = jnp.concatenate([left, right], axis=3).reshape(peers, share * tile_rows, 2 * tile_cols)
    owned = lax.all_to_all(both, AXES, split_axis=0, concat_axis=0, tiled=True)
    owned = owned.reshape(rows, cols, share, tile_rows, 2, tile_cols)
    owned = owned.transpose(4, 2, 0, 3, 1, 5).reshape(2, share, residues, residues)
    tri = jnp.einsum(
        "cik,cjk->cij", owned[0], owned[1], preferred_element_type=jnp.float32
    ).astype(jnp.bfloat16)
    tri = tri.reshape(share, rows, tile_rows, cols, tile_cols).transpose(1, 3, 0, 2, 4)
    tri = tri.reshape(peers, share, spots)
    tri = lax.all_to_all(tri, AXES, split_axis=0, concat_axis=0, tiled=True)
    tri = tri.reshape(channels, spots).astype(jnp.float32)
    tri_normed = layer_norm(tri, 0).astype(jnp.bfloat16)
    out_gate = jax.nn.sigmoid(jnp.dot(normed, out_gate_weight, preferred_element_type=jnp.float32))
    update = out_gate * tn_dot(tri_normed, out_weight)
    pair_out = (pair_repr.astype(jnp.float32).reshape(spots, channels) + update).astype(
        jnp.bfloat16
    )
    logits = jnp.dot(pair_out, dist_weight, preferred_element_type=jnp.float32)
    log_total = jnp.log(jnp.sum(jnp.exp(logits), axis=-1))
    bin_ids = jnp.arange(logits.shape[1], dtype=jnp.int32)
    picked = jnp.sum(
        jnp.where(bin_ids[None, :] == distance_bins.reshape(-1, 1), logits, 0.0), axis=-1
    )
    loss_sum = jnp.sum(flat_mask * (log_total - picked))
    sums = lax.all_to_all(
        jnp.full((peers, 1, 128), loss_sum), AXES, split_axis=0, concat_axis=0, tiled=True
    )
    pair_count = (live_count * live_count).astype(jnp.float32)
    loss_value = (jnp.sum(sums[:, 0, 0]) / pair_count).reshape(1)
    return (pair_out.reshape(pair_repr.shape), loss_value)


def on_device(pair_repr, *others):
    tile_rows, tile_cols, channels = pair_repr.shape
    rows, cols = lax.axis_size("row"), lax.axis_size("col")
    fits = (
        rows == 2 * OWNERS
        and cols == 2
        and tile_rows * rows == tile_cols * cols
        and 2 * tile_cols == 128
        and tile_rows == 16
        and channels == 32 * OWNERS
    )
    return (by_kernels if fits else by_all_to_all)(pair_repr, *others)


def solution(mesh):
    in_specs = (
        P(("groups", "row"), "col", None),
        P(("groups", "row"), "col"),
        P("groups"),
        P(),
        P(),
        P(),
        P(),
        P(),
        P(),
        P(),
    )
    out_specs = (P(("groups", "row"), "col", None), P("groups"))
    return jax.shard_map(
        on_device, mesh=mesh, in_specs=in_specs, out_specs=out_specs, check_vma=False
    )
```

```python
import jax
import jax.numpy as jnp
from jax import lax
from jax.experimental import pallas as pl
from jax.experimental.pallas import tpu as pltpu
from jax.sharding import PartitionSpec as P

AXES = ("row", "col")
OWNERS = 4
DIAGONAL_FIRST = (3, 1, 2, 0)
VMEM = pl.BlockSpec(memory_space=pltpu.VMEM)
SMEM = pl.BlockSpec(memory_space=pltpu.SMEM)
PARAMS = pltpu.CompilerParams(vmem_limit_bytes=24 * 1024 * 1024)


def layer_norm(values, axis):
    average = jnp.mean(values, axis=axis, keepdims=True)
    centred = values - average
    spread = jnp.mean(centred * centred, axis=axis, keepdims=True)
    return centred * lax.rsqrt(spread + 1e-05)


def sigmoid(values):
    return 0.5 * jnp.tanh(0.5 * values) + 0.5


def nt_dot(a, b):
    return lax.dot_general(a, b, (((1,), (1,)), ((), ())), preferred_element_type=jnp.float32)


def tn_dot(a, b):
    return lax.dot_general(a, b, (((0,), (0,)), ((), ())), preferred_element_type=jnp.float32)


def lanes_of(shape):
    return lax.broadcasted_iota(jnp.int32, shape, 1)


def make_masks(lens_ref, tile_rows, tile_cols):
    live = tile_rows * lax.axis_size("row") - lens_ref[lens_ref.shape[0] - 1]
    lane = lanes_of((1, 2 * tile_cols))
    upper = (lane >= tile_cols).astype(jnp.int32)
    place = lane - tile_cols * upper
    row, col = lax.axis_index("row"), lax.axis_index("col")
    keeps = [(place + (col ^ dx) * tile_cols < live).astype(jnp.float32) for dx in (0, 1)]
    pairs = [
        ((row ^ d) * tile_rows + first + upper < live).astype(jnp.float32) * keeps[0]
        for d in (0, OWNERS // 2)
        for first in range(0, tile_rows, 2)
    ]
    count = jnp.full(lane.shape, live * live, jnp.int32).astype(jnp.float32)
    return pairs, keeps, 1.0 / count


def turn(w_refs, turned):
    channels = w_refs[0].shape[0]
    share = channels // OWNERS
    half = share // 2
    for at, w_ref in enumerate(w_refs):
        w = w_ref[...].astype(jnp.float32).T
        blocks = [
            w[o * share + g * half : o * share + (g + 1) * half] for g in (0, 1) for o in range(OWNERS)
        ]
        turned[at * channels : (at + 1) * channels] = jnp.concatenate(blocks, 0).astype(jnp.bfloat16)


def store_rows(held, first, value, tile_cols):
    packed = value.shape[0] // 2
    stride = held.shape[0] // packed
    a, b = value[:packed], value[packed:]
    low = lanes_of(a.shape) < tile_cols
    held[pl.ds(first, packed, stride=stride), :] = jnp.where(low, a, pltpu.roll(b, tile_cols, 1))
    held[pl.ds(first + 1, packed, stride=stride), :] = jnp.where(low, pltpu.roll(a, tile_cols, 1), b)


def chip_rows(turned, mine):
    size = mine.shape[0] // (turned.shape[0] // mine.shape[1]) // 2
    pair = owner_place() // 2
    for at in range(mine.shape[0] // size):
        start = pl.multiple_of(at * (mine.shape[1] // 2) + pair * size, size)
        mine[at * size : (at + 1) * size] = turned[pl.ds(start, size), :]


def owner_place():
    return lax.axis_index("row") % OWNERS


def owner_block(held, d, size):
    at = pl.multiple_of((owner_place() ^ d) * size, size)
    return held[pl.ds(at, size)].astype(jnp.bfloat16)


def core_block(held, d, size):
    at = pl.multiple_of((owner_place() % 2 ^ d) * size, size)
    return held[pl.ds(at, size)].astype(jnp.bfloat16)


def norm_kernel(x_ref, normed_ref):
    x = x_ref[...].astype(jnp.float32).reshape(normed_ref.shape)
    normed_ref[...] = layer_norm(x, -1).astype(jnp.bfloat16)


def right_kernel(normed_ref, w_ref, g_ref, stay_ref, move_ref, turned, held):
    channels = normed_ref.shape[1]
    width = held.shape[1]
    turn((w_ref, g_ref), turned)
    for at in range(normed_ref.shape[0] // width):
        flat = nt_dot(turned[...], normed_ref[at * width : (at + 1) * width])
        store_rows(held, 2 * at, sigmoid(flat[channels:]) * flat[:channels], width // 2)
    size = stay_ref.shape[0] // 2
    for d, ref in enumerate((stay_ref, stay_ref, move_ref, move_ref)):
        ref[d % 2 * size : (d % 2 + 1) * size] = owner_block(held, d, size)


def left_kernel(lens_ref, normed_ref, w_ref, g_ref, stay_ref, own_ref, core_ref, masks_ref, *refs):
    turned, mine, held = refs
    width = held.shape[1]
    half = mine.shape[0] // 2
    pairs, keeps, share = make_masks(lens_ref, 2 * normed_ref.shape[0] // width, width // 2)
    masks_ref[...] = jnp.concatenate(
        pairs + keeps + [share] * (masks_ref.shape[0] - len(pairs) - len(keeps)), 0
    )
    turn((w_ref, g_ref), turned)
    chip_rows(turned, mine)
    for at in range(normed_ref.shape[0] // width):
        flat = nt_dot(mine[...], normed_ref[at * width : (at + 1) * width])
        store_rows(held, 2 * at, sigmoid(flat[half:]) * flat[:half] * pairs[at], width // 2)
    size = stay_ref.shape[0] // 2
    for d, ref in enumerate((own_ref, core_ref)):
        ref[:size] = core_block(held, d, size)
        ref[size:] = stay_ref[d * size : (d + 1) * size]


def near_kernel(masks_ref, x_ref, lw_ref, lg_ref, rw_ref, rg_ref, near_ref, over_ref, *refs):
    turned, mine, held_left, held_right = refs
    tile_rows, tile_cols, channels = x_ref.shape
    share = mine.shape[0] // 4
    turn((lw_ref, lg_ref, rw_ref, rg_ref), turned)
    chip_rows(turned, mine)
    for first in range(0, tile_rows, 2):
        x = x_ref[first : first + 2].astype(jnp.float32).reshape(2 * tile_cols, channels)
        flat = nt_dot(mine[...], layer_norm(x, -1).astype(jnp.bfloat16))
        lv, lg, rv, rg = [flat[at * share : (at + 1) * share] for at in range(4)]
        line = (tile_rows + first) // 2
        store_rows(held_left, first, sigmoid(lg) * lv * masks_ref[line : line + 1], tile_cols)
        store_rows(held_right, first, sigmoid(rg) * rv, tile_cols)
    size = near_ref.shape[0] // 2
    for d, ref in enumerate((near_ref, over_ref)):
        ref[:size] = core_block(held_left, d, size)
        ref[size:] = core_block(held_right, d, size)


def pack_kernel(far_ref, cross_ref, ready_ref, out_ref):
    del ready_ref
    size = out_ref.shape[0] // 2
    out_ref[:size] = far_ref[size:]
    out_ref[size:] = cross_ref[size:]


def gate_kernel(x_ref, normed_ref, gw_ref, ow_ref, dw_ref, gate_ref, x_turned_ref, ow_turned, dw_turned):
    tile_rows, tile_cols, channels = x_ref.shape
    share = channels // OWNERS
    half = share // 2
    blocks = [
        ow_ref[o * share + g * half : o * share + (g + 1) * half].astype(jnp.float32)
        for g in (0, 1)
        for o in range(OWNERS)
    ]
    ow_turned[...] = jnp.concatenate(blocks, 0).T.astype(jnp.bfloat16)
    dw_turned[...] = dw_ref[...].astype(jnp.float32).T.astype(jnp.bfloat16)
    gate_turned = gw_ref[...].astype(jnp.float32).T.astype(jnp.bfloat16)
    for first in range(0, tile_rows, 2):
        at = slice(first * tile_cols, (first + 2) * tile_cols)
        gate_ref[:, at] = sigmoid(nt_dot(gate_turned, normed_ref[at]))
        x = x_ref[first : first + 2].astype(jnp.float32).reshape(2 * tile_cols, channels)
        x_turned_ref[:, at] = x.T


def tri_kernel(masks_ref, own, core, near, near_over, far, cross, both_over, *refs):
    outs, rights = refs[:-1], refs[-1]
    half, _, width = rights.shape
    size = own.shape[0] // 2
    tile_rows = size // half
    side = OWNERS * tile_rows
    me, col = lax.axis_index("row"), lax.axis_index("col")
    lefts = (own, core, near, near_over)
    pieces = (
        (0, own, size),
        (1, core, size),
        (2, near, size),
        (3, near_over, size),
        (4, far, 0),
        (5, both_over, 0),
        (6, cross, 0),
        (7, both_over, size),
    )
    for away, ref, start in pieces:
        at = pl.multiple_of((me ^ away) * tile_rows, tile_rows)
        for m in range(half):
            rights[m, pl.ds(at, tile_rows), :] = ref[
                start + m * tile_rows : start + (m + 1) * tile_rows
            ]
    low = lanes_of((side, width)) < width // 2
    first = masks_ref.shape[0] - tile_rows // 2
    keep = jnp.concatenate([masks_ref[first : first + 1], masks_ref[first + 1 : first + 2]], 1)
    for m in range(half):
        left = jnp.concatenate(
            [ref[m * tile_rows : (m + 1) * tile_rows] for ref in lefts], 0
        )
        pieces = []
        for dx in (0, 1):
            block = rights[m, pl.ds(pl.multiple_of((col ^ dx) * side, side), side), :]
            block = block.astype(jnp.float32)
            pieces += [jnp.where(low, block, 0.0), jnp.where(low, 0.0, block)]
        right = jnp.concatenate(pieces, 0).astype(jnp.bfloat16)
        product = (nt_dot(left, right) * keep).astype(jnp.bfloat16)
        for d in range(OWNERS):
            for dx in (0, 1):
                at = d % 2 * size + m * tile_rows
                outs[d // 2 * 2 + dx][at : at + tile_rows] = product[
                    d * tile_rows : (d + 1) * tile_rows, dx * width : (dx + 1) * width
                ]


def finish_kernel(masks_ref, x_ref, gate_ref, bins_ref, ow_ref, dw_ref, *refs):
    parts, overs = [
        [refs[first + DIAGONAL_FIRST.index(d)] for d in range(OWNERS)] for first in (0, OWNERS)
    ]
    out_ref, loss_ref, held = refs[2 * OWNERS :]
    channels = x_ref.shape[0]
    size, width = parts[0].shape[0] // 2, parts[0].shape[1]
    half = channels // 2 // OWNERS
    tile_rows, tile_cols = size // half, width // 2
    packed = OWNERS * half
    owner = owner_place()
    total = jnp.zeros((tile_rows, width), jnp.float32)
    for d in range(OWNERS):
        refs, at = ((parts, 0), (overs, size))[d % 2]
        a, b = [refs[d // 2 * 2 + dx][at : at + size].astype(jnp.float32) for dx in (0, 1)]
        block = a + b
        held[pl.ds(pl.multiple_of((owner ^ d) * size, size), size), :] = block
        total = total + jnp.sum(block.reshape(half, tile_rows, width), 0)
    average = (total + pltpu.roll(total, tile_cols, 1)) * (1.0 / channels)
    total = jnp.zeros((tile_rows, width), jnp.float32)
    for om in range(packed):
        centred = held[om * tile_rows : (om + 1) * tile_rows] - average
        total = total + centred * centred
    spread = (total + pltpu.roll(total, tile_cols, 1)) * (1.0 / channels)
    scale = lax.rsqrt(spread + 1e-05)
    low = lanes_of((packed, width)) < tile_cols
    bin_ids = lax.broadcasted_iota(jnp.int32, (dw_ref.shape[0], width), 0)
    loss = jnp.zeros((1, width), jnp.float32)
    for first in range(0, tile_rows, 2):
        a, b = [
            (held[pl.ds(ii, packed, stride=tile_rows), :] - average[ii : ii + 1]) * scale[ii : ii + 1]
            for ii in (first, first + 1)
        ]
        normed = jnp.concatenate(
            [
                jnp.where(low, a, pltpu.roll(b, tile_cols, 1)),
                jnp.where(low, pltpu.roll(a, tile_cols, 1), b),
            ],
            0,
        ).astype(jnp.bfloat16)
        update = jnp.dot(ow_ref[...], normed, preferred_element_type=jnp.float32)
        at = slice(first * tile_cols, (first + 2) * tile_cols)
        pair_out = (x_ref[:, at] + gate_ref[:, at] * update).astype(jnp.bfloat16)
        out_ref[:, at] = pair_out
        logits = jnp.dot(dw_ref[...], pair_out, preferred_element_type=jnp.float32)
        log_total = jnp.log(jnp.sum(jnp.exp(logits), axis=0, keepdims=True))
        bins = bins_ref[first // 2 : first // 2 + 1]
        picked = jnp.sum(jnp.where(bin_ids == bins, logits, 0.0), axis=0, keepdims=True)
        loss = loss + masks_ref[first // 2 : first // 2 + 1] * (log_total - picked)
    last = masks_ref.shape[0] - 1
    loss = jnp.sum(loss * masks_ref[last : last + 1], axis=1, keepdims=True)
    loss_ref[...] = jnp.broadcast_to(loss, loss_ref.shape)


def turn_back_kernel(turned_ref, out_ref):
    tile_rows, tile_cols, channels = out_ref.shape
    for first in range(0, tile_rows, 2):
        block = turned_ref[:, first * tile_cols : (first + 2) * tile_cols].astype(jnp.float32).T
        out_ref[first : first + 2] = block.astype(jnp.bfloat16).reshape(2, tile_cols, channels)


def exchange(value, places, mask):
    return lax.ppermute(value, AXES, [(at, at ^ mask) for at in range(places)])


def call(kernel, outs, scratch=(), specs=None, out_specs=None, args=(), flops=0):
    return pl.pallas_call(
        kernel,
        out_shape=outs,
        in_specs=specs if specs is not None else [VMEM] * len(args),
        out_specs=out_specs if out_specs is not None else jax.tree.map(lambda _: VMEM, outs),
        scratch_shapes=list(scratch),
        compiler_params=PARAMS,
        cost_estimate=pl.CostEstimate(flops=flops, bytes_accessed=1 << 20, transcendentals=1 << 18),
    )(*args)


def by_kernels(
    pair_repr,
    distance_bins,
    chain_lengths,
    left_weight,
    left_gate_weight,
    right_weight,
    right_gate_weight,
    out_weight,
    out_gate_weight,
    dist_weight,
):
    tile_rows, tile_cols, channels = pair_repr.shape
    rows, cols = lax.axis_size("row"), lax.axis_size("col")
    places = rows * cols
    width = 2 * tile_cols
    spots = tile_rows * tile_cols
    size = channels // OWNERS // 2 * tile_rows
    bf16, f32 = jnp.bfloat16, jnp.float32
    struct = jax.ShapeDtypeStruct
    turned = pltpu.VMEM((2 * channels, channels), bf16)
    held = pltpu.VMEM((OWNERS * size, width), f32)
    over_x, over_core, over_z, over_half = 1, cols, 2 * cols, OWNERS * cols
    near = exchange(pair_repr, places, over_z)
    normed = call(
        norm_kernel, struct((spots, channels), bf16), args=(pair_repr,), flops=1 << 30
    )
    stay, move = call(
        right_kernel,
        [struct((2 * size, width), bf16)] * 2,
        [turned, held],
        args=(normed, right_weight, right_gate_weight),
        flops=4 * spots * channels * channels,
    )
    cross = exchange(move, places, over_half + over_z)
    far = exchange(stay, places, over_half)
    block = struct((2 * size, width), bf16)
    own, core, masks = call(
        left_kernel,
        [block, block, struct((3 * tile_rows // 2, width), f32)],
        [turned, pltpu.VMEM((channels, channels), bf16), pltpu.VMEM((2 * size, width), f32)],
        [SMEM] + [VMEM] * 4,
        args=(chain_lengths, normed, left_weight, left_gate_weight, stay),
        flops=2 * spots * channels * channels,
    )
    near, near_over = call(
        near_kernel,
        [block, block],
        [
            pltpu.VMEM((4 * channels, channels), bf16),
            pltpu.VMEM((2 * channels, channels), bf16),
            pltpu.VMEM((2 * size, width), f32),
            pltpu.VMEM((2 * size, width), f32),
        ],
        args=(masks, near, left_weight, left_gate_weight, right_weight, right_gate_weight),
        flops=4 * spots * channels * channels,
    )
    near_over = exchange(near_over, places, over_core)
    core = exchange(core, places, over_core)
    both_over = call(
        pack_kernel,
        block,
        specs=[VMEM, VMEM, pl.BlockSpec(memory_space=pl.ANY)],
        args=(far, cross, near_over),
    )
    both_over = exchange(both_over, places, over_core)
    parts = call(
        tri_kernel,
        [struct((2 * size, width), bf16)] * OWNERS,
        [pltpu.VMEM((size // tile_rows, rows * tile_rows, width), bf16)],
        args=(masks, own, core, near, near_over, far, cross, both_over),
        flops=8 * size * 2 * tile_rows * 2 * width,
    )
    parts = [
        exchange(parts[d], places, d // 2 * over_z + d % 2 * over_x) if d else parts[0] for d in DIAGONAL_FIRST
    ]
    parts += [exchange(value, places, over_core) for value in parts]
    gate, x_turned, out_turned, dist_turned = call(
        gate_kernel,
        [
            struct((channels, spots), f32),
            struct((channels, spots), f32),
            struct((channels, channels), bf16),
            struct(dist_weight.shape[::-1], bf16),
        ],
        args=(pair_repr, normed, out_gate_weight, out_weight, dist_weight),
        flops=2 * spots * channels * channels,
    )
    pair_out, loss = call(
        finish_kernel,
        [struct((channels, spots), bf16), struct((8, 128), f32)],
        [held],
        args=(
            masks,
            x_turned,
            gate,
            distance_bins.reshape(tile_rows // 2, width),
            out_turned,
            dist_turned,
            *parts,
        ),
        flops=6 * spots * channels * channels,
    )
    pair_out = call(turn_back_kernel, struct(pair_repr.shape, bf16), args=(pair_out,), flops=1 << 26)
    loss = loss + exchange(loss, places, over_core)
    diagonal, beside, near_loss = [
        exchange(loss, places, mask) for mask in (over_z + over_x, over_x, over_z)
    ]
    loss = (diagonal + near_loss) + (beside + loss)
    loss = loss + exchange(loss, places, over_half)
    return (pair_out, loss[0, :1])


def by_all_to_all(
    pair_repr,
    distance_bins,
    chain_lengths,
    left_weight,
    left_gate_weight,
    right_weight,
    right_gate_weight,
    out_weight,
    out_gate_weight,
    dist_weight,
):
    tile_rows, tile_cols, channels = pair_repr.shape
    rows, cols = lax.axis_size("row"), lax.axis_size("col")
    peers = rows * cols
    share = channels // peers
    residues = tile_rows * rows
    spots = tile_rows * tile_cols
    live_count = residues - chain_lengths[chain_lengths.shape[0] - 1]
    row_place = lax.axis_index("row") * tile_rows + jnp.arange(tile_rows, dtype=jnp.int32)
    col_place = lax.axis_index("col") * tile_cols + jnp.arange(tile_cols, dtype=jnp.int32)
    live_rows = (row_place < live_count).astype(jnp.float32)
    live_cols = (col_place < live_count).astype(jnp.float32)
    flat_mask = (live_rows[:, None] * live_cols[None, :]).reshape(-1)
    normed = layer_norm(pair_repr.astype(jnp.float32), -1).astype(jnp.bfloat16)
    normed = normed.reshape(spots, channels)

    def project_turned(weight):
        return lax.dot_general(
            weight, normed, (((0,), (1,)), ((), ())), preferred_element_type=jnp.float32
        )

    def gated(gate_weight, weight):
        values = jax.nn.sigmoid(project_turned(gate_weight)) * project_turned(weight)
        return (values * flat_mask[None, :]).astype(jnp.bfloat16)

    left = gated(left_gate_weight, left_weight).reshape(peers, share, tile_rows, tile_cols)
    right = gated(right_gate_weight, right_weight).reshape(peers, share, tile_rows, tile_cols)
    both = jnp.concatenate([left, right], axis=3).reshape(peers, share * tile_rows, 2 * tile_cols)
    owned = lax.all_to_all(both, AXES, split_axis=0, concat_axis=0, tiled=True)
    owned = owned.reshape(rows, cols, share, tile_rows, 2, tile_cols)
    owned = owned.transpose(4, 2, 0, 3, 1, 5).reshape(2, share, residues, residues)
    tri = jnp.einsum(
        "cik,cjk->cij", owned[0], owned[1], preferred_element_type=jnp.float32
    ).astype(jnp.bfloat16)
    tri = tri.reshape(share, rows, tile_rows, cols, tile_cols).transpose(1, 3, 0, 2, 4)
    tri = tri.reshape(peers, share, spots)
    tri = lax.all_to_all(tri, AXES, split_axis=0, concat_axis=0, tiled=True)
    tri = tri.reshape(channels, spots).astype(jnp.float32)
    tri_normed = layer_norm(tri, 0).astype(jnp.bfloat16)
    out_gate = jax.nn.sigmoid(jnp.dot(normed, out_gate_weight, preferred_element_type=jnp.float32))
    update = out_gate * tn_dot(tri_normed, out_weight)
    pair_out = (pair_repr.astype(jnp.float32).reshape(spots, channels) + update).astype(
        jnp.bfloat16
    )
    logits = jnp.dot(pair_out, dist_weight, preferred_element_type=jnp.float32)
    log_total = jnp.log(jnp.sum(jnp.exp(logits), axis=-1))
    bin_ids = jnp.arange(logits.shape[1], dtype=jnp.int32)
    picked = jnp.sum(
        jnp.where(bin_ids[None, :] == distance_bins.reshape(-1, 1), logits, 0.0), axis=-1
    )
    loss_sum = jnp.sum(flat_mask * (log_total - picked))
    sums = lax.all_to_all(
        jnp.full((peers, 1, 128), loss_sum), AXES, split_axis=0, concat_axis=0, tiled=True
    )
    pair_count = (live_count * live_count).astype(jnp.float32)
    loss_value = (jnp.sum(sums[:, 0, 0]) / pair_count).reshape(1)
    return (pair_out.reshape(pair_repr.shape), loss_value)


def on_device(pair_repr, *others):
    tile_rows, tile_cols, channels = pair_repr.shape
    rows, cols = lax.axis_size("row"), lax.axis_size("col")
    fits = (
        rows == 2 * OWNERS
        and cols == 2
        and tile_rows * rows == tile_cols * cols
        and 2 * tile_cols == 128
        and tile_rows == 16
        and channels == 32 * OWNERS
    )
    return (by_kernels if fits else by_all_to_all)(pair_repr, *others)


def solution(mesh):
    in_specs = (
        P(("groups", "row"), "col", None),
        P(("groups", "row"), "col"),
        P("groups"),
        P(),
        P(),
        P(),
        P(),
        P(),
        P(),
        P(),
    )
    out_specs = (P(("groups", "row"), "col", None), P("groups"))
    return jax.shard_map(
        on_device, mesh=mesh, in_specs=in_specs, out_specs=out_specs, check_vma=False
    )
```

```python
import jax
import jax.numpy as jnp
from jax import lax
from jax.experimental import pallas as pl
from jax.experimental.pallas import tpu as pltpu
from jax.sharding import PartitionSpec as P

AXES = ("row", "col")
OWNERS = 4
DIAGONAL_FIRST = (0, 3, 1, 2)
VMEM = pl.BlockSpec(memory_space=pltpu.VMEM)
SMEM = pl.BlockSpec(memory_space=pltpu.SMEM)
PARAMS = pltpu.CompilerParams(vmem_limit_bytes=24 * 1024 * 1024)


def layer_norm(values, axis):
    average = jnp.mean(values, axis=axis, keepdims=True)
    centred = values - average
    spread = jnp.mean(centred * centred, axis=axis, keepdims=True)
    return centred * lax.rsqrt(spread + 1e-05)


def sigmoid(values):
    return 0.5 * jnp.tanh(0.5 * values) + 0.5


def nt_dot(a, b):
    return lax.dot_general(a, b, (((1,), (1,)), ((), ())), preferred_element_type=jnp.float32)


def tn_dot(a, b):
    return lax.dot_general(a, b, (((0,), (0,)), ((), ())), preferred_element_type=jnp.float32)


def lanes_of(shape):
    return lax.broadcasted_iota(jnp.int32, shape, 1)


def make_masks(lens_ref, tile_rows, tile_cols):
    live = tile_rows * lax.axis_size("row") - lens_ref[lens_ref.shape[0] - 1]
    lane = lanes_of((1, 2 * tile_cols))
    upper = (lane >= tile_cols).astype(jnp.int32)
    place = lane - tile_cols * upper
    row, col = lax.axis_index("row"), lax.axis_index("col")
    keeps = [(place + (col ^ dx) * tile_cols < live).astype(jnp.float32) for dx in (0, 1)]
    pairs = [
        ((row ^ d) * tile_rows + first + upper < live).astype(jnp.float32) * keeps[0]
        for d in (0, OWNERS // 2)
        for first in range(0, tile_rows, 2)
    ]
    count = jnp.full(lane.shape, live * live, jnp.int32).astype(jnp.float32)
    return pairs, keeps, 1.0 / count


def turn(w_refs, turned):
    channels = w_refs[0].shape[0]
    share = channels // OWNERS
    half = share // 2
    for at, w_ref in enumerate(w_refs):
        w = w_ref[...].astype(jnp.float32).T
        blocks = [
            w[o * share + g * half : o * share + (g + 1) * half] for g in (0, 1) for o in range(OWNERS)
        ]
        turned[at * channels : (at + 1) * channels] = jnp.concatenate(blocks, 0).astype(jnp.bfloat16)


def store_rows(held, first, value, tile_cols):
    packed = value.shape[0] // 2
    stride = held.shape[0] // packed
    a, b = value[:packed], value[packed:]
    low = lanes_of(a.shape) < tile_cols
    held[pl.ds(first, packed, stride=stride), :] = jnp.where(low, a, pltpu.roll(b, tile_cols, 1))
    held[pl.ds(first + 1, packed, stride=stride), :] = jnp.where(low, pltpu.roll(a, tile_cols, 1), b)


def chip_rows(turned, mine):
    size = mine.shape[0] // (turned.shape[0] // mine.shape[1]) // 2
    pair = owner_place() // 2
    for at in range(mine.shape[0] // size):
        start = pl.multiple_of(at * (mine.shape[1] // 2) + pair * size, size)
        mine[at * size : (at + 1) * size] = turned[pl.ds(start, size), :]


def owner_place():
    return lax.axis_index("row") % OWNERS


def owner_block(held, d, size):
    at = pl.multiple_of((owner_place() ^ d) * size, size)
    return held[pl.ds(at, size)].astype(jnp.bfloat16)


def core_block(held, d, size):
    at = pl.multiple_of((owner_place() % 2 ^ d) * size, size)
    return held[pl.ds(at, size)].astype(jnp.bfloat16)


def norm_kernel(x_ref, normed_ref):
    x = x_ref[...].astype(jnp.float32).reshape(normed_ref.shape)
    normed_ref[...] = layer_norm(x, -1).astype(jnp.bfloat16)


def right_kernel(normed_ref, w_ref, g_ref, stay_ref, move_ref, turned, held):
    channels = normed_ref.shape[1]
    width = held.shape[1]
    turn((w_ref, g_ref), turned)
    for at in range(normed_ref.shape[0] // width):
        flat = nt_dot(turned[...], normed_ref[at * width : (at + 1) * width])
        store_rows(held, 2 * at, sigmoid(flat[channels:]) * flat[:channels], width // 2)
    size = stay_ref.shape[0] // 2
    for d, ref in enumerate((stay_ref, stay_ref, move_ref, move_ref)):
        ref[d % 2 * size : (d % 2 + 1) * size] = owner_block(held, d, size)


def left_kernel(lens_ref, normed_ref, w_ref, g_ref, stay_ref, own_ref, core_ref, masks_ref, *refs):
    turned, mine, held = refs
    width = held.shape[1]
    half = mine.shape[0] // 2
    pairs, keeps, share = make_masks(lens_ref, 2 * normed_ref.shape[0] // width, width // 2)
    masks_ref[...] = jnp.concatenate(
        pairs + keeps + [share] * (masks_ref.shape[0] - len(pairs) - len(keeps)), 0
    )
    turn((w_ref, g_ref), turned)
    chip_rows(turned, mine)
    for at in range(normed_ref.shape[0] // width):
        flat = nt_dot(mine[...], normed_ref[at * width : (at + 1) * width])
        store_rows(held, 2 * at, sigmoid(flat[half:]) * flat[:half] * pairs[at], width // 2)
    size = stay_ref.shape[0] // 2
    for d, ref in enumerate((own_ref, core_ref)):
        ref[:size] = core_block(held, d, size)
        ref[size:] = stay_ref[d * size : (d + 1) * size]


def near_kernel(masks_ref, x_ref, lw_ref, lg_ref, rw_ref, rg_ref, near_ref, over_ref, *refs):
    turned, mine, held_left, held_right = refs
    tile_rows, tile_cols, channels = x_ref.shape
    share = mine.shape[0] // 4
    turn((lw_ref, lg_ref, rw_ref, rg_ref), turned)
    chip_rows(turned, mine)
    for first in range(0, tile_rows, 2):
        x = x_ref[first : first + 2].astype(jnp.float32).reshape(2 * tile_cols, channels)
        flat = nt_dot(mine[...], layer_norm(x, -1).astype(jnp.bfloat16))
        lv, lg, rv, rg = [flat[at * share : (at + 1) * share] for at in range(4)]
        line = (tile_rows + first) // 2
        store_rows(held_left, first, sigmoid(lg) * lv * masks_ref[line : line + 1], tile_cols)
        store_rows(held_right, first, sigmoid(rg) * rv, tile_cols)
    size = near_ref.shape[0] // 2
    for d, ref in enumerate((near_ref, over_ref)):
        ref[:size] = core_block(held_left, d, size)
        ref[size:] = core_block(held_right, d, size)


def pack_kernel(far_ref, cross_ref, ready_ref, out_ref):
    del ready_ref
    size = out_ref.shape[0] // 2
    out_ref[:size] = far_ref[size:]
    out_ref[size:] = cross_ref[size:]


def gate_kernel(x_ref, normed_ref, gw_ref, ow_ref, dw_ref, gate_ref, x_turned_ref, ow_turned, dw_turned):
    tile_rows, tile_cols, channels = x_ref.shape
    share = channels // OWNERS
    half = share // 2
    blocks = [
        ow_ref[o * share + g * half : o * share + (g + 1) * half].astype(jnp.float32)
        for g in (0, 1)
        for o in range(OWNERS)
    ]
    ow_turned[...] = jnp.concatenate(blocks, 0).T.astype(jnp.bfloat16)
    dw_turned[...] = dw_ref[...].astype(jnp.float32).T.astype(jnp.bfloat16)
    gate_turned = gw_ref[...].astype(jnp.float32).T.astype(jnp.bfloat16)
    for first in range(0, tile_rows, 2):
        at = slice(first * tile_cols, (first + 2) * tile_cols)
        gate_ref[:, at] = sigmoid(nt_dot(gate_turned, normed_ref[at]))
        x = x_ref[first : first + 2].astype(jnp.float32).reshape(2 * tile_cols, channels)
        x_turned_ref[:, at] = x.T


def tri_kernel(masks_ref, own, core, near, near_over, far, cross, both_over, *refs):
    outs, rights = refs[:-1], refs[-1]
    half, _, width = rights.shape
    size = own.shape[0] // 2
    tile_rows = size // half
    side = OWNERS * tile_rows
    me, col = lax.axis_index("row"), lax.axis_index("col")
    lefts = (own, core, near, near_over)
    pieces = (
        (0, own, size),
        (1, core, size),
        (2, near, size),
        (3, near_over, size),
        (4, far, 0),
        (5, both_over, 0),
        (6, cross, 0),
        (7, both_over, size),
    )
    for away, ref, start in pieces:
        at = pl.multiple_of((me ^ away) * tile_rows, tile_rows)
        for m in range(half):
            rights[m, pl.ds(at, tile_rows), :] = ref[
                start + m * tile_rows : start + (m + 1) * tile_rows
            ]
    low = lanes_of((side, width)) < width // 2
    first = masks_ref.shape[0] - tile_rows // 2
    keep = jnp.concatenate([masks_ref[first : first + 1], masks_ref[first + 1 : first + 2]], 1)
    for m in range(half):
        left = jnp.concatenate(
            [ref[m * tile_rows : (m + 1) * tile_rows] for ref in lefts], 0
        )
        pieces = []
        for dx in (0, 1):
            block = rights[m, pl.ds(pl.multiple_of((col ^ dx) * side, side), side), :]
            block = block.astype(jnp.float32)
            pieces += [jnp.where(low, block, 0.0), jnp.where(low, 0.0, block)]
        right = jnp.concatenate(pieces, 0).astype(jnp.bfloat16)
        product = (nt_dot(left, right) * keep).astype(jnp.bfloat16)
        for d in range(OWNERS):
            for dx in (0, 1):
                at = d % 2 * size + m * tile_rows
                outs[d // 2 * 2 + dx][at : at + tile_rows] = product[
                    d * tile_rows : (d + 1) * tile_rows, dx * width : (dx + 1) * width
                ]


def finish_kernel(masks_ref, x_ref, gate_ref, bins_ref, ow_ref, dw_ref, *refs):
    parts, overs = [
        [refs[first + DIAGONAL_FIRST.index(d)] for d in range(OWNERS)] for first in (0, OWNERS)
    ]
    out_ref, loss_ref, held = refs[2 * OWNERS :]
    channels = x_ref.shape[0]
    size, width = parts[0].shape[0] // 2, parts[0].shape[1]
    half = channels // 2 // OWNERS
    tile_rows, tile_cols = size // half, width // 2
    packed = OWNERS * half
    owner = owner_place()
    total = jnp.zeros((tile_rows, width), jnp.float32)
    for d in range(OWNERS):
        refs, at = ((parts, 0), (overs, size))[d % 2]
        a, b = [refs[d // 2 * 2 + dx][at : at + size].astype(jnp.float32) for dx in (0, 1)]
        block = a + b
        held[pl.ds(pl.multiple_of((owner ^ d) * size, size), size), :] = block
        total = total + jnp.sum(block.reshape(half, tile_rows, width), 0)
    average = (total + pltpu.roll(total, tile_cols, 1)) * (1.0 / channels)
    total = jnp.zeros((tile_rows, width), jnp.float32)
    for om in range(packed):
        centred = held[om * tile_rows : (om + 1) * tile_rows] - average
        total = total + centred * centred
    spread = (total + pltpu.roll(total, tile_cols, 1)) * (1.0 / channels)
    scale = lax.rsqrt(spread + 1e-05)
    low = lanes_of((packed, width)) < tile_cols
    bin_ids = lax.broadcasted_iota(jnp.int32, (dw_ref.shape[0], width), 0)
    loss = jnp.zeros((1, width), jnp.float32)
    for first in range(0, tile_rows, 2):
        a, b = [
            (held[pl.ds(ii, packed, stride=tile_rows), :] - average[ii : ii + 1]) * scale[ii : ii + 1]
            for ii in (first, first + 1)
        ]
        normed = jnp.concatenate(
            [
                jnp.where(low, a, pltpu.roll(b, tile_cols, 1)),
                jnp.where(low, pltpu.roll(a, tile_cols, 1), b),
            ],
            0,
        ).astype(jnp.bfloat16)
        update = jnp.dot(ow_ref[...], normed, preferred_element_type=jnp.float32)
        at = slice(first * tile_cols, (first + 2) * tile_cols)
        pair_out = (x_ref[:, at] + gate_ref[:, at] * update).astype(jnp.bfloat16)
        out_ref[:, at] = pair_out
        logits = jnp.dot(dw_ref[...], pair_out, preferred_element_type=jnp.float32)
        log_total = jnp.log(jnp.sum(jnp.exp(logits), axis=0, keepdims=True))
        bins = bins_ref[first // 2 : first // 2 + 1]
        picked = jnp.sum(jnp.where(bin_ids == bins, logits, 0.0), axis=0, keepdims=True)
        loss = loss + masks_ref[first // 2 : first // 2 + 1] * (log_total - picked)
    last = masks_ref.shape[0] - 1
    loss = jnp.sum(loss * masks_ref[last : last + 1], axis=1, keepdims=True)
    loss_ref[...] = jnp.broadcast_to(loss, loss_ref.shape)


def turn_back_kernel(turned_ref, out_ref):
    tile_rows, tile_cols, channels = out_ref.shape
    for first in range(0, tile_rows, 2):
        block = turned_ref[:, first * tile_cols : (first + 2) * tile_cols].astype(jnp.float32).T
        out_ref[first : first + 2] = block.astype(jnp.bfloat16).reshape(2, tile_cols, channels)


def exchange(value, places, mask):
    return lax.ppermute(value, AXES, [(at, at ^ mask) for at in range(places)])


def call(kernel, outs, scratch=(), specs=None, out_specs=None, args=(), flops=0):
    return pl.pallas_call(
        kernel,
        out_shape=outs,
        in_specs=specs if specs is not None else [VMEM] * len(args),
        out_specs=out_specs if out_specs is not None else jax.tree.map(lambda _: VMEM, outs),
        scratch_shapes=list(scratch),
        compiler_params=PARAMS,
        cost_estimate=pl.CostEstimate(flops=flops, bytes_accessed=1 << 20, transcendentals=1 << 18),
    )(*args)


def by_kernels(
    pair_repr,
    distance_bins,
    chain_lengths,
    left_weight,
    left_gate_weight,
    right_weight,
    right_gate_weight,
    out_weight,
    out_gate_weight,
    dist_weight,
):
    tile_rows, tile_cols, channels = pair_repr.shape
    rows, cols = lax.axis_size("row"), lax.axis_size("col")
    places = rows * cols
    width = 2 * tile_cols
    spots = tile_rows * tile_cols
    size = channels // OWNERS // 2 * tile_rows
    bf16, f32 = jnp.bfloat16, jnp.float32
    struct = jax.ShapeDtypeStruct
    turned = pltpu.VMEM((2 * channels, channels), bf16)
    held = pltpu.VMEM((OWNERS * size, width), f32)
    over_x, over_core, over_z, over_half = 1, cols, 2 * cols, OWNERS * cols
    near = exchange(pair_repr, places, over_z)
    normed = call(
        norm_kernel, struct((spots, channels), bf16), args=(pair_repr,), flops=1 << 30
    )
    stay, move = call(
        right_kernel,
        [struct((2 * size, width), bf16)] * 2,
        [turned, held],
        args=(normed, right_weight, right_gate_weight),
        flops=4 * spots * channels * channels,
    )
    cross = exchange(move, places, over_half + over_z)
    far = exchange(stay, places, over_half)
    block = struct((2 * size, width), bf16)
    own, core, masks = call(
        left_kernel,
        [block, block, struct((3 * tile_rows // 2, width), f32)],
        [turned, pltpu.VMEM((channels, channels), bf16), pltpu.VMEM((2 * size, width), f32)],
        [SMEM] + [VMEM] * 4,
        args=(chain_lengths, normed, left_weight, left_gate_weight, stay),
        flops=2 * spots * channels * channels,
    )
    near, near_over = call(
        near_kernel,
        [block, block],
        [
            pltpu.VMEM((4 * channels, channels), bf16),
            pltpu.VMEM((2 * channels, channels), bf16),
            pltpu.VMEM((2 * size, width), f32),
            pltpu.VMEM((2 * size, width), f32),
        ],
        args=(masks, near, left_weight, left_gate_weight, right_weight, right_gate_weight),
        flops=4 * spots * channels * channels,
    )
    near_over = exchange(near_over, places, over_core)
    core = exchange(core, places, over_core)
    both_over = call(
        pack_kernel,
        block,
        specs=[VMEM, VMEM, pl.BlockSpec(memory_space=pl.ANY)],
        args=(far, cross, near_over),
    )
    both_over = exchange(both_over, places, over_core)
    parts = call(
        tri_kernel,
        [struct((2 * size, width), bf16)] * OWNERS,
        [pltpu.VMEM((size // tile_rows, rows * tile_rows, width), bf16)],
        args=(masks, own, core, near, near_over, far, cross, both_over),
        flops=8 * size * 2 * tile_rows * 2 * width,
    )
    parts = [
        exchange(parts[d], places, d // 2 * over_z + d % 2 * over_x) if d else parts[0] for d in DIAGONAL_FIRST
    ]
    parts += [exchange(value, places, over_core) for value in parts]
    gate, x_turned, out_turned, dist_turned = call(
        gate_kernel,
        [
            struct((channels, spots), f32),
            struct((channels, spots), f32),
            struct((channels, channels), bf16),
            struct(dist_weight.shape[::-1], bf16),
        ],
        args=(pair_repr, normed, out_gate_weight, out_weight, dist_weight),
        flops=2 * spots * channels * channels,
    )
    pair_out, loss = call(
        finish_kernel,
        [struct((channels, spots), bf16), struct((8, 128), f32)],
        [held],
        args=(
            masks,
            x_turned,
            gate,
            distance_bins.reshape(tile_rows // 2, width),
            out_turned,
            dist_turned,
            *parts,
        ),
        flops=6 * spots * channels * channels,
    )
    pair_out = call(turn_back_kernel, struct(pair_repr.shape, bf16), args=(pair_out,), flops=1 << 26)
    loss = loss + exchange(loss, places, over_core)
    diagonal, beside, near_loss = [
        exchange(loss, places, mask) for mask in (over_z + over_x, over_x, over_z)
    ]
    loss = (diagonal + near_loss) + (beside + loss)
    loss = loss + exchange(loss, places, over_half)
    return (pair_out, loss[0, :1])


def by_all_to_all(
    pair_repr,
    distance_bins,
    chain_lengths,
    left_weight,
    left_gate_weight,
    right_weight,
    right_gate_weight,
    out_weight,
    out_gate_weight,
    dist_weight,
):
    tile_rows, tile_cols, channels = pair_repr.shape
    rows, cols = lax.axis_size("row"), lax.axis_size("col")
    peers = rows * cols
    share = channels // peers
    residues = tile_rows * rows
    spots = tile_rows * tile_cols
    live_count = residues - chain_lengths[chain_lengths.shape[0] - 1]
    row_place = lax.axis_index("row") * tile_rows + jnp.arange(tile_rows, dtype=jnp.int32)
    col_place = lax.axis_index("col") * tile_cols + jnp.arange(tile_cols, dtype=jnp.int32)
    live_rows = (row_place < live_count).astype(jnp.float32)
    live_cols = (col_place < live_count).astype(jnp.float32)
    flat_mask = (live_rows[:, None] * live_cols[None, :]).reshape(-1)
    normed = layer_norm(pair_repr.astype(jnp.float32), -1).astype(jnp.bfloat16)
    normed = normed.reshape(spots, channels)

    def project_turned(weight):
        return lax.dot_general(
            weight, normed, (((0,), (1,)), ((), ())), preferred_element_type=jnp.float32
        )

    def gated(gate_weight, weight):
        values = jax.nn.sigmoid(project_turned(gate_weight)) * project_turned(weight)
        return (values * flat_mask[None, :]).astype(jnp.bfloat16)

    left = gated(left_gate_weight, left_weight).reshape(peers, share, tile_rows, tile_cols)
    right = gated(right_gate_weight, right_weight).reshape(peers, share, tile_rows, tile_cols)
    both = jnp.concatenate([left, right], axis=3).reshape(peers, share * tile_rows, 2 * tile_cols)
    owned = lax.all_to_all(both, AXES, split_axis=0, concat_axis=0, tiled=True)
    owned = owned.reshape(rows, cols, share, tile_rows, 2, tile_cols)
    owned = owned.transpose(4, 2, 0, 3, 1, 5).reshape(2, share, residues, residues)
    tri = jnp.einsum(
        "cik,cjk->cij", owned[0], owned[1], preferred_element_type=jnp.float32
    ).astype(jnp.bfloat16)
    tri = tri.reshape(share, rows, tile_rows, cols, tile_cols).transpose(1, 3, 0, 2, 4)
    tri = tri.reshape(peers, share, spots)
    tri = lax.all_to_all(tri, AXES, split_axis=0, concat_axis=0, tiled=True)
    tri = tri.reshape(channels, spots).astype(jnp.float32)
    tri_normed = layer_norm(tri, 0).astype(jnp.bfloat16)
    out_gate = jax.nn.sigmoid(jnp.dot(normed, out_gate_weight, preferred_element_type=jnp.float32))
    update = out_gate * tn_dot(tri_normed, out_weight)
    pair_out = (pair_repr.astype(jnp.float32).reshape(spots, channels) + update).astype(
        jnp.bfloat16
    )
    logits = jnp.dot(pair_out, dist_weight, preferred_element_type=jnp.float32)
    log_total = jnp.log(jnp.sum(jnp.exp(logits), axis=-1))
    bin_ids = jnp.arange(logits.shape[1], dtype=jnp.int32)
    picked = jnp.sum(
        jnp.where(bin_ids[None, :] == distance_bins.reshape(-1, 1), logits, 0.0), axis=-1
    )
    loss_sum = jnp.sum(flat_mask * (log_total - picked))
    sums = lax.all_to_all(
        jnp.full((peers, 1, 128), loss_sum), AXES, split_axis=0, concat_axis=0, tiled=True
    )
    pair_count = (live_count * live_count).astype(jnp.float32)
    loss_value = (jnp.sum(sums[:, 0, 0]) / pair_count).reshape(1)
    return (pair_out.reshape(pair_repr.shape), loss_value)


def on_device(pair_repr, *others):
    tile_rows, tile_cols, channels = pair_repr.shape
    rows, cols = lax.axis_size("row"), lax.axis_size("col")
    fits = (
        rows == 2 * OWNERS
        and cols == 2
        and tile_rows * rows == tile_cols * cols
        and 2 * tile_cols == 128
        and tile_rows == 16
        and channels == 32 * OWNERS
    )
    return (by_kernels if fits else by_all_to_all)(pair_repr, *others)


def solution(mesh):
    in_specs = (
        P(("groups", "row"), "col", None),
        P(("groups", "row"), "col"),
        P("groups"),
        P(),
        P(),
        P(),
        P(),
        P(),
        P(),
        P(),
    )
    out_specs = (P(("groups", "row"), "col", None), P("groups"))
    return jax.shard_map(
        on_device, mesh=mesh, in_specs=in_specs, out_specs=out_specs, check_vma=False
    )
```

```python
import jax
import jax.numpy as jnp
from jax import lax
from jax.experimental import pallas as pl
from jax.experimental.pallas import tpu as pltpu
from jax.sharding import PartitionSpec as P

AXES = ("row", "col")
OWNERS = 4
DIAGONAL_FIRST = (0, 3, 1, 2)
VMEM = pl.BlockSpec(memory_space=pltpu.VMEM)
SMEM = pl.BlockSpec(memory_space=pltpu.SMEM)
PARAMS = pltpu.CompilerParams(vmem_limit_bytes=24 * 1024 * 1024)


def layer_norm(values, axis):
    average = jnp.mean(values, axis=axis, keepdims=True)
    centred = values - average
    spread = jnp.mean(centred * centred, axis=axis, keepdims=True)
    return centred * lax.rsqrt(spread + 1e-05)


def sigmoid(values):
    return 0.5 * jnp.tanh(0.5 * values) + 0.5


def nt_dot(a, b):
    return lax.dot_general(a, b, (((1,), (1,)), ((), ())), preferred_element_type=jnp.float32)


def tn_dot(a, b):
    return lax.dot_general(a, b, (((0,), (0,)), ((), ())), preferred_element_type=jnp.float32)


def lanes_of(shape):
    return lax.broadcasted_iota(jnp.int32, shape, 1)


def make_masks(lens_ref, tile_rows, tile_cols):
    live = tile_rows * lax.axis_size("row") - lens_ref[lens_ref.shape[0] - 1]
    lane = lanes_of((1, 2 * tile_cols))
    upper = (lane >= tile_cols).astype(jnp.int32)
    place = lane - tile_cols * upper
    row, col = lax.axis_index("row"), lax.axis_index("col")
    keeps = [(place + (col ^ dx) * tile_cols < live).astype(jnp.float32) for dx in (0, 1)]
    pairs = [
        ((row ^ d) * tile_rows + first + upper < live).astype(jnp.float32) * keeps[0]
        for d in (0, OWNERS // 2)
        for first in range(0, tile_rows, 2)
    ]
    count = jnp.full(lane.shape, live * live, jnp.int32).astype(jnp.float32)
    return pairs, keeps, 1.0 / count


def turn(w_refs, turned):
    channels = w_refs[0].shape[0]
    share = channels // OWNERS
    half = share // 2
    for at, w_ref in enumerate(w_refs):
        w = w_ref[...].astype(jnp.float32).T
        blocks = [
            w[o * share + g * half : o * share + (g + 1) * half] for g in (0, 1) for o in range(OWNERS)
        ]
        turned[at * channels : (at + 1) * channels] = jnp.concatenate(blocks, 0).astype(jnp.bfloat16)


def store_rows(held, first, value, tile_cols):
    packed = value.shape[0] // 2
    stride = held.shape[0] // packed
    a, b = value[:packed], value[packed:]
    low = lanes_of(a.shape) < tile_cols
    held[pl.ds(first, packed, stride=stride), :] = jnp.where(low, a, pltpu.roll(b, tile_cols, 1))
    held[pl.ds(first + 1, packed, stride=stride), :] = jnp.where(low, pltpu.roll(a, tile_cols, 1), b)


def chip_rows(turned, mine):
    size = mine.shape[0] // (turned.shape[0] // mine.shape[1]) // 2
    pair = owner_place() // 2
    for at in range(mine.shape[0] // size):
        start = pl.multiple_of(at * (mine.shape[1] // 2) + pair * size, size)
        mine[at * size : (at + 1) * size] = turned[pl.ds(start, size), :]


def owner_place():
    return lax.axis_index("row") % OWNERS


def owner_block(held, d, size):
    at = pl.multiple_of((owner_place() ^ d) * size, size)
    return held[pl.ds(at, size)].astype(jnp.bfloat16)


def core_block(held, d, size):
    at = pl.multiple_of((owner_place() % 2 ^ d) * size, size)
    return held[pl.ds(at, size)].astype(jnp.bfloat16)


def norm_kernel(x_ref, normed_ref):
    x = x_ref[...].astype(jnp.float32).reshape(normed_ref.shape)
    normed_ref[...] = layer_norm(x, -1).astype(jnp.bfloat16)


def right_kernel(normed_ref, w_ref, g_ref, stay_ref, move_ref, turned, held):
    channels = normed_ref.shape[1]
    width = held.shape[1]
    turn((w_ref, g_ref), turned)
    for at in range(normed_ref.shape[0] // width):
        flat = nt_dot(turned[...], normed_ref[at * width : (at + 1) * width])
        store_rows(held, 2 * at, sigmoid(flat[channels:]) * flat[:channels], width // 2)
    size = stay_ref.shape[0] // 2
    for d, ref in enumerate((stay_ref, stay_ref, move_ref, move_ref)):
        ref[d % 2 * size : (d % 2 + 1) * size] = owner_block(held, d, size)


def left_kernel(lens_ref, normed_ref, w_ref, g_ref, stay_ref, own_ref, core_ref, masks_ref, *refs):
    turned, mine, held = refs
    width = held.shape[1]
    half = mine.shape[0] // 2
    pairs, keeps, share = make_masks(lens_ref, 2 * normed_ref.shape[0] // width, width // 2)
    masks_ref[...] = jnp.concatenate(
        pairs + keeps + [share] * (masks_ref.shape[0] - len(pairs) - len(keeps)), 0
    )
    turn((w_ref, g_ref), turned)
    chip_rows(turned, mine)
    for at in range(normed_ref.shape[0] // width):
        flat = nt_dot(mine[...], normed_ref[at * width : (at + 1) * width])
        store_rows(held, 2 * at, sigmoid(flat[half:]) * flat[:half] * pairs[at], width // 2)
    size = stay_ref.shape[0] // 2
    for d, ref in enumerate((own_ref, core_ref)):
        ref[:size] = core_block(held, d, size)
        ref[size:] = stay_ref[d * size : (d + 1) * size]


def near_kernel(masks_ref, x_ref, lw_ref, lg_ref, rw_ref, rg_ref, near_ref, over_ref, *refs):
    turned, mine, held_left, held_right = refs
    tile_rows, tile_cols, channels = x_ref.shape
    share = mine.shape[0] // 4
    turn((lw_ref, lg_ref, rw_ref, rg_ref), turned)
    chip_rows(turned, mine)
    for first in range(0, tile_rows, 2):
        x = x_ref[first : first + 2].astype(jnp.float32).reshape(2 * tile_cols, channels)
        flat = nt_dot(mine[...], layer_norm(x, -1).astype(jnp.bfloat16))
        lv, lg, rv, rg = [flat[at * share : (at + 1) * share] for at in range(4)]
        line = (tile_rows + first) // 2
        store_rows(held_left, first, sigmoid(lg) * lv * masks_ref[line : line + 1], tile_cols)
        store_rows(held_right, first, sigmoid(rg) * rv, tile_cols)
    size = near_ref.shape[0] // 2
    for d, ref in enumerate((near_ref, over_ref)):
        ref[:size] = core_block(held_left, d, size)
        ref[size:] = core_block(held_right, d, size)


def pack_kernel(far_ref, cross_ref, ready_ref, out_ref):
    del ready_ref
    size = out_ref.shape[0] // 2
    out_ref[:size] = far_ref[size:]
    out_ref[size:] = cross_ref[size:]


def gate_kernel(x_ref, normed_ref, gw_ref, ow_ref, dw_ref, gate_ref, x_turned_ref, ow_turned, dw_turned):
    tile_rows, tile_cols, channels = x_ref.shape
    share = channels // OWNERS
    half = share // 2
    blocks = [
        ow_ref[o * share + g * half : o * share + (g + 1) * half].astype(jnp.float32)
        for g in (0, 1)
        for o in range(OWNERS)
    ]
    ow_turned[...] = jnp.concatenate(blocks, 0).T.astype(jnp.bfloat16)
    dw_turned[...] = dw_ref[...].astype(jnp.float32).T.astype(jnp.bfloat16)
    gate_turned = gw_ref[...].astype(jnp.float32).T.astype(jnp.bfloat16)
    for first in range(0, tile_rows, 2):
        at = slice(first * tile_cols, (first + 2) * tile_cols)
        gate_ref[:, at] = sigmoid(nt_dot(gate_turned, normed_ref[at]))
        x = x_ref[first : first + 2].astype(jnp.float32).reshape(2 * tile_cols, channels)
        x_turned_ref[:, at] = x.T


def tri_kernel(masks_ref, own, core, near, near_over, far, cross, both_over, *refs):
    outs, rights = refs[:-1], refs[-1]
    half, _, width = rights.shape
    size = own.shape[0] // 2
    tile_rows = size // half
    side = OWNERS * tile_rows
    me, col = lax.axis_index("row"), lax.axis_index("col")
    lefts = (own, core, near, near_over)
    pieces = (
        (0, own, size),
        (1, core, size),
        (2, near, size),
        (3, near_over, size),
        (4, far, 0),
        (5, both_over, 0),
        (6, cross, 0),
        (7, both_over, size),
    )
    for away, ref, start in pieces:
        at = pl.multiple_of((me ^ away) * tile_rows, tile_rows)
        for m in range(half):
            rights[m, pl.ds(at, tile_rows), :] = ref[
                start + m * tile_rows : start + (m + 1) * tile_rows
            ]
    low = lanes_of((side, width)) < width // 2
    first = masks_ref.shape[0] - tile_rows // 2
    keep = jnp.concatenate([masks_ref[first : first + 1], masks_ref[first + 1 : first + 2]], 1)
    for m in range(half):
        left = jnp.concatenate(
            [ref[m * tile_rows : (m + 1) * tile_rows] for ref in lefts], 0
        )
        pieces = []
        for dx in (0, 1):
            block = rights[m, pl.ds(pl.multiple_of((col ^ dx) * side, side), side), :]
            block = block.astype(jnp.float32)
            pieces += [jnp.where(low, block, 0.0), jnp.where(low, 0.0, block)]
        right = jnp.concatenate(pieces, 0).astype(jnp.bfloat16)
        product = (nt_dot(left, right) * keep).astype(jnp.bfloat16)
        for d in range(OWNERS):
            for dx in (0, 1):
                at = d % 2 * size + m * tile_rows
                outs[d // 2 * 2 + dx][at : at + tile_rows] = product[
                    d * tile_rows : (d + 1) * tile_rows, dx * width : (dx + 1) * width
                ]


def finish_kernel(masks_ref, x_ref, gate_ref, bins_ref, ow_ref, dw_ref, *refs):
    parts, overs = [
        [refs[first + DIAGONAL_FIRST.index(d)] for d in range(OWNERS)] for first in (0, OWNERS)
    ]
    out_ref, loss_ref, held = refs[2 * OWNERS :]
    channels = x_ref.shape[0]
    size, width = parts[0].shape[0] // 2, parts[0].shape[1]
    half = channels // 2 // OWNERS
    tile_rows, tile_cols = size // half, width // 2
    packed = OWNERS * half
    owner = owner_place()
    total = jnp.zeros((tile_rows, width), jnp.float32)
    for d in range(OWNERS):
        refs, at = ((parts, 0), (overs, size))[d % 2]
        a, b = [refs[d // 2 * 2 + dx][at : at + size].astype(jnp.float32) for dx in (0, 1)]
        block = a + b
        held[pl.ds(pl.multiple_of((owner ^ d) * size, size), size), :] = block
        total = total + jnp.sum(block.reshape(half, tile_rows, width), 0)
    average = (total + pltpu.roll(total, tile_cols, 1)) * (1.0 / channels)
    total = jnp.zeros((tile_rows, width), jnp.float32)
    for om in range(packed):
        centred = held[om * tile_rows : (om + 1) * tile_rows] - average
        total = total + centred * centred
    spread = (total + pltpu.roll(total, tile_cols, 1)) * (1.0 / channels)
    scale = lax.rsqrt(spread + 1e-05)
    low = lanes_of((packed, width)) < tile_cols
    bin_ids = lax.broadcasted_iota(jnp.int32, (dw_ref.shape[0], width), 0)
    loss = jnp.zeros((1, width), jnp.float32)
    for first in range(0, tile_rows, 2):
        a, b = [
            (held[pl.ds(ii, packed, stride=tile_rows), :] - average[ii : ii + 1]) * scale[ii : ii + 1]
            for ii in (first, first + 1)
        ]
        normed = jnp.concatenate(
            [
                jnp.where(low, a, pltpu.roll(b, tile_cols, 1)),
                jnp.where(low, pltpu.roll(a, tile_cols, 1), b),
            ],
            0,
        ).astype(jnp.bfloat16)
        update = jnp.dot(ow_ref[...], normed, preferred_element_type=jnp.float32)
        at = slice(first * tile_cols, (first + 2) * tile_cols)
        pair_out = (x_ref[:, at] + gate_ref[:, at] * update).astype(jnp.bfloat16)
        out_ref[:, at] = pair_out
        logits = jnp.dot(dw_ref[...], pair_out, preferred_element_type=jnp.float32)
        log_total = jnp.log(jnp.sum(jnp.exp(logits), axis=0, keepdims=True))
        bins = bins_ref[first // 2 : first // 2 + 1]
        picked = jnp.sum(jnp.where(bin_ids == bins, logits, 0.0), axis=0, keepdims=True)
        loss = loss + masks_ref[first // 2 : first // 2 + 1] * (log_total - picked)
    last = masks_ref.shape[0] - 1
    loss = jnp.sum(loss * masks_ref[last : last + 1], axis=1, keepdims=True)
    loss_ref[...] = jnp.broadcast_to(loss, loss_ref.shape)


def turn_back_kernel(turned_ref, out_ref):
    tile_rows, tile_cols, channels = out_ref.shape
    for first in range(0, tile_rows, 2):
        block = turned_ref[:, first * tile_cols : (first + 2) * tile_cols].astype(jnp.float32).T
        out_ref[first : first + 2] = block.astype(jnp.bfloat16).reshape(2, tile_cols, channels)


def exchange(value, places, mask):
    return lax.ppermute(value, AXES, [(at, at ^ mask) for at in range(places)])


def call(kernel, outs, scratch=(), specs=None, out_specs=None, args=(), flops=0):
    return pl.pallas_call(
        kernel,
        out_shape=outs,
        in_specs=specs if specs is not None else [VMEM] * len(args),
        out_specs=out_specs if out_specs is not None else jax.tree.map(lambda _: VMEM, outs),
        scratch_shapes=list(scratch),
        compiler_params=PARAMS,
        cost_estimate=pl.CostEstimate(flops=flops, bytes_accessed=1 << 20, transcendentals=1 << 18),
    )(*args)


def by_kernels(
    pair_repr,
    distance_bins,
    chain_lengths,
    left_weight,
    left_gate_weight,
    right_weight,
    right_gate_weight,
    out_weight,
    out_gate_weight,
    dist_weight,
):
    tile_rows, tile_cols, channels = pair_repr.shape
    rows, cols = lax.axis_size("row"), lax.axis_size("col")
    places = rows * cols
    width = 2 * tile_cols
    spots = tile_rows * tile_cols
    size = channels // OWNERS // 2 * tile_rows
    bf16, f32 = jnp.bfloat16, jnp.float32
    struct = jax.ShapeDtypeStruct
    turned = pltpu.VMEM((2 * channels, channels), bf16)
    held = pltpu.VMEM((OWNERS * size, width), f32)
    over_x, over_core, over_z, over_half = 1, cols, 2 * cols, OWNERS * cols
    near = exchange(pair_repr, places, over_z)
    normed = call(
        norm_kernel, struct((spots, channels), bf16), args=(pair_repr,), flops=1 << 30
    )
    stay, move = call(
        right_kernel,
        [struct((2 * size, width), bf16)] * 2,
        [turned, held],
        args=(normed, right_weight, right_gate_weight),
        flops=4 * spots * channels * channels,
    )
    cross = exchange(move, places, over_half + over_z)
    far = exchange(stay, places, over_half)
    block = struct((2 * size, width), bf16)
    own, core, masks = call(
        left_kernel,
        [block, block, struct((3 * tile_rows // 2, width), f32)],
        [turned, pltpu.VMEM((channels, channels), bf16), pltpu.VMEM((2 * size, width), f32)],
        [SMEM] + [VMEM] * 4,
        args=(chain_lengths, normed, left_weight, left_gate_weight, stay),
        flops=2 * spots * channels * channels,
    )
    near, near_over = call(
        near_kernel,
        [block, block],
        [
            pltpu.VMEM((4 * channels, channels), bf16),
            pltpu.VMEM((2 * channels, channels), bf16),
            pltpu.VMEM((2 * size, width), f32),
            pltpu.VMEM((2 * size, width), f32),
        ],
        args=(masks, near, left_weight, left_gate_weight, right_weight, right_gate_weight),
        flops=4 * spots * channels * channels,
    )
    near_over = exchange(near_over, places, over_core)
    core = exchange(core, places, over_core)
    both_over = call(
        pack_kernel,
        block,
        specs=[VMEM, VMEM, pl.BlockSpec(memory_space=pl.ANY)],
        args=(far, cross, near_over),
    )
    both_over = exchange(both_over, places, over_core)
    parts = call(
        tri_kernel,
        [struct((2 * size, width), bf16)] * OWNERS,
        [pltpu.VMEM((size // tile_rows, rows * tile_rows, width), bf16)],
        args=(masks, own, core, near, near_over, far, cross, both_over),
        flops=8 * size * 2 * tile_rows * 2 * width,
    )
    parts = [
        exchange(parts[d], places, d // 2 * over_z + d % 2 * over_x) if d else parts[0] for d in DIAGONAL_FIRST
    ]
    parts += [exchange(value, places, over_core) for value in parts]
    gate, x_turned, out_turned, dist_turned = call(
        gate_kernel,
        [
            struct((channels, spots), f32),
            struct((channels, spots), f32),
            struct((channels, channels), bf16),
            struct(dist_weight.shape[::-1], bf16),
        ],
        args=(pair_repr, normed, out_gate_weight, out_weight, dist_weight),
        flops=2 * spots * channels * channels,
    )
    pair_out, loss = call(
        finish_kernel,
        [struct((channels, spots), bf16), struct((8, 128), f32)],
        [held],
        args=(
            masks,
            x_turned,
            gate,
            distance_bins.reshape(tile_rows // 2, width),
            out_turned,
            dist_turned,
            *parts,
        ),
        flops=6 * spots * channels * channels,
    )
    pair_out = call(turn_back_kernel, struct(pair_repr.shape, bf16), args=(pair_out,), flops=1 << 26)
    diagonal, beside, near_loss = [
        exchange(loss, places, mask) for mask in (over_z + over_x, over_x, over_z)
    ]
    loss = (diagonal + near_loss) + (beside + loss)
    half, half_over, sibling = [
        exchange(loss, places, mask) for mask in (over_half, over_half + over_core, over_core)
    ]
    loss = (half + half_over) + (sibling + loss)
    return (pair_out, loss[0, :1])


def by_all_to_all(
    pair_repr,
    distance_bins,
    chain_lengths,
    left_weight,
    left_gate_weight,
    right_weight,
    right_gate_weight,
    out_weight,
    out_gate_weight,
    dist_weight,
):
    tile_rows, tile_cols, channels = pair_repr.shape
    rows, cols = lax.axis_size("row"), lax.axis_size("col")
    peers = rows * cols
    share = channels // peers
    residues = tile_rows * rows
    spots = tile_rows * tile_cols
    live_count = residues - chain_lengths[chain_lengths.shape[0] - 1]
    row_place = lax.axis_index("row") * tile_rows + jnp.arange(tile_rows, dtype=jnp.int32)
    col_place = lax.axis_index("col") * tile_cols + jnp.arange(tile_cols, dtype=jnp.int32)
    live_rows = (row_place < live_count).astype(jnp.float32)
    live_cols = (col_place < live_count).astype(jnp.float32)
    flat_mask = (live_rows[:, None] * live_cols[None, :]).reshape(-1)
    normed = layer_norm(pair_repr.astype(jnp.float32), -1).astype(jnp.bfloat16)
    normed = normed.reshape(spots, channels)

    def project_turned(weight):
        return lax.dot_general(
            weight, normed, (((0,), (1,)), ((), ())), preferred_element_type=jnp.float32
        )

    def gated(gate_weight, weight):
        values = jax.nn.sigmoid(project_turned(gate_weight)) * project_turned(weight)
        return (values * flat_mask[None, :]).astype(jnp.bfloat16)

    left = gated(left_gate_weight, left_weight).reshape(peers, share, tile_rows, tile_cols)
    right = gated(right_gate_weight, right_weight).reshape(peers, share, tile_rows, tile_cols)
    both = jnp.concatenate([left, right], axis=3).reshape(peers, share * tile_rows, 2 * tile_cols)
    owned = lax.all_to_all(both, AXES, split_axis=0, concat_axis=0, tiled=True)
    owned = owned.reshape(rows, cols, share, tile_rows, 2, tile_cols)
    owned = owned.transpose(4, 2, 0, 3, 1, 5).reshape(2, share, residues, residues)
    tri = jnp.einsum(
        "cik,cjk->cij", owned[0], owned[1], preferred_element_type=jnp.float32
    ).astype(jnp.bfloat16)
    tri = tri.reshape(share, rows, tile_rows, cols, tile_cols).transpose(1, 3, 0, 2, 4)
    tri = tri.reshape(peers, share, spots)
    tri = lax.all_to_all(tri, AXES, split_axis=0, concat_axis=0, tiled=True)
    tri = tri.reshape(channels, spots).astype(jnp.float32)
    tri_normed = layer_norm(tri, 0).astype(jnp.bfloat16)
    out_gate = jax.nn.sigmoid(jnp.dot(normed, out_gate_weight, preferred_element_type=jnp.float32))
    update = out_gate * tn_dot(tri_normed, out_weight)
    pair_out = (pair_repr.astype(jnp.float32).reshape(spots, channels) + update).astype(
        jnp.bfloat16
    )
    logits = jnp.dot(pair_out, dist_weight, preferred_element_type=jnp.float32)
    log_total = jnp.log(jnp.sum(jnp.exp(logits), axis=-1))
    bin_ids = jnp.arange(logits.shape[1], dtype=jnp.int32)
    picked = jnp.sum(
        jnp.where(bin_ids[None, :] == distance_bins.reshape(-1, 1), logits, 0.0), axis=-1
    )
    loss_sum = jnp.sum(flat_mask * (log_total - picked))
    sums = lax.all_to_all(
        jnp.full((peers, 1, 128), loss_sum), AXES, split_axis=0, concat_axis=0, tiled=True
    )
    pair_count = (live_count * live_count).astype(jnp.float32)
    loss_value = (jnp.sum(sums[:, 0, 0]) / pair_count).reshape(1)
    return (pair_out.reshape(pair_repr.shape), loss_value)


def on_device(pair_repr, *others):
    tile_rows, tile_cols, channels = pair_repr.shape
    rows, cols = lax.axis_size("row"), lax.axis_size("col")
    fits = (
        rows == 2 * OWNERS
        and cols == 2
        and tile_rows * rows == tile_cols * cols
        and 2 * tile_cols == 128
        and tile_rows == 16
        and channels == 32 * OWNERS
    )
    return (by_kernels if fits else by_all_to_all)(pair_repr, *others)


def solution(mesh):
    in_specs = (
        P(("groups", "row"), "col", None),
        P(("groups", "row"), "col"),
        P("groups"),
        P(),
        P(),
        P(),
        P(),
        P(),
        P(),
        P(),
    )
    out_specs = (P(("groups", "row"), "col", None), P("groups"))
    return jax.shard_map(
        on_device, mesh=mesh, in_specs=in_specs, out_specs=out_specs, check_vma=False
    )
```

```python
import jax
import jax.numpy as jnp
from jax import lax
from jax.experimental import pallas as pl
from jax.experimental.pallas import tpu as pltpu
from jax.sharding import PartitionSpec as P

AXES = ("row", "col")
OWNERS = 4
DIAGONAL_FIRST = (0, 3, 1, 2)
VMEM = pl.BlockSpec(memory_space=pltpu.VMEM)
SMEM = pl.BlockSpec(memory_space=pltpu.SMEM)
PARAMS = pltpu.CompilerParams(vmem_limit_bytes=24 * 1024 * 1024)


def layer_norm(values, axis):
    average = jnp.mean(values, axis=axis, keepdims=True)
    centred = values - average
    spread = jnp.mean(centred * centred, axis=axis, keepdims=True)
    return centred * lax.rsqrt(spread + 1e-05)


def sigmoid(values):
    return 0.5 * jnp.tanh(0.5 * values) + 0.5


def nt_dot(a, b):
    return lax.dot_general(a, b, (((1,), (1,)), ((), ())), preferred_element_type=jnp.float32)


def tn_dot(a, b):
    return lax.dot_general(a, b, (((0,), (0,)), ((), ())), preferred_element_type=jnp.float32)


def lanes_of(shape):
    return lax.broadcasted_iota(jnp.int32, shape, 1)


def make_masks(lens_ref, tile_rows, tile_cols):
    live = tile_rows * lax.axis_size("row") - lens_ref[lens_ref.shape[0] - 1]
    lane = lanes_of((1, 2 * tile_cols))
    upper = (lane >= tile_cols).astype(jnp.int32)
    place = lane - tile_cols * upper
    row, col = lax.axis_index("row"), lax.axis_index("col")
    keeps = [(place + (col ^ dx) * tile_cols < live).astype(jnp.float32) for dx in (0, 1)]
    pairs = [
        ((row ^ d) * tile_rows + first + upper < live).astype(jnp.float32) * keeps[0]
        for d in (0, OWNERS // 2)
        for first in range(0, tile_rows, 2)
    ]
    count = jnp.full(lane.shape, live * live, jnp.int32).astype(jnp.float32)
    return pairs, keeps, 1.0 / count


def turn(w_refs, turned):
    channels = w_refs[0].shape[0]
    share = channels // OWNERS
    half = share // 2
    for at, w_ref in enumerate(w_refs):
        w = w_ref[...].astype(jnp.float32).T
        blocks = [
            w[o * share + g * half : o * share + (g + 1) * half] for g in (0, 1) for o in range(OWNERS)
        ]
        turned[at * channels : (at + 1) * channels] = jnp.concatenate(blocks, 0).astype(jnp.bfloat16)


def store_rows(held, first, value, tile_cols):
    packed = value.shape[0] // 2
    stride = held.shape[0] // packed
    a, b = value[:packed], value[packed:]
    low = lanes_of(a.shape) < tile_cols
    held[pl.ds(first, packed, stride=stride), :] = jnp.where(low, a, pltpu.roll(b, tile_cols, 1))
    held[pl.ds(first + 1, packed, stride=stride), :] = jnp.where(low, pltpu.roll(a, tile_cols, 1), b)


def chip_rows(turned, mine):
    size = mine.shape[0] // (turned.shape[0] // mine.shape[1]) // 2
    pair = owner_place() // 2
    for at in range(mine.shape[0] // size):
        start = pl.multiple_of(at * (mine.shape[1] // 2) + pair * size, size)
        mine[at * size : (at + 1) * size] = turned[pl.ds(start, size), :]


def owner_place():
    return lax.axis_index("row") % OWNERS


def owner_block(held, d, size):
    at = pl.multiple_of((owner_place() ^ d) * size, size)
    return held[pl.ds(at, size)].astype(jnp.bfloat16)


def core_block(held, d, size):
    at = pl.multiple_of((owner_place() % 2 ^ d) * size, size)
    return held[pl.ds(at, size)].astype(jnp.bfloat16)


def norm_kernel(x_ref, normed_ref):
    x = x_ref[...].astype(jnp.float32).reshape(normed_ref.shape)
    normed_ref[...] = layer_norm(x, -1).astype(jnp.bfloat16)


def right_kernel(normed_ref, w_ref, g_ref, stay_ref, move_ref, turned, held):
    channels = normed_ref.shape[1]
    width = held.shape[1]
    turn((w_ref, g_ref), turned)
    for at in range(normed_ref.shape[0] // width):
        flat = nt_dot(turned[...], normed_ref[at * width : (at + 1) * width])
        store_rows(held, 2 * at, sigmoid(flat[channels:]) * flat[:channels], width // 2)
    size = stay_ref.shape[0] // 2
    for d, ref in enumerate((stay_ref, stay_ref, move_ref, move_ref)):
        ref[d % 2 * size : (d % 2 + 1) * size] = owner_block(held, d, size)


def left_kernel(lens_ref, normed_ref, w_ref, g_ref, stay_ref, own_ref, core_ref, masks_ref, *refs):
    turned, mine, held = refs
    width = held.shape[1]
    half = mine.shape[0] // 2
    pairs, keeps, share = make_masks(lens_ref, 2 * normed_ref.shape[0] // width, width // 2)
    masks_ref[...] = jnp.concatenate(
        pairs + keeps + [share] * (masks_ref.shape[0] - len(pairs) - len(keeps)), 0
    )
    turn((w_ref, g_ref), turned)
    chip_rows(turned, mine)
    for at in range(normed_ref.shape[0] // width):
        flat = nt_dot(mine[...], normed_ref[at * width : (at + 1) * width])
        store_rows(held, 2 * at, sigmoid(flat[half:]) * flat[:half] * pairs[at], width // 2)
    size = stay_ref.shape[0] // 2
    for d, ref in enumerate((own_ref, core_ref)):
        ref[:size] = core_block(held, d, size)
        ref[size:] = stay_ref[d * size : (d + 1) * size]


def near_kernel(masks_ref, x_ref, lw_ref, lg_ref, rw_ref, rg_ref, near_ref, over_ref, *refs):
    turned, mine, held_left, held_right = refs
    tile_rows, tile_cols, channels = x_ref.shape
    share = mine.shape[0] // 4
    turn((lw_ref, lg_ref, rw_ref, rg_ref), turned)
    chip_rows(turned, mine)
    for first in range(0, tile_rows, 2):
        x = x_ref[first : first + 2].astype(jnp.float32).reshape(2 * tile_cols, channels)
        flat = nt_dot(mine[...], layer_norm(x, -1).astype(jnp.bfloat16))
        lv, lg, rv, rg = [flat[at * share : (at + 1) * share] for at in range(4)]
        line = (tile_rows + first) // 2
        store_rows(held_left, first, sigmoid(lg) * lv * masks_ref[line : line + 1], tile_cols)
        store_rows(held_right, first, sigmoid(rg) * rv, tile_cols)
    size = near_ref.shape[0] // 2
    for d, ref in enumerate((near_ref, over_ref)):
        ref[:size] = core_block(held_left, d, size)
        ref[size:] = core_block(held_right, d, size)


def pack_kernel(far_ref, cross_ref, ready_ref, out_ref):
    del ready_ref
    size = out_ref.shape[0] // 2
    out_ref[:size] = far_ref[size:]
    out_ref[size:] = cross_ref[size:]


def gate_kernel(x_ref, normed_ref, gw_ref, ow_ref, dw_ref, gate_ref, x_turned_ref, ow_turned, dw_turned):
    tile_rows, tile_cols, channels = x_ref.shape
    share = channels // OWNERS
    half = share // 2
    blocks = [
        ow_ref[o * share + g * half : o * share + (g + 1) * half].astype(jnp.float32)
        for g in (0, 1)
        for o in range(OWNERS)
    ]
    ow_turned[...] = jnp.concatenate(blocks, 0).T.astype(jnp.bfloat16)
    dw_turned[...] = dw_ref[...].astype(jnp.float32).T.astype(jnp.bfloat16)
    gate_turned = gw_ref[...].astype(jnp.float32).T.astype(jnp.bfloat16)
    for first in range(0, tile_rows, 2):
        at = slice(first * tile_cols, (first + 2) * tile_cols)
        gate_ref[:, at] = sigmoid(nt_dot(gate_turned, normed_ref[at]))
        x = x_ref[first : first + 2].astype(jnp.float32).reshape(2 * tile_cols, channels)
        x_turned_ref[:, at] = x.T


def tri_kernel(masks_ref, own, core, near, near_over, far, cross, both_over, *refs):
    outs, rights = refs[:-1], refs[-1]
    half, _, width = rights.shape
    size = own.shape[0] // 2
    tile_rows = size // half
    side = OWNERS * tile_rows
    me, col = lax.axis_index("row"), lax.axis_index("col")
    lefts = (own, core, near, near_over)
    pieces = (
        (0, own, size),
        (1, core, size),
        (2, near, size),
        (3, near_over, size),
        (4, far, 0),
        (5, both_over, 0),
        (6, cross, 0),
        (7, both_over, size),
    )
    for away, ref, start in pieces:
        at = pl.multiple_of((me ^ away) * tile_rows, tile_rows)
        for m in range(half):
            rights[m, pl.ds(at, tile_rows), :] = ref[
                start + m * tile_rows : start + (m + 1) * tile_rows
            ]
    low = lanes_of((side, width)) < width // 2
    first = masks_ref.shape[0] - tile_rows // 2
    keep = jnp.concatenate([masks_ref[first : first + 1], masks_ref[first + 1 : first + 2]], 1)
    for m in range(half):
        left = jnp.concatenate(
            [ref[m * tile_rows : (m + 1) * tile_rows] for ref in lefts], 0
        )
        pieces = []
        for dx in (0, 1):
            block = rights[m, pl.ds(pl.multiple_of((col ^ dx) * side, side), side), :]
            block = block.astype(jnp.float32)
            pieces += [jnp.where(low, block, 0.0), jnp.where(low, 0.0, block)]
        right = jnp.concatenate(pieces, 0).astype(jnp.bfloat16)
        product = (nt_dot(left, right) * keep).astype(jnp.bfloat16)
        for d in range(OWNERS):
            for dx in (0, 1):
                at = d % 2 * size + m * tile_rows
                outs[d // 2 * 2 + dx][at : at + tile_rows] = product[
                    d * tile_rows : (d + 1) * tile_rows, dx * width : (dx + 1) * width
                ]


def finish_kernel(masks_ref, x_ref, gate_ref, bins_ref, ow_ref, dw_ref, *refs):
    parts, overs = [
        [refs[first + DIAGONAL_FIRST.index(d)] for d in range(OWNERS)] for first in (0, OWNERS)
    ]
    out_ref, loss_ref, held = refs[2 * OWNERS :]
    channels = x_ref.shape[0]
    size, width = parts[0].shape[0] // 2, parts[0].shape[1]
    half = channels // 2 // OWNERS
    tile_rows, tile_cols = size // half, width // 2
    packed = OWNERS * half
    owner = owner_place()
    total = jnp.zeros((tile_rows, width), jnp.float32)
    for d in range(OWNERS):
        refs, at = ((parts, 0), (overs, size))[d % 2]
        a, b = [refs[d // 2 * 2 + dx][at : at + size].astype(jnp.float32) for dx in (0, 1)]
        block = a + b
        held[pl.ds(pl.multiple_of((owner ^ d) * size, size), size), :] = block
        total = total + jnp.sum(block.reshape(half, tile_rows, width), 0)
    average = (total + pltpu.roll(total, tile_cols, 1)) * (1.0 / channels)
    total = jnp.zeros((tile_rows, width), jnp.float32)
    for om in range(packed):
        centred = held[om * tile_rows : (om + 1) * tile_rows] - average
        total = total + centred * centred
    spread = (total + pltpu.roll(total, tile_cols, 1)) * (1.0 / channels)
    scale = lax.rsqrt(spread + 1e-05)
    low = lanes_of((packed, width)) < tile_cols
    bin_ids = lax.broadcasted_iota(jnp.int32, (dw_ref.shape[0], width), 0)
    loss = jnp.zeros((1, width), jnp.float32)
    for first in range(0, tile_rows, 2):
        a, b = [
            (held[pl.ds(ii, packed, stride=tile_rows), :] - average[ii : ii + 1]) * scale[ii : ii + 1]
            for ii in (first, first + 1)
        ]
        normed = jnp.concatenate(
            [
                jnp.where(low, a, pltpu.roll(b, tile_cols, 1)),
                jnp.where(low, pltpu.roll(a, tile_cols, 1), b),
            ],
            0,
        ).astype(jnp.bfloat16)
        update = jnp.dot(ow_ref[...], normed, preferred_element_type=jnp.float32)
        at = slice(first * tile_cols, (first + 2) * tile_cols)
        pair_out = (x_ref[:, at] + gate_ref[:, at] * update).astype(jnp.bfloat16)
        out_ref[:, at] = pair_out
        logits = jnp.dot(dw_ref[...], pair_out, preferred_element_type=jnp.float32)
        log_total = jnp.log(jnp.sum(jnp.exp(logits), axis=0, keepdims=True))
        bins = bins_ref[first // 2 : first // 2 + 1]
        picked = jnp.sum(jnp.where(bin_ids == bins, logits, 0.0), axis=0, keepdims=True)
        loss = loss + masks_ref[first // 2 : first // 2 + 1] * (log_total - picked)
    last = masks_ref.shape[0] - 1
    loss = jnp.sum(loss * masks_ref[last : last + 1], axis=1, keepdims=True)
    loss_ref[...] = jnp.broadcast_to(loss, loss_ref.shape)


def turn_back_kernel(turned_ref, out_ref):
    tile_rows, tile_cols, channels = out_ref.shape
    for first in range(0, tile_rows, 2):
        block = turned_ref[:, first * tile_cols : (first + 2) * tile_cols].astype(jnp.float32).T
        out_ref[first : first + 2] = block.astype(jnp.bfloat16).reshape(2, tile_cols, channels)


def exchange(value, places, mask):
    return lax.ppermute(value, AXES, [(at, at ^ mask) for at in range(places)])


def call(kernel, outs, scratch=(), specs=None, out_specs=None, args=(), flops=0):
    return pl.pallas_call(
        kernel,
        out_shape=outs,
        in_specs=specs if specs is not None else [VMEM] * len(args),
        out_specs=out_specs if out_specs is not None else jax.tree.map(lambda _: VMEM, outs),
        scratch_shapes=list(scratch),
        compiler_params=PARAMS,
        cost_estimate=pl.CostEstimate(flops=flops, bytes_accessed=1 << 20, transcendentals=1 << 18),
    )(*args)


def by_kernels(
    pair_repr,
    distance_bins,
    chain_lengths,
    left_weight,
    left_gate_weight,
    right_weight,
    right_gate_weight,
    out_weight,
    out_gate_weight,
    dist_weight,
):
    tile_rows, tile_cols, channels = pair_repr.shape
    rows, cols = lax.axis_size("row"), lax.axis_size("col")
    places = rows * cols
    width = 2 * tile_cols
    spots = tile_rows * tile_cols
    size = channels // OWNERS // 2 * tile_rows
    bf16, f32 = jnp.bfloat16, jnp.float32
    struct = jax.ShapeDtypeStruct
    turned = pltpu.VMEM((2 * channels, channels), bf16)
    held = pltpu.VMEM((OWNERS * size, width), f32)
    over_x, over_core, over_z, over_half = 1, cols, 2 * cols, OWNERS * cols
    near = exchange(pair_repr, places, over_z)
    normed = call(
        norm_kernel, struct((spots, channels), bf16), args=(pair_repr,), flops=1 << 30
    )
    stay, move = call(
        right_kernel,
        [struct((2 * size, width), bf16)] * 2,
        [turned, held],
        args=(normed, right_weight, right_gate_weight),
        flops=4 * spots * channels * channels,
    )
    cross = exchange(move, places, over_half + over_z)
    far = exchange(stay, places, over_half)
    block = struct((2 * size, width), bf16)
    own, core, masks = call(
        left_kernel,
        [block, block, struct((3 * tile_rows // 2, width), f32)],
        [turned, pltpu.VMEM((channels, channels), bf16), pltpu.VMEM((2 * size, width), f32)],
        [SMEM] + [VMEM] * 4,
        args=(chain_lengths, normed, left_weight, left_gate_weight, stay),
        flops=2 * spots * channels * channels,
    )
    near, near_over = call(
        near_kernel,
        [block, block],
        [
            pltpu.VMEM((4 * channels, channels), bf16),
            pltpu.VMEM((2 * channels, channels), bf16),
            pltpu.VMEM((2 * size, width), f32),
            pltpu.VMEM((2 * size, width), f32),
        ],
        args=(masks, near, left_weight, left_gate_weight, right_weight, right_gate_weight),
        flops=4 * spots * channels * channels,
    )
    near_over = exchange(near_over, places, over_core)
    core = exchange(core, places, over_core)
    both_over = call(
        pack_kernel,
        block,
        specs=[VMEM, VMEM, pl.BlockSpec(memory_space=pl.ANY)],
        args=(far, cross, near_over),
    )
    both_over = exchange(both_over, places, over_core)
    parts = call(
        tri_kernel,
        [struct((2 * size, width), bf16)] * OWNERS,
        [pltpu.VMEM((size // tile_rows, rows * tile_rows, width), bf16)],
        args=(masks, own, core, near, near_over, far, cross, both_over),
        flops=8 * size * 2 * tile_rows * 2 * width,
    )
    parts = [
        exchange(parts[d], places, d // 2 * over_z + d % 2 * over_x) if d else parts[0] for d in DIAGONAL_FIRST
    ]
    parts += [exchange(value, places, over_core) for value in parts]
    gate, x_turned, out_turned, dist_turned = call(
        gate_kernel,
        [
            struct((channels, spots), f32),
            struct((channels, spots), f32),
            struct((channels, channels), bf16),
            struct(dist_weight.shape[::-1], bf16),
        ],
        args=(pair_repr, normed, out_gate_weight, out_weight, dist_weight),
        flops=2 * spots * channels * channels,
    )
    pair_out, loss = call(
        finish_kernel,
        [struct((channels, spots), bf16), struct((8, 128), f32)],
        [held],
        args=(
            masks,
            x_turned,
            gate,
            distance_bins.reshape(tile_rows // 2, width),
            out_turned,
            dist_turned,
            *parts,
        ),
        flops=6 * spots * channels * channels,
    )
    pair_out = call(turn_back_kernel, struct(pair_repr.shape, bf16), args=(pair_out,), flops=1 << 26)
    loss = loss + exchange(loss, places, over_core)
    loss = loss + exchange(loss, places, over_x)
    cross_loss, half, near_loss = [
        exchange(loss, places, mask) for mask in (over_half + over_z, over_half, over_z)
    ]
    loss = (cross_loss + half) + (near_loss + loss)
    return (pair_out, loss[0, :1])


def by_all_to_all(
    pair_repr,
    distance_bins,
    chain_lengths,
    left_weight,
    left_gate_weight,
    right_weight,
    right_gate_weight,
    out_weight,
    out_gate_weight,
    dist_weight,
):
    tile_rows, tile_cols, channels = pair_repr.shape
    rows, cols = lax.axis_size("row"), lax.axis_size("col")
    peers = rows * cols
    share = channels // peers
    residues = tile_rows * rows
    spots = tile_rows * tile_cols
    live_count = residues - chain_lengths[chain_lengths.shape[0] - 1]
    row_place = lax.axis_index("row") * tile_rows + jnp.arange(tile_rows, dtype=jnp.int32)
    col_place = lax.axis_index("col") * tile_cols + jnp.arange(tile_cols, dtype=jnp.int32)
    live_rows = (row_place < live_count).astype(jnp.float32)
    live_cols = (col_place < live_count).astype(jnp.float32)
    flat_mask = (live_rows[:, None] * live_cols[None, :]).reshape(-1)
    normed = layer_norm(pair_repr.astype(jnp.float32), -1).astype(jnp.bfloat16)
    normed = normed.reshape(spots, channels)

    def project_turned(weight):
        return lax.dot_general(
            weight, normed, (((0,), (1,)), ((), ())), preferred_element_type=jnp.float32
        )

    def gated(gate_weight, weight):
        values = jax.nn.sigmoid(project_turned(gate_weight)) * project_turned(weight)
        return (values * flat_mask[None, :]).astype(jnp.bfloat16)

    left = gated(left_gate_weight, left_weight).reshape(peers, share, tile_rows, tile_cols)
    right = gated(right_gate_weight, right_weight).reshape(peers, share, tile_rows, tile_cols)
    both = jnp.concatenate([left, right], axis=3).reshape(peers, share * tile_rows, 2 * tile_cols)
    owned = lax.all_to_all(both, AXES, split_axis=0, concat_axis=0, tiled=True)
    owned = owned.reshape(rows, cols, share, tile_rows, 2, tile_cols)
    owned = owned.transpose(4, 2, 0, 3, 1, 5).reshape(2, share, residues, residues)
    tri = jnp.einsum(
        "cik,cjk->cij", owned[0], owned[1], preferred_element_type=jnp.float32
    ).astype(jnp.bfloat16)
    tri = tri.reshape(share, rows, tile_rows, cols, tile_cols).transpose(1, 3, 0, 2, 4)
    tri = tri.reshape(peers, share, spots)
    tri = lax.all_to_all(tri, AXES, split_axis=0, concat_axis=0, tiled=True)
    tri = tri.reshape(channels, spots).astype(jnp.float32)
    tri_normed = layer_norm(tri, 0).astype(jnp.bfloat16)
    out_gate = jax.nn.sigmoid(jnp.dot(normed, out_gate_weight, preferred_element_type=jnp.float32))
    update = out_gate * tn_dot(tri_normed, out_weight)
    pair_out = (pair_repr.astype(jnp.float32).reshape(spots, channels) + update).astype(
        jnp.bfloat16
    )
    logits = jnp.dot(pair_out, dist_weight, preferred_element_type=jnp.float32)
    log_total = jnp.log(jnp.sum(jnp.exp(logits), axis=-1))
    bin_ids = jnp.arange(logits.shape[1], dtype=jnp.int32)
    picked = jnp.sum(
        jnp.where(bin_ids[None, :] == distance_bins.reshape(-1, 1), logits, 0.0), axis=-1
    )
    loss_sum = jnp.sum(flat_mask * (log_total - picked))
    sums = lax.all_to_all(
        jnp.full((peers, 1, 128), loss_sum), AXES, split_axis=0, concat_axis=0, tiled=True
    )
    pair_count = (live_count * live_count).astype(jnp.float32)
    loss_value = (jnp.sum(sums[:, 0, 0]) / pair_count).reshape(1)
    return (pair_out.reshape(pair_repr.shape), loss_value)


def on_device(pair_repr, *others):
    tile_rows, tile_cols, channels = pair_repr.shape
    rows, cols = lax.axis_size("row"), lax.axis_size("col")
    fits = (
        rows == 2 * OWNERS
        and cols == 2
        and tile_rows * rows == tile_cols * cols
        and 2 * tile_cols == 128
        and tile_rows == 16
        and channels == 32 * OWNERS
    )
    return (by_kernels if fits else by_all_to_all)(pair_repr, *others)


def solution(mesh):
    in_specs = (
        P(("groups", "row"), "col", None),
        P(("groups", "row"), "col"),
        P("groups"),
        P(),
        P(),
        P(),
        P(),
        P(),
        P(),
        P(),
    )
    out_specs = (P(("groups", "row"), "col", None), P("groups"))
    return jax.shard_map(
        on_device, mesh=mesh, in_specs=in_specs, out_specs=out_specs, check_vma=False
    )
```

```python
import jax
import jax.numpy as jnp
from jax import lax
from jax.experimental import pallas as pl
from jax.experimental.pallas import tpu as pltpu
from jax.sharding import PartitionSpec as P

AXES = ("row", "col")
OWNERS = 4
DIAGONAL_FIRST = (0, 3, 2, 1)
VMEM = pl.BlockSpec(memory_space=pltpu.VMEM)
SMEM = pl.BlockSpec(memory_space=pltpu.SMEM)
PARAMS = pltpu.CompilerParams(vmem_limit_bytes=24 * 1024 * 1024)


def layer_norm(values, axis):
    average = jnp.mean(values, axis=axis, keepdims=True)
    centred = values - average
    spread = jnp.mean(centred * centred, axis=axis, keepdims=True)
    return centred * lax.rsqrt(spread + 1e-05)


def sigmoid(values):
    return 0.5 * jnp.tanh(0.5 * values) + 0.5


def nt_dot(a, b):
    return lax.dot_general(a, b, (((1,), (1,)), ((), ())), preferred_element_type=jnp.float32)


def tn_dot(a, b):
    return lax.dot_general(a, b, (((0,), (0,)), ((), ())), preferred_element_type=jnp.float32)


def lanes_of(shape):
    return lax.broadcasted_iota(jnp.int32, shape, 1)


def make_masks(lens_ref, tile_rows, tile_cols):
    live = tile_rows * lax.axis_size("row") - lens_ref[lens_ref.shape[0] - 1]
    lane = lanes_of((1, 2 * tile_cols))
    upper = (lane >= tile_cols).astype(jnp.int32)
    place = lane - tile_cols * upper
    row, col = lax.axis_index("row"), lax.axis_index("col")
    keeps = [(place + (col ^ dx) * tile_cols < live).astype(jnp.float32) for dx in (0, 1)]
    pairs = [
        ((row ^ d) * tile_rows + first + upper < live).astype(jnp.float32) * keeps[0]
        for d in (0, OWNERS // 2)
        for first in range(0, tile_rows, 2)
    ]
    count = jnp.full(lane.shape, live * live, jnp.int32).astype(jnp.float32)
    return pairs, keeps, 1.0 / count


def turn(w_refs, turned):
    channels = w_refs[0].shape[0]
    share = channels // OWNERS
    half = share // 2
    for at, w_ref in enumerate(w_refs):
        w = w_ref[...].astype(jnp.float32).T
        blocks = [
            w[o * share + g * half : o * share + (g + 1) * half] for g in (0, 1) for o in range(OWNERS)
        ]
        turned[at * channels : (at + 1) * channels] = jnp.concatenate(blocks, 0).astype(jnp.bfloat16)


def store_rows(held, first, value, tile_cols):
    packed = value.shape[0] // 2
    stride = held.shape[0] // packed
    a, b = value[:packed], value[packed:]
    low = lanes_of(a.shape) < tile_cols
    held[pl.ds(first, packed, stride=stride), :] = jnp.where(low, a, pltpu.roll(b, tile_cols, 1))
    held[pl.ds(first + 1, packed, stride=stride), :] = jnp.where(low, pltpu.roll(a, tile_cols, 1), b)


def chip_rows(turned, mine):
    size = mine.shape[0] // (turned.shape[0] // mine.shape[1]) // 2
    pair = owner_place() // 2
    for at in range(mine.shape[0] // size):
        start = pl.multiple_of(at * (mine.shape[1] // 2) + pair * size, size)
        mine[at * size : (at + 1) * size] = turned[pl.ds(start, size), :]


def owner_place():
    return lax.axis_index("row") % OWNERS


def owner_block(held, d, size):
    at = pl.multiple_of((owner_place() ^ d) * size, size)
    return held[pl.ds(at, size)].astype(jnp.bfloat16)


def core_block(held, d, size):
    at = pl.multiple_of((owner_place() % 2 ^ d) * size, size)
    return held[pl.ds(at, size)].astype(jnp.bfloat16)


def norm_kernel(x_ref, normed_ref):
    x = x_ref[...].astype(jnp.float32).reshape(normed_ref.shape)
    normed_ref[...] = layer_norm(x, -1).astype(jnp.bfloat16)


def right_kernel(normed_ref, w_ref, g_ref, stay_ref, move_ref, turned, held):
    channels = normed_ref.shape[1]
    width = held.shape[1]
    turn((w_ref, g_ref), turned)
    for at in range(normed_ref.shape[0] // width):
        flat = nt_dot(turned[...], normed_ref[at * width : (at + 1) * width])
        store_rows(held, 2 * at, sigmoid(flat[channels:]) * flat[:channels], width // 2)
    size = stay_ref.shape[0] // 2
    for d, ref in enumerate((stay_ref, stay_ref, move_ref, move_ref)):
        ref[d % 2 * size : (d % 2 + 1) * size] = owner_block(held, d, size)


def left_kernel(lens_ref, normed_ref, w_ref, g_ref, stay_ref, own_ref, core_ref, masks_ref, *refs):
    turned, mine, held = refs
    width = held.shape[1]
    half = mine.shape[0] // 2
    pairs, keeps, share = make_masks(lens_ref, 2 * normed_ref.shape[0] // width, width // 2)
    masks_ref[...] = jnp.concatenate(
        pairs + keeps + [share] * (masks_ref.shape[0] - len(pairs) - len(keeps)), 0
    )
    turn((w_ref, g_ref), turned)
    chip_rows(turned, mine)
    for at in range(normed_ref.shape[0] // width):
        flat = nt_dot(mine[...], normed_ref[at * width : (at + 1) * width])
        store_rows(held, 2 * at, sigmoid(flat[half:]) * flat[:half] * pairs[at], width // 2)
    size = stay_ref.shape[0] // 2
    for d, ref in enumerate((own_ref, core_ref)):
        ref[:size] = core_block(held, d, size)
        ref[size:] = stay_ref[d * size : (d + 1) * size]


def near_kernel(masks_ref, x_ref, lw_ref, lg_ref, rw_ref, rg_ref, near_ref, over_ref, *refs):
    turned, mine, held_left, held_right = refs
    tile_rows, tile_cols, channels = x_ref.shape
    share = mine.shape[0] // 4
    turn((lw_ref, lg_ref, rw_ref, rg_ref), turned)
    chip_rows(turned, mine)
    for first in range(0, tile_rows, 2):
        x = x_ref[first : first + 2].astype(jnp.float32).reshape(2 * tile_cols, channels)
        flat = nt_dot(mine[...], layer_norm(x, -1).astype(jnp.bfloat16))
        lv, lg, rv, rg = [flat[at * share : (at + 1) * share] for at in range(4)]
        line = (tile_rows + first) // 2
        store_rows(held_left, first, sigmoid(lg) * lv * masks_ref[line : line + 1], tile_cols)
        store_rows(held_right, first, sigmoid(rg) * rv, tile_cols)
    size = near_ref.shape[0] // 2
    for d, ref in enumerate((near_ref, over_ref)):
        ref[:size] = core_block(held_left, d, size)
        ref[size:] = core_block(held_right, d, size)


def pack_kernel(far_ref, cross_ref, ready_ref, out_ref):
    del ready_ref
    size = out_ref.shape[0] // 2
    out_ref[:size] = far_ref[size:]
    out_ref[size:] = cross_ref[size:]


def gate_kernel(x_ref, normed_ref, gw_ref, ow_ref, dw_ref, gate_ref, x_turned_ref, ow_turned, dw_turned):
    tile_rows, tile_cols, channels = x_ref.shape
    share = channels // OWNERS
    half = share // 2
    blocks = [
        ow_ref[o * share + g * half : o * share + (g + 1) * half].astype(jnp.float32)
        for g in (0, 1)
        for o in range(OWNERS)
    ]
    ow_turned[...] = jnp.concatenate(blocks, 0).T.astype(jnp.bfloat16)
    dw_turned[...] = dw_ref[...].astype(jnp.float32).T.astype(jnp.bfloat16)
    gate_turned = gw_ref[...].astype(jnp.float32).T.astype(jnp.bfloat16)
    for first in range(0, tile_rows, 2):
        at = slice(first * tile_cols, (first + 2) * tile_cols)
        gate_ref[:, at] = sigmoid(nt_dot(gate_turned, normed_ref[at]))
        x = x_ref[first : first + 2].astype(jnp.float32).reshape(2 * tile_cols, channels)
        x_turned_ref[:, at] = x.T


def tri_kernel(masks_ref, own, core, near, near_over, far, cross, both_over, *refs):
    outs, rights = refs[:-1], refs[-1]
    half, _, width = rights.shape
    size = own.shape[0] // 2
    tile_rows = size // half
    side = OWNERS * tile_rows
    me, col = lax.axis_index("row"), lax.axis_index("col")
    lefts = (own, core, near, near_over)
    pieces = (
        (0, own, size),
        (1, core, size),
        (2, near, size),
        (3, near_over, size),
        (4, far, 0),
        (5, both_over, 0),
        (6, cross, 0),
        (7, both_over, size),
    )
    for away, ref, start in pieces:
        at = pl.multiple_of((me ^ away) * tile_rows, tile_rows)
        for m in range(half):
            rights[m, pl.ds(at, tile_rows), :] = ref[
                start + m * tile_rows : start + (m + 1) * tile_rows
            ]
    low = lanes_of((side, width)) < width // 2
    first = masks_ref.shape[0] - tile_rows // 2
    keep = jnp.concatenate([masks_ref[first : first + 1], masks_ref[first + 1 : first + 2]], 1)
    for m in range(half):
        left = jnp.concatenate(
            [ref[m * tile_rows : (m + 1) * tile_rows] for ref in lefts], 0
        )
        pieces = []
        for dx in (0, 1):
            block = rights[m, pl.ds(pl.multiple_of((col ^ dx) * side, side), side), :]
            block = block.astype(jnp.float32)
            pieces += [jnp.where(low, block, 0.0), jnp.where(low, 0.0, block)]
        right = jnp.concatenate(pieces, 0).astype(jnp.bfloat16)
        product = (nt_dot(left, right) * keep).astype(jnp.bfloat16)
        for d in range(OWNERS):
            for dx in (0, 1):
                at = d % 2 * size + m * tile_rows
                outs[d // 2 * 2 + dx][at : at + tile_rows] = product[
                    d * tile_rows : (d + 1) * tile_rows, dx * width : (dx + 1) * width
                ]


def finish_kernel(masks_ref, x_ref, gate_ref, bins_ref, ow_ref, dw_ref, *refs):
    parts, overs = [
        [refs[first + DIAGONAL_FIRST.index(d)] for d in range(OWNERS)] for first in (0, OWNERS)
    ]
    out_ref, loss_ref, held = refs[2 * OWNERS :]
    channels = x_ref.shape[0]
    size, width = parts[0].shape[0] // 2, parts[0].shape[1]
    half = channels // 2 // OWNERS
    tile_rows, tile_cols = size // half, width // 2
    packed = OWNERS * half
    owner = owner_place()
    total = jnp.zeros((tile_rows, width), jnp.float32)
    for d in range(OWNERS):
        refs, at = ((parts, 0), (overs, size))[d % 2]
        a, b = [refs[d // 2 * 2 + dx][at : at + size].astype(jnp.float32) for dx in (0, 1)]
        block = a + b
        held[pl.ds(pl.multiple_of((owner ^ d) * size, size), size), :] = block
        total = total + jnp.sum(block.reshape(half, tile_rows, width), 0)
    average = (total + pltpu.roll(total, tile_cols, 1)) * (1.0 / channels)
    total = jnp.zeros((tile_rows, width), jnp.float32)
    for om in range(packed):
        centred = held[om * tile_rows : (om + 1) * tile_rows] - average
        total = total + centred * centred
    spread = (total + pltpu.roll(total, tile_cols, 1)) * (1.0 / channels)
    scale = lax.rsqrt(spread + 1e-05)
    low = lanes_of((packed, width)) < tile_cols
    bin_ids = lax.broadcasted_iota(jnp.int32, (dw_ref.shape[0], width), 0)
    loss = jnp.zeros((1, width), jnp.float32)
    for first in range(0, tile_rows, 2):
        a, b = [
            (held[pl.ds(ii, packed, stride=tile_rows), :] - average[ii : ii + 1]) * scale[ii : ii + 1]
            for ii in (first, first + 1)
        ]
        normed = jnp.concatenate(
            [
                jnp.where(low, a, pltpu.roll(b, tile_cols, 1)),
                jnp.where(low, pltpu.roll(a, tile_cols, 1), b),
            ],
            0,
        ).astype(jnp.bfloat16)
        update = jnp.dot(ow_ref[...], normed, preferred_element_type=jnp.float32)
        at = slice(first * tile_cols, (first + 2) * tile_cols)
        pair_out = (x_ref[:, at] + gate_ref[:, at] * update).astype(jnp.bfloat16)
        out_ref[:, at] = pair_out
        logits = jnp.dot(dw_ref[...], pair_out, preferred_element_type=jnp.float32)
        log_total = jnp.log(jnp.sum(jnp.exp(logits), axis=0, keepdims=True))
        bins = bins_ref[first // 2 : first // 2 + 1]
        picked = jnp.sum(jnp.where(bin_ids == bins, logits, 0.0), axis=0, keepdims=True)
        loss = loss + masks_ref[first // 2 : first // 2 + 1] * (log_total - picked)
    last = masks_ref.shape[0] - 1
    loss = jnp.sum(loss * masks_ref[last : last + 1], axis=1, keepdims=True)
    loss_ref[...] = jnp.broadcast_to(loss, loss_ref.shape)


def turn_back_kernel(turned_ref, out_ref):
    tile_rows, tile_cols, channels = out_ref.shape
    for first in range(0, tile_rows, 2):
        block = turned_ref[:, first * tile_cols : (first + 2) * tile_cols].astype(jnp.float32).T
        out_ref[first : first + 2] = block.astype(jnp.bfloat16).reshape(2, tile_cols, channels)


def exchange(value, places, mask):
    return lax.ppermute(value, AXES, [(at, at ^ mask) for at in range(places)])


def call(kernel, outs, scratch=(), specs=None, out_specs=None, args=(), flops=0):
    return pl.pallas_call(
        kernel,
        out_shape=outs,
        in_specs=specs if specs is not None else [VMEM] * len(args),
        out_specs=out_specs if out_specs is not None else jax.tree.map(lambda _: VMEM, outs),
        scratch_shapes=list(scratch),
        compiler_params=PARAMS,
        cost_estimate=pl.CostEstimate(flops=flops, bytes_accessed=1 << 20, transcendentals=1 << 18),
    )(*args)


def by_kernels(
    pair_repr,
    distance_bins,
    chain_lengths,
    left_weight,
    left_gate_weight,
    right_weight,
    right_gate_weight,
    out_weight,
    out_gate_weight,
    dist_weight,
):
    tile_rows, tile_cols, channels = pair_repr.shape
    rows, cols = lax.axis_size("row"), lax.axis_size("col")
    places = rows * cols
    width = 2 * tile_cols
    spots = tile_rows * tile_cols
    size = channels // OWNERS // 2 * tile_rows
    bf16, f32 = jnp.bfloat16, jnp.float32
    struct = jax.ShapeDtypeStruct
    turned = pltpu.VMEM((2 * channels, channels), bf16)
    held = pltpu.VMEM((OWNERS * size, width), f32)
    over_x, over_core, over_z, over_half = 1, cols, 2 * cols, OWNERS * cols
    near = exchange(pair_repr, places, over_z)
    normed = call(
        norm_kernel, struct((spots, channels), bf16), args=(pair_repr,), flops=1 << 30
    )
    stay, move = call(
        right_kernel,
        [struct((2 * size, width), bf16)] * 2,
        [turned, held],
        args=(normed, right_weight, right_gate_weight),
        flops=4 * spots * channels * channels,
    )
    cross = exchange(move, places, over_half + over_z)
    far = exchange(stay, places, over_half)
    block = struct((2 * size, width), bf16)
    own, core, masks = call(
        left_kernel,
        [block, block, struct((3 * tile_rows // 2, width), f32)],
        [turned, pltpu.VMEM((channels, channels), bf16), pltpu.VMEM((2 * size, width), f32)],
        [SMEM] + [VMEM] * 4,
        args=(chain_lengths, normed, left_weight, left_gate_weight, stay),
        flops=2 * spots * channels * channels,
    )
    near, near_over = call(
        near_kernel,
        [block, block],
        [
            pltpu.VMEM((4 * channels, channels), bf16),
            pltpu.VMEM((2 * channels, channels), bf16),
            pltpu.VMEM((2 * size, width), f32),
            pltpu.VMEM((2 * size, width), f32),
        ],
        args=(masks, near, left_weight, left_gate_weight, right_weight, right_gate_weight),
        flops=4 * spots * channels * channels,
    )
    near_over = exchange(near_over, places, over_core)
    core = exchange(core, places, over_core)
    both_over = call(
        pack_kernel,
        block,
        specs=[VMEM, VMEM, pl.BlockSpec(memory_space=pl.ANY)],
        args=(far, cross, near_over),
    )
    both_over = exchange(both_over, places, over_core)
    parts = call(
        tri_kernel,
        [struct((2 * size, width), bf16)] * OWNERS,
        [pltpu.VMEM((size // tile_rows, rows * tile_rows, width), bf16)],
        args=(masks, own, core, near, near_over, far, cross, both_over),
        flops=8 * size * 2 * tile_rows * 2 * width,
    )
    parts = [
        exchange(parts[d], places, d // 2 * over_z + d % 2 * over_x) if d else parts[0] for d in DIAGONAL_FIRST
    ]
    parts += [exchange(value, places, over_core) for value in parts]
    gate, x_turned, out_turned, dist_turned = call(
        gate_kernel,
        [
            struct((channels, spots), f32),
            struct((channels, spots), f32),
            struct((channels, channels), bf16),
            struct(dist_weight.shape[::-1], bf16),
        ],
        args=(pair_repr, normed, out_gate_weight, out_weight, dist_weight),
        flops=2 * spots * channels * channels,
    )
    pair_out, loss = call(
        finish_kernel,
        [struct((channels, spots), bf16), struct((8, 128), f32)],
        [held],
        args=(
            masks,
            x_turned,
            gate,
            distance_bins.reshape(tile_rows // 2, width),
            out_turned,
            dist_turned,
            *parts,
        ),
        flops=6 * spots * channels * channels,
    )
    pair_out = call(turn_back_kernel, struct(pair_repr.shape, bf16), args=(pair_out,), flops=1 << 26)
    loss = loss + exchange(loss, places, over_core)
    loss = loss + exchange(loss, places, over_x)
    cross_loss, half, near_loss = [
        exchange(loss, places, mask) for mask in (over_half + over_z, over_half, over_z)
    ]
    loss = (cross_loss + half) + (near_loss + loss)
    return (pair_out, loss[0, :1])


def by_all_to_all(
    pair_repr,
    distance_bins,
    chain_lengths,
    left_weight,
    left_gate_weight,
    right_weight,
    right_gate_weight,
    out_weight,
    out_gate_weight,
    dist_weight,
):
    tile_rows, tile_cols, channels = pair_repr.shape
    rows, cols = lax.axis_size("row"), lax.axis_size("col")
    peers = rows * cols
    share = channels // peers
    residues = tile_rows * rows
    spots = tile_rows * tile_cols
    live_count = residues - chain_lengths[chain_lengths.shape[0] - 1]
    row_place = lax.axis_index("row") * tile_rows + jnp.arange(tile_rows, dtype=jnp.int32)
    col_place = lax.axis_index("col") * tile_cols + jnp.arange(tile_cols, dtype=jnp.int32)
    live_rows = (row_place < live_count).astype(jnp.float32)
    live_cols = (col_place < live_count).astype(jnp.float32)
    flat_mask = (live_rows[:, None] * live_cols[None, :]).reshape(-1)
    normed = layer_norm(pair_repr.astype(jnp.float32), -1).astype(jnp.bfloat16)
    normed = normed.reshape(spots, channels)

    def project_turned(weight):
        return lax.dot_general(
            weight, normed, (((0,), (1,)), ((), ())), preferred_element_type=jnp.float32
        )

    def gated(gate_weight, weight):
        values = jax.nn.sigmoid(project_turned(gate_weight)) * project_turned(weight)
        return (values * flat_mask[None, :]).astype(jnp.bfloat16)

    left = gated(left_gate_weight, left_weight).reshape(peers, share, tile_rows, tile_cols)
    right = gated(right_gate_weight, right_weight).reshape(peers, share, tile_rows, tile_cols)
    both = jnp.concatenate([left, right], axis=3).reshape(peers, share * tile_rows, 2 * tile_cols)
    owned = lax.all_to_all(both, AXES, split_axis=0, concat_axis=0, tiled=True)
    owned = owned.reshape(rows, cols, share, tile_rows, 2, tile_cols)
    owned = owned.transpose(4, 2, 0, 3, 1, 5).reshape(2, share, residues, residues)
    tri = jnp.einsum(
        "cik,cjk->cij", owned[0], owned[1], preferred_element_type=jnp.float32
    ).astype(jnp.bfloat16)
    tri = tri.reshape(share, rows, tile_rows, cols, tile_cols).transpose(1, 3, 0, 2, 4)
    tri = tri.reshape(peers, share, spots)
    tri = lax.all_to_all(tri, AXES, split_axis=0, concat_axis=0, tiled=True)
    tri = tri.reshape(channels, spots).astype(jnp.float32)
    tri_normed = layer_norm(tri, 0).astype(jnp.bfloat16)
    out_gate = jax.nn.sigmoid(jnp.dot(normed, out_gate_weight, preferred_element_type=jnp.float32))
    update = out_gate * tn_dot(tri_normed, out_weight)
    pair_out = (pair_repr.astype(jnp.float32).reshape(spots, channels) + update).astype(
        jnp.bfloat16
    )
    logits = jnp.dot(pair_out, dist_weight, preferred_element_type=jnp.float32)
    log_total = jnp.log(jnp.sum(jnp.exp(logits), axis=-1))
    bin_ids = jnp.arange(logits.shape[1], dtype=jnp.int32)
    picked = jnp.sum(
        jnp.where(bin_ids[None, :] == distance_bins.reshape(-1, 1), logits, 0.0), axis=-1
    )
    loss_sum = jnp.sum(flat_mask * (log_total - picked))
    sums = lax.all_to_all(
        jnp.full((peers, 1, 128), loss_sum), AXES, split_axis=0, concat_axis=0, tiled=True
    )
    pair_count = (live_count * live_count).astype(jnp.float32)
    loss_value = (jnp.sum(sums[:, 0, 0]) / pair_count).reshape(1)
    return (pair_out.reshape(pair_repr.shape), loss_value)


def on_device(pair_repr, *others):
    tile_rows, tile_cols, channels = pair_repr.shape
    rows, cols = lax.axis_size("row"), lax.axis_size("col")
    fits = (
        rows == 2 * OWNERS
        and cols == 2
        and tile_rows * rows == tile_cols * cols
        and 2 * tile_cols == 128
        and tile_rows == 16
        and channels == 32 * OWNERS
    )
    return (by_kernels if fits else by_all_to_all)(pair_repr, *others)


def solution(mesh):
    in_specs = (
        P(("groups", "row"), "col", None),
        P(("groups", "row"), "col"),
        P("groups"),
        P(),
        P(),
        P(),
        P(),
        P(),
        P(),
        P(),
    )
    out_specs = (P(("groups", "row"), "col", None), P("groups"))
    return jax.shard_map(
        on_device, mesh=mesh, in_specs=in_specs, out_specs=out_specs, check_vma=False
    )
```

```python
import jax
import jax.numpy as jnp
from jax import lax
from jax.experimental import pallas as pl
from jax.experimental.pallas import tpu as pltpu
from jax.sharding import PartitionSpec as P

AXES = ("row", "col")
OWNERS = 4
DIAGONAL_FIRST = (0, 3, 2, 1)
VMEM = pl.BlockSpec(memory_space=pltpu.VMEM)
SMEM = pl.BlockSpec(memory_space=pltpu.SMEM)
PARAMS = pltpu.CompilerParams(vmem_limit_bytes=24 * 1024 * 1024)


def layer_norm(values, axis):
    average = jnp.mean(values, axis=axis, keepdims=True)
    centred = values - average
    spread = jnp.mean(centred * centred, axis=axis, keepdims=True)
    return centred * lax.rsqrt(spread + 1e-05)


def sigmoid(values):
    return 0.5 * jnp.tanh(0.5 * values) + 0.5


def nt_dot(a, b):
    return lax.dot_general(a, b, (((1,), (1,)), ((), ())), preferred_element_type=jnp.float32)


def tn_dot(a, b):
    return lax.dot_general(a, b, (((0,), (0,)), ((), ())), preferred_element_type=jnp.float32)


def lanes_of(shape):
    return lax.broadcasted_iota(jnp.int32, shape, 1)


def make_masks(lens_ref, tile_rows, tile_cols):
    live = tile_rows * lax.axis_size("row") - lens_ref[lens_ref.shape[0] - 1]
    lane = lanes_of((1, 2 * tile_cols))
    upper = (lane >= tile_cols).astype(jnp.int32)
    place = lane - tile_cols * upper
    row, col = lax.axis_index("row"), lax.axis_index("col")
    keeps = [(place + (col ^ dx) * tile_cols < live).astype(jnp.float32) for dx in (0, 1)]
    pairs = [
        ((row ^ d) * tile_rows + first + upper < live).astype(jnp.float32) * keeps[0]
        for d in (0, OWNERS // 2)
        for first in range(0, tile_rows, 2)
    ]
    count = jnp.full(lane.shape, live * live, jnp.int32).astype(jnp.float32)
    return pairs, keeps, 1.0 / count


def turn(w_refs, turned):
    channels = w_refs[0].shape[0]
    share = channels // OWNERS
    half = share // 2
    for at, w_ref in enumerate(w_refs):
        w = w_ref[...].astype(jnp.float32).T
        blocks = [
            w[o * share + g * half : o * share + (g + 1) * half] for g in (0, 1) for o in range(OWNERS)
        ]
        turned[at * channels : (at + 1) * channels] = jnp.concatenate(blocks, 0).astype(jnp.bfloat16)


def store_rows(held, first, value, tile_cols):
    packed = value.shape[0] // 2
    stride = held.shape[0] // packed
    a, b = value[:packed], value[packed:]
    low = lanes_of(a.shape) < tile_cols
    held[pl.ds(first, packed, stride=stride), :] = jnp.where(low, a, pltpu.roll(b, tile_cols, 1))
    held[pl.ds(first + 1, packed, stride=stride), :] = jnp.where(low, pltpu.roll(a, tile_cols, 1), b)


def chip_rows(turned, mine):
    size = mine.shape[0] // (turned.shape[0] // mine.shape[1]) // 2
    pair = owner_place() // 2
    for at in range(mine.shape[0] // size):
        start = pl.multiple_of(at * (mine.shape[1] // 2) + pair * size, size)
        mine[at * size : (at + 1) * size] = turned[pl.ds(start, size), :]


def owner_place():
    return lax.axis_index("row") % OWNERS


def owner_block(held, d, size):
    at = pl.multiple_of((owner_place() ^ d) * size, size)
    return held[pl.ds(at, size)].astype(jnp.bfloat16)


def core_block(held, d, size):
    at = pl.multiple_of((owner_place() % 2 ^ d) * size, size)
    return held[pl.ds(at, size)].astype(jnp.bfloat16)


def norm_kernel(x_ref, normed_ref):
    x = x_ref[...].astype(jnp.float32).reshape(normed_ref.shape)
    normed_ref[...] = layer_norm(x, -1).astype(jnp.bfloat16)


def right_kernel(normed_ref, w_ref, g_ref, stay_ref, move_ref, turned, held):
    channels = normed_ref.shape[1]
    width = held.shape[1]
    turn((w_ref, g_ref), turned)
    for at in range(normed_ref.shape[0] // width):
        flat = nt_dot(turned[...], normed_ref[at * width : (at + 1) * width])
        store_rows(held, 2 * at, sigmoid(flat[channels:]) * flat[:channels], width // 2)
    size = stay_ref.shape[0] // 2
    for d, ref in enumerate((stay_ref, stay_ref, move_ref, move_ref)):
        ref[d % 2 * size : (d % 2 + 1) * size] = owner_block(held, d, size)


def left_kernel(lens_ref, normed_ref, w_ref, g_ref, stay_ref, own_ref, core_ref, masks_ref, *refs):
    turned, mine, held = refs
    width = held.shape[1]
    half = mine.shape[0] // 2
    pairs, keeps, share = make_masks(lens_ref, 2 * normed_ref.shape[0] // width, width // 2)
    masks_ref[...] = jnp.concatenate(
        pairs + keeps + [share] * (masks_ref.shape[0] - len(pairs) - len(keeps)), 0
    )
    turn((w_ref, g_ref), turned)
    chip_rows(turned, mine)
    for at in range(normed_ref.shape[0] // width):
        flat = nt_dot(mine[...], normed_ref[at * width : (at + 1) * width])
        store_rows(held, 2 * at, sigmoid(flat[half:]) * flat[:half] * pairs[at], width // 2)
    size = stay_ref.shape[0] // 2
    for d, ref in enumerate((own_ref, core_ref)):
        ref[:size] = core_block(held, d, size)
        ref[size:] = stay_ref[d * size : (d + 1) * size]


def near_kernel(masks_ref, x_ref, lw_ref, lg_ref, rw_ref, rg_ref, near_ref, over_ref, *refs):
    turned, mine, held_left, held_right = refs
    tile_rows, tile_cols, channels = x_ref.shape
    share = mine.shape[0] // 4
    turn((lw_ref, lg_ref, rw_ref, rg_ref), turned)
    chip_rows(turned, mine)
    for first in range(0, tile_rows, 2):
        x = x_ref[first : first + 2].astype(jnp.float32).reshape(2 * tile_cols, channels)
        flat = nt_dot(mine[...], layer_norm(x, -1).astype(jnp.bfloat16))
        lv, lg, rv, rg = [flat[at * share : (at + 1) * share] for at in range(4)]
        line = (tile_rows + first) // 2
        store_rows(held_left, first, sigmoid(lg) * lv * masks_ref[line : line + 1], tile_cols)
        store_rows(held_right, first, sigmoid(rg) * rv, tile_cols)
    size = near_ref.shape[0] // 2
    for d, ref in enumerate((near_ref, over_ref)):
        ref[:size] = core_block(held_left, d, size)
        ref[size:] = core_block(held_right, d, size)


def pack_kernel(far_ref, cross_ref, ready_ref, out_ref):
    del ready_ref
    size = out_ref.shape[0] // 2
    out_ref[:size] = far_ref[size:]
    out_ref[size:] = cross_ref[size:]


def gate_kernel(x_ref, normed_ref, gw_ref, ow_ref, dw_ref, gate_ref, x_turned_ref, ow_turned, dw_turned):
    tile_rows, tile_cols, channels = x_ref.shape
    share = channels // OWNERS
    half = share // 2
    blocks = [
        ow_ref[o * share + g * half : o * share + (g + 1) * half].astype(jnp.float32)
        for g in (0, 1)
        for o in range(OWNERS)
    ]
    ow_turned[...] = jnp.concatenate(blocks, 0).T.astype(jnp.bfloat16)
    dw_turned[...] = dw_ref[...].astype(jnp.float32).T.astype(jnp.bfloat16)
    gate_turned = gw_ref[...].astype(jnp.float32).T.astype(jnp.bfloat16)
    for first in range(0, tile_rows, 2):
        at = slice(first * tile_cols, (first + 2) * tile_cols)
        gate_ref[:, at] = sigmoid(nt_dot(gate_turned, normed_ref[at]))
        x = x_ref[first : first + 2].astype(jnp.float32).reshape(2 * tile_cols, channels)
        x_turned_ref[:, at] = x.T


def tri_kernel(masks_ref, own, core, near, near_over, far, cross, both_over, *refs):
    outs, rights = refs[:-1], refs[-1]
    half, _, width = rights.shape
    size = own.shape[0] // 2
    tile_rows = size // half
    side = OWNERS * tile_rows
    me, col = lax.axis_index("row"), lax.axis_index("col")
    lefts = (own, core, near, near_over)
    pieces = (
        (0, own, size),
        (1, core, size),
        (2, near, size),
        (3, near_over, size),
        (4, far, 0),
        (5, both_over, 0),
        (6, cross, 0),
        (7, both_over, size),
    )
    for away, ref, start in pieces:
        at = pl.multiple_of((me ^ away) * tile_rows, tile_rows)
        for m in range(half):
            rights[m, pl.ds(at, tile_rows), :] = ref[
                start + m * tile_rows : start + (m + 1) * tile_rows
            ]
    low = lanes_of((side, width)) < width // 2
    first = masks_ref.shape[0] - tile_rows // 2
    keep = jnp.concatenate([masks_ref[first : first + 1], masks_ref[first + 1 : first + 2]], 1)
    for m in range(half):
        left = jnp.concatenate(
            [ref[m * tile_rows : (m + 1) * tile_rows] for ref in lefts], 0
        )
        pieces = []
        for dx in (0, 1):
            block = rights[m, pl.ds(pl.multiple_of((col ^ dx) * side, side), side), :]
            block = block.astype(jnp.float32)
            pieces += [jnp.where(low, block, 0.0), jnp.where(low, 0.0, block)]
        right = jnp.concatenate(pieces, 0).astype(jnp.bfloat16)
        product = (nt_dot(left, right) * keep).astype(jnp.bfloat16)
        for d in range(OWNERS):
            for dx in (0, 1):
                at = d % 2 * size + m * tile_rows
                outs[d // 2 * 2 + dx][at : at + tile_rows] = product[
                    d * tile_rows : (d + 1) * tile_rows, dx * width : (dx + 1) * width
                ]


def finish_kernel(masks_ref, x_ref, gate_ref, bins_ref, ow_ref, dw_ref, *refs):
    parts, overs = [
        [refs[first + DIAGONAL_FIRST.index(d)] for d in range(OWNERS)] for first in (0, OWNERS)
    ]
    out_ref, loss_ref, held = refs[2 * OWNERS :]
    channels = x_ref.shape[0]
    size, width = parts[0].shape[0] // 2, parts[0].shape[1]
    half = channels // 2 // OWNERS
    tile_rows, tile_cols = size // half, width // 2
    packed = OWNERS * half
    owner = owner_place()
    total = jnp.zeros((tile_rows, width), jnp.float32)
    for d in range(OWNERS):
        refs, at = ((parts, 0), (overs, size))[d % 2]
        a, b = [refs[d // 2 * 2 + dx][at : at + size].astype(jnp.float32) for dx in (0, 1)]
        block = a + b
        held[pl.ds(pl.multiple_of((owner ^ d) * size, size), size), :] = block
        total = total + jnp.sum(block.reshape(half, tile_rows, width), 0)
    average = (total + pltpu.roll(total, tile_cols, 1)) * (1.0 / channels)
    total = jnp.zeros((tile_rows, width), jnp.float32)
    for om in range(packed):
        centred = held[om * tile_rows : (om + 1) * tile_rows] - average
        total = total + centred * centred
    spread = (total + pltpu.roll(total, tile_cols, 1)) * (1.0 / channels)
    scale = lax.rsqrt(spread + 1e-05)
    low = lanes_of((packed, width)) < tile_cols
    bin_ids = lax.broadcasted_iota(jnp.int32, (dw_ref.shape[0], width), 0)
    loss = jnp.zeros((1, width), jnp.float32)
    for first in range(0, tile_rows, 2):
        a, b = [
            (held[pl.ds(ii, packed, stride=tile_rows), :] - average[ii : ii + 1]) * scale[ii : ii + 1]
            for ii in (first, first + 1)
        ]
        normed = jnp.concatenate(
            [
                jnp.where(low, a, pltpu.roll(b, tile_cols, 1)),
                jnp.where(low, pltpu.roll(a, tile_cols, 1), b),
            ],
            0,
        ).astype(jnp.bfloat16)
        update = jnp.dot(ow_ref[...], normed, preferred_element_type=jnp.float32)
        at = slice(first * tile_cols, (first + 2) * tile_cols)
        pair_out = (x_ref[:, at] + gate_ref[:, at] * update).astype(jnp.bfloat16)
        out_ref[:, at] = pair_out
        logits = jnp.dot(dw_ref[...], pair_out, preferred_element_type=jnp.float32)
        log_total = jnp.log(jnp.sum(jnp.exp(logits), axis=0, keepdims=True))
        bins = bins_ref[first // 2 : first // 2 + 1]
        picked = jnp.sum(jnp.where(bin_ids == bins, logits, 0.0), axis=0, keepdims=True)
        loss = loss + masks_ref[first // 2 : first // 2 + 1] * (log_total - picked)
    last = masks_ref.shape[0] - 1
    loss = jnp.sum(loss * masks_ref[last : last + 1], axis=1, keepdims=True)
    loss_ref[...] = jnp.broadcast_to(loss, loss_ref.shape)


def turn_back_kernel(turned_ref, out_ref):
    tile_rows, tile_cols, channels = out_ref.shape
    for first in range(0, tile_rows, 2):
        block = turned_ref[:, first * tile_cols : (first + 2) * tile_cols].astype(jnp.float32).T
        out_ref[first : first + 2] = block.astype(jnp.bfloat16).reshape(2, tile_cols, channels)


def exchange(value, places, mask):
    return lax.ppermute(value, AXES, [(at, at ^ mask) for at in range(places)])


def call(kernel, outs, scratch=(), specs=None, out_specs=None, args=(), flops=0):
    return pl.pallas_call(
        kernel,
        out_shape=outs,
        in_specs=specs if specs is not None else [VMEM] * len(args),
        out_specs=out_specs if out_specs is not None else jax.tree.map(lambda _: VMEM, outs),
        scratch_shapes=list(scratch),
        compiler_params=PARAMS,
        cost_estimate=pl.CostEstimate(flops=flops, bytes_accessed=1 << 20, transcendentals=1 << 18),
    )(*args)


def by_kernels(
    pair_repr,
    distance_bins,
    chain_lengths,
    left_weight,
    left_gate_weight,
    right_weight,
    right_gate_weight,
    out_weight,
    out_gate_weight,
    dist_weight,
):
    tile_rows, tile_cols, channels = pair_repr.shape
    rows, cols = lax.axis_size("row"), lax.axis_size("col")
    places = rows * cols
    width = 2 * tile_cols
    spots = tile_rows * tile_cols
    size = channels // OWNERS // 2 * tile_rows
    bf16, f32 = jnp.bfloat16, jnp.float32
    struct = jax.ShapeDtypeStruct
    turned = pltpu.VMEM((2 * channels, channels), bf16)
    held = pltpu.VMEM((OWNERS * size, width), f32)
    over_x, over_core, over_z, over_half = 1, cols, 2 * cols, OWNERS * cols
    near = exchange(pair_repr, places, over_z)
    normed = call(
        norm_kernel, struct((spots, channels), bf16), args=(pair_repr,), flops=1 << 30
    )
    stay, move = call(
        right_kernel,
        [struct((2 * size, width), bf16)] * 2,
        [turned, held],
        args=(normed, right_weight, right_gate_weight),
        flops=4 * spots * channels * channels,
    )
    cross = exchange(move, places, over_half + over_z)
    far = exchange(stay, places, over_half)
    block = struct((2 * size, width), bf16)
    own, core, masks = call(
        left_kernel,
        [block, block, struct((3 * tile_rows // 2, width), f32)],
        [turned, pltpu.VMEM((channels, channels), bf16), pltpu.VMEM((2 * size, width), f32)],
        [SMEM] + [VMEM] * 4,
        args=(chain_lengths, normed, left_weight, left_gate_weight, stay),
        flops=2 * spots * channels * channels,
    )
    near, near_over = call(
        near_kernel,
        [block, block],
        [
            pltpu.VMEM((4 * channels, channels), bf16),
            pltpu.VMEM((2 * channels, channels), bf16),
            pltpu.VMEM((2 * size, width), f32),
            pltpu.VMEM((2 * size, width), f32),
        ],
        args=(masks, near, left_weight, left_gate_weight, right_weight, right_gate_weight),
        flops=4 * spots * channels * channels,
    )
    near_over = exchange(near_over, places, over_core)
    core = exchange(core, places, over_core)
    both_over = call(
        pack_kernel,
        block,
        specs=[VMEM, VMEM, pl.BlockSpec(memory_space=pl.ANY)],
        args=(far, cross, near_over),
    )
    both_over = exchange(both_over, places, over_core)
    parts = call(
        tri_kernel,
        [struct((2 * size, width), bf16)] * OWNERS,
        [pltpu.VMEM((size // tile_rows, rows * tile_rows, width), bf16)],
        args=(masks, own, core, near, near_over, far, cross, both_over),
        flops=8 * size * 2 * tile_rows * 2 * width,
    )
    parts = [
        exchange(parts[d], places, d // 2 * over_z + d % 2 * over_x) if d else parts[0] for d in DIAGONAL_FIRST
    ]
    parts += [exchange(value, places, over_core) for value in parts]
    gate, x_turned, out_turned, dist_turned = call(
        gate_kernel,
        [
            struct((channels, spots), f32),
            struct((channels, spots), f32),
            struct((channels, channels), bf16),
            struct(dist_weight.shape[::-1], bf16),
        ],
        args=(pair_repr, normed, out_gate_weight, out_weight, dist_weight),
        flops=2 * spots * channels * channels,
    )
    pair_out, loss = call(
        finish_kernel,
        [struct((channels, spots), bf16), struct((8, 128), f32)],
        [held],
        args=(
            masks,
            x_turned,
            gate,
            distance_bins.reshape(tile_rows // 2, width),
            out_turned,
            dist_turned,
            *parts,
        ),
        flops=6 * spots * channels * channels,
    )
    pair_out = call(turn_back_kernel, struct(pair_repr.shape, bf16), args=(pair_out,), flops=1 << 26)
    loss = loss + exchange(loss, places, over_x)
    loss = loss + exchange(loss, places, over_core)
    cross_loss, half, near_loss = [
        exchange(loss, places, mask) for mask in (over_half + over_z, over_half, over_z)
    ]
    loss = (cross_loss + half) + (near_loss + loss)
    return (pair_out, loss[0, :1])


def by_all_to_all(
    pair_repr,
    distance_bins,
    chain_lengths,
    left_weight,
    left_gate_weight,
    right_weight,
    right_gate_weight,
    out_weight,
    out_gate_weight,
    dist_weight,
):
    tile_rows, tile_cols, channels = pair_repr.shape
    rows, cols = lax.axis_size("row"), lax.axis_size("col")
    peers = rows * cols
    share = channels // peers
    residues = tile_rows * rows
    spots = tile_rows * tile_cols
    live_count = residues - chain_lengths[chain_lengths.shape[0] - 1]
    row_place = lax.axis_index("row") * tile_rows + jnp.arange(tile_rows, dtype=jnp.int32)
    col_place = lax.axis_index("col") * tile_cols + jnp.arange(tile_cols, dtype=jnp.int32)
    live_rows = (row_place < live_count).astype(jnp.float32)
    live_cols = (col_place < live_count).astype(jnp.float32)
    flat_mask = (live_rows[:, None] * live_cols[None, :]).reshape(-1)
    normed = layer_norm(pair_repr.astype(jnp.float32), -1).astype(jnp.bfloat16)
    normed = normed.reshape(spots, channels)

    def project_turned(weight):
        return lax.dot_general(
            weight, normed, (((0,), (1,)), ((), ())), preferred_element_type=jnp.float32
        )

    def gated(gate_weight, weight):
        values = jax.nn.sigmoid(project_turned(gate_weight)) * project_turned(weight)
        return (values * flat_mask[None, :]).astype(jnp.bfloat16)

    left = gated(left_gate_weight, left_weight).reshape(peers, share, tile_rows, tile_cols)
    right = gated(right_gate_weight, right_weight).reshape(peers, share, tile_rows, tile_cols)
    both = jnp.concatenate([left, right], axis=3).reshape(peers, share * tile_rows, 2 * tile_cols)
    owned = lax.all_to_all(both, AXES, split_axis=0, concat_axis=0, tiled=True)
    owned = owned.reshape(rows, cols, share, tile_rows, 2, tile_cols)
    owned = owned.transpose(4, 2, 0, 3, 1, 5).reshape(2, share, residues, residues)
    tri = jnp.einsum(
        "cik,cjk->cij", owned[0], owned[1], preferred_element_type=jnp.float32
    ).astype(jnp.bfloat16)
    tri = tri.reshape(share, rows, tile_rows, cols, tile_cols).transpose(1, 3, 0, 2, 4)
    tri = tri.reshape(peers, share, spots)
    tri = lax.all_to_all(tri, AXES, split_axis=0, concat_axis=0, tiled=True)
    tri = tri.reshape(channels, spots).astype(jnp.float32)
    tri_normed = layer_norm(tri, 0).astype(jnp.bfloat16)
    out_gate = jax.nn.sigmoid(jnp.dot(normed, out_gate_weight, preferred_element_type=jnp.float32))
    update = out_gate * tn_dot(tri_normed, out_weight)
    pair_out = (pair_repr.astype(jnp.float32).reshape(spots, channels) + update).astype(
        jnp.bfloat16
    )
    logits = jnp.dot(pair_out, dist_weight, preferred_element_type=jnp.float32)
    log_total = jnp.log(jnp.sum(jnp.exp(logits), axis=-1))
    bin_ids = jnp.arange(logits.shape[1], dtype=jnp.int32)
    picked = jnp.sum(
        jnp.where(bin_ids[None, :] == distance_bins.reshape(-1, 1), logits, 0.0), axis=-1
    )
    loss_sum = jnp.sum(flat_mask * (log_total - picked))
    sums = lax.all_to_all(
        jnp.full((peers, 1, 128), loss_sum), AXES, split_axis=0, concat_axis=0, tiled=True
    )
    pair_count = (live_count * live_count).astype(jnp.float32)
    loss_value = (jnp.sum(sums[:, 0, 0]) / pair_count).reshape(1)
    return (pair_out.reshape(pair_repr.shape), loss_value)


def on_device(pair_repr, *others):
    tile_rows, tile_cols, channels = pair_repr.shape
    rows, cols = lax.axis_size("row"), lax.axis_size("col")
    fits = (
        rows == 2 * OWNERS
        and cols == 2
        and tile_rows * rows == tile_cols * cols
        and 2 * tile_cols == 128
        and tile_rows == 16
        and channels == 32 * OWNERS
    )
    return (by_kernels if fits else by_all_to_all)(pair_repr, *others)


def solution(mesh):
    in_specs = (
        P(("groups", "row"), "col", None),
        P(("groups", "row"), "col"),
        P("groups"),
        P(),
        P(),
        P(),
        P(),
        P(),
        P(),
        P(),
    )
    out_specs = (P(("groups", "row"), "col", None), P("groups"))
    return jax.shard_map(
        on_device, mesh=mesh, in_specs=in_specs, out_specs=out_specs, check_vma=False
    )
```

```python
import jax
import jax.numpy as jnp
from jax import lax
from jax.experimental import pallas as pl
from jax.experimental.pallas import tpu as pltpu
from jax.sharding import PartitionSpec as P

AXES = ("row", "col")
OWNERS = 4
DIAGONAL_FIRST = (0, 3, 2, 1)
VMEM = pl.BlockSpec(memory_space=pltpu.VMEM)
SMEM = pl.BlockSpec(memory_space=pltpu.SMEM)
PARAMS = pltpu.CompilerParams(vmem_limit_bytes=24 * 1024 * 1024)


def layer_norm(values, axis):
    average = jnp.mean(values, axis=axis, keepdims=True)
    centred = values - average
    spread = jnp.mean(centred * centred, axis=axis, keepdims=True)
    return centred * lax.rsqrt(spread + 1e-05)


def sigmoid(values):
    return 0.5 * jnp.tanh(0.5 * values) + 0.5


def nt_dot(a, b):
    return lax.dot_general(a, b, (((1,), (1,)), ((), ())), preferred_element_type=jnp.float32)


def tn_dot(a, b):
    return lax.dot_general(a, b, (((0,), (0,)), ((), ())), preferred_element_type=jnp.float32)


def lanes_of(shape):
    return lax.broadcasted_iota(jnp.int32, shape, 1)


def make_masks(lens_ref, tile_rows, tile_cols):
    live = tile_rows * lax.axis_size("row") - lens_ref[lens_ref.shape[0] - 1]
    lane = lanes_of((1, 2 * tile_cols))
    upper = (lane >= tile_cols).astype(jnp.int32)
    place = lane - tile_cols * upper
    row, col = lax.axis_index("row"), lax.axis_index("col")
    keeps = [(place + (col ^ dx) * tile_cols < live).astype(jnp.float32) for dx in (0, 1)]
    pairs = [
        ((row ^ d) * tile_rows + first + upper < live).astype(jnp.float32) * keeps[0]
        for d in (0, OWNERS // 2)
        for first in range(0, tile_rows, 2)
    ]
    count = jnp.full(lane.shape, live * live, jnp.int32).astype(jnp.float32)
    return pairs, keeps, 1.0 / count


def turn(w_refs, turned):
    channels = w_refs[0].shape[0]
    share = channels // OWNERS
    half = share // 2
    for at, w_ref in enumerate(w_refs):
        w = w_ref[...].astype(jnp.float32).T
        blocks = [
            w[o * share + g * half : o * share + (g + 1) * half] for g in (0, 1) for o in range(OWNERS)
        ]
        turned[at * channels : (at + 1) * channels] = jnp.concatenate(blocks, 0).astype(jnp.bfloat16)


def store_rows(held, first, value, tile_cols):
    packed = value.shape[0] // 2
    stride = held.shape[0] // packed
    a, b = value[:packed], value[packed:]
    low = lanes_of(a.shape) < tile_cols
    held[pl.ds(first, packed, stride=stride), :] = jnp.where(low, a, pltpu.roll(b, tile_cols, 1))
    held[pl.ds(first + 1, packed, stride=stride), :] = jnp.where(low, pltpu.roll(a, tile_cols, 1), b)


def chip_rows(turned, mine):
    size = mine.shape[0] // (turned.shape[0] // mine.shape[1]) // 2
    pair = owner_place() // 2
    for at in range(mine.shape[0] // size):
        start = pl.multiple_of(at * (mine.shape[1] // 2) + pair * size, size)
        mine[at * size : (at + 1) * size] = turned[pl.ds(start, size), :]


def owner_place():
    return lax.axis_index("row") % OWNERS


def owner_block(held, d, size):
    at = pl.multiple_of((owner_place() ^ d) * size, size)
    return held[pl.ds(at, size)].astype(jnp.bfloat16)


def core_block(held, d, size):
    at = pl.multiple_of((owner_place() % 2 ^ d) * size, size)
    return held[pl.ds(at, size)].astype(jnp.bfloat16)


def norm_kernel(x_ref, normed_ref):
    x = x_ref[...].astype(jnp.float32).reshape(normed_ref.shape)
    normed_ref[...] = layer_norm(x, -1).astype(jnp.bfloat16)


def right_kernel(normed_ref, w_ref, g_ref, stay_ref, move_ref, turned, held):
    channels = normed_ref.shape[1]
    width = held.shape[1]
    turn((w_ref, g_ref), turned)
    for at in range(normed_ref.shape[0] // width):
        flat = nt_dot(turned[...], normed_ref[at * width : (at + 1) * width])
        store_rows(held, 2 * at, sigmoid(flat[channels:]) * flat[:channels], width // 2)
    size = stay_ref.shape[0] // 2
    for d, ref in enumerate((stay_ref, stay_ref, move_ref, move_ref)):
        ref[d % 2 * size : (d % 2 + 1) * size] = owner_block(held, d, size)


def left_kernel(lens_ref, normed_ref, w_ref, g_ref, stay_ref, own_ref, core_ref, masks_ref, *refs):
    turned, mine, held = refs
    width = held.shape[1]
    half = mine.shape[0] // 2
    pairs, keeps, share = make_masks(lens_ref, 2 * normed_ref.shape[0] // width, width // 2)
    masks_ref[...] = jnp.concatenate(
        pairs + keeps + [share] * (masks_ref.shape[0] - len(pairs) - len(keeps)), 0
    )
    turn((w_ref, g_ref), turned)
    chip_rows(turned, mine)
    for at in range(normed_ref.shape[0] // width):
        flat = nt_dot(mine[...], normed_ref[at * width : (at + 1) * width])
        store_rows(held, 2 * at, sigmoid(flat[half:]) * flat[:half] * pairs[at], width // 2)
    size = stay_ref.shape[0] // 2
    for d, ref in enumerate((own_ref, core_ref)):
        ref[:size] = core_block(held, d, size)
        ref[size:] = stay_ref[d * size : (d + 1) * size]


def near_kernel(masks_ref, x_ref, lw_ref, lg_ref, rw_ref, rg_ref, near_ref, over_ref, *refs):
    turned, mine, held_left, held_right = refs
    tile_rows, tile_cols, channels = x_ref.shape
    share = mine.shape[0] // 4
    turn((lw_ref, lg_ref, rw_ref, rg_ref), turned)
    chip_rows(turned, mine)
    for first in range(0, tile_rows, 2):
        x = x_ref[first : first + 2].astype(jnp.float32).reshape(2 * tile_cols, channels)
        flat = nt_dot(mine[...], layer_norm(x, -1).astype(jnp.bfloat16))
        lv, lg, rv, rg = [flat[at * share : (at + 1) * share] for at in range(4)]
        line = (tile_rows + first) // 2
        store_rows(held_left, first, sigmoid(lg) * lv * masks_ref[line : line + 1], tile_cols)
        store_rows(held_right, first, sigmoid(rg) * rv, tile_cols)
    size = near_ref.shape[0] // 2
    for d, ref in enumerate((near_ref, over_ref)):
        ref[:size] = core_block(held_left, d, size)
        ref[size:] = core_block(held_right, d, size)


def pack_kernel(far_ref, cross_ref, ready_ref, out_ref):
    del ready_ref
    size = out_ref.shape[0] // 2
    out_ref[:size] = far_ref[size:]
    out_ref[size:] = cross_ref[size:]


def gate_kernel(x_ref, normed_ref, gw_ref, ow_ref, dw_ref, gate_ref, x_turned_ref, ow_turned, dw_turned):
    tile_rows, tile_cols, channels = x_ref.shape
    share = channels // OWNERS
    half = share // 2
    blocks = [
        ow_ref[o * share + g * half : o * share + (g + 1) * half].astype(jnp.float32)
        for g in (0, 1)
        for o in range(OWNERS)
    ]
    ow_turned[...] = jnp.concatenate(blocks, 0).T.astype(jnp.bfloat16)
    dw_turned[...] = dw_ref[...].astype(jnp.float32).T.astype(jnp.bfloat16)
    gate_turned = gw_ref[...].astype(jnp.float32).T.astype(jnp.bfloat16)
    for first in range(0, tile_rows, 2):
        at = slice(first * tile_cols, (first + 2) * tile_cols)
        gate_ref[:, at] = sigmoid(nt_dot(gate_turned, normed_ref[at]))
        x = x_ref[first : first + 2].astype(jnp.float32).reshape(2 * tile_cols, channels)
        x_turned_ref[:, at] = x.T


def tri_kernel(masks_ref, own, core, near, near_over, far, cross, both_over, *refs):
    outs, rights = refs[:-1], refs[-1]
    half, _, width = rights.shape
    size = own.shape[0] // 2
    tile_rows = size // half
    side = OWNERS * tile_rows
    me, col = lax.axis_index("row"), lax.axis_index("col")
    lefts = (own, core, near, near_over)
    pieces = (
        (0, own, size),
        (1, core, size),
        (2, near, size),
        (3, near_over, size),
        (4, far, 0),
        (5, both_over, 0),
        (6, cross, 0),
        (7, both_over, size),
    )
    for away, ref, start in pieces:
        at = pl.multiple_of((me ^ away) * tile_rows, tile_rows)
        for m in range(half):
            rights[m, pl.ds(at, tile_rows), :] = ref[
                start + m * tile_rows : start + (m + 1) * tile_rows
            ]
    low = lanes_of((side, width)) < width // 2
    first = masks_ref.shape[0] - tile_rows // 2
    keep = jnp.concatenate([masks_ref[first : first + 1], masks_ref[first + 1 : first + 2]], 1)
    for m in range(half):
        left = jnp.concatenate(
            [ref[m * tile_rows : (m + 1) * tile_rows] for ref in lefts], 0
        )
        pieces = []
        for dx in (0, 1):
            block = rights[m, pl.ds(pl.multiple_of((col ^ dx) * side, side), side), :]
            block = block.astype(jnp.float32)
            pieces += [jnp.where(low, block, 0.0), jnp.where(low, 0.0, block)]
        right = jnp.concatenate(pieces, 0).astype(jnp.bfloat16)
        product = (nt_dot(left, right) * keep).astype(jnp.bfloat16)
        for d in range(OWNERS):
            for dx in (0, 1):
                at = d % 2 * size + m * tile_rows
                outs[d // 2 * 2 + dx][at : at + tile_rows] = product[
                    d * tile_rows : (d + 1) * tile_rows, dx * width : (dx + 1) * width
                ]


def finish_kernel(masks_ref, x_ref, gate_ref, bins_ref, ow_ref, dw_ref, *refs):
    parts, overs = [
        [refs[first + DIAGONAL_FIRST.index(d)] for d in range(OWNERS)] for first in (0, OWNERS)
    ]
    out_ref, loss_ref, held = refs[2 * OWNERS :]
    channels = x_ref.shape[0]
    size, width = parts[0].shape[0] // 2, parts[0].shape[1]
    half = channels // 2 // OWNERS
    tile_rows, tile_cols = size // half, width // 2
    packed = OWNERS * half
    owner = owner_place()
    total = jnp.zeros((tile_rows, width), jnp.float32)
    for d in range(OWNERS):
        refs, at = ((parts, 0), (overs, size))[d % 2]
        a, b = [refs[d // 2 * 2 + dx][at : at + size].astype(jnp.float32) for dx in (0, 1)]
        block = a + b
        held[pl.ds(pl.multiple_of((owner ^ d) * size, size), size), :] = block
        total = total + jnp.sum(block.reshape(half, tile_rows, width), 0)
    average = (total + pltpu.roll(total, tile_cols, 1)) * (1.0 / channels)
    total = jnp.zeros((tile_rows, width), jnp.float32)
    for om in range(packed):
        centred = held[om * tile_rows : (om + 1) * tile_rows] - average
        total = total + centred * centred
    spread = (total + pltpu.roll(total, tile_cols, 1)) * (1.0 / channels)
    scale = lax.rsqrt(spread + 1e-05)
    low = lanes_of((packed, width)) < tile_cols
    bin_ids = lax.broadcasted_iota(jnp.int32, (dw_ref.shape[0], width), 0)
    loss = jnp.zeros((1, width), jnp.float32)
    for first in range(0, tile_rows, 2):
        a, b = [
            (held[pl.ds(ii, packed, stride=tile_rows), :] - average[ii : ii + 1]) * scale[ii : ii + 1]
            for ii in (first, first + 1)
        ]
        normed = jnp.concatenate(
            [
                jnp.where(low, a, pltpu.roll(b, tile_cols, 1)),
                jnp.where(low, pltpu.roll(a, tile_cols, 1), b),
            ],
            0,
        ).astype(jnp.bfloat16)
        update = jnp.dot(ow_ref[...], normed, preferred_element_type=jnp.float32)
        at = slice(first * tile_cols, (first + 2) * tile_cols)
        pair_out = (x_ref[:, at] + gate_ref[:, at] * update).astype(jnp.bfloat16)
        out_ref[:, at] = pair_out
        logits = jnp.dot(dw_ref[...], pair_out, preferred_element_type=jnp.float32)
        log_total = jnp.log(jnp.sum(jnp.exp(logits), axis=0, keepdims=True))
        bins = bins_ref[first // 2 : first // 2 + 1]
        picked = jnp.sum(jnp.where(bin_ids == bins, logits, 0.0), axis=0, keepdims=True)
        loss = loss + masks_ref[first // 2 : first // 2 + 1] * (log_total - picked)
    last = masks_ref.shape[0] - 1
    loss = jnp.sum(loss * masks_ref[last : last + 1], axis=1, keepdims=True)
    loss_ref[...] = jnp.broadcast_to(loss, loss_ref.shape)


def turn_back_kernel(turned_ref, out_ref):
    tile_rows, tile_cols, channels = out_ref.shape
    for first in range(0, tile_rows, 2):
        block = turned_ref[:, first * tile_cols : (first + 2) * tile_cols].astype(jnp.float32).T
        out_ref[first : first + 2] = block.astype(jnp.bfloat16).reshape(2, tile_cols, channels)


def exchange(value, places, mask):
    return lax.ppermute(value, AXES, [(at, at ^ mask) for at in range(places)])


def call(kernel, outs, scratch=(), specs=None, out_specs=None, args=(), flops=0):
    return pl.pallas_call(
        kernel,
        out_shape=outs,
        in_specs=specs if specs is not None else [VMEM] * len(args),
        out_specs=out_specs if out_specs is not None else jax.tree.map(lambda _: VMEM, outs),
        scratch_shapes=list(scratch),
        compiler_params=PARAMS,
        cost_estimate=pl.CostEstimate(flops=flops, bytes_accessed=1 << 20, transcendentals=1 << 18),
    )(*args)


def by_kernels(
    pair_repr,
    distance_bins,
    chain_lengths,
    left_weight,
    left_gate_weight,
    right_weight,
    right_gate_weight,
    out_weight,
    out_gate_weight,
    dist_weight,
):
    tile_rows, tile_cols, channels = pair_repr.shape
    rows, cols = lax.axis_size("row"), lax.axis_size("col")
    places = rows * cols
    width = 2 * tile_cols
    spots = tile_rows * tile_cols
    size = channels // OWNERS // 2 * tile_rows
    bf16, f32 = jnp.bfloat16, jnp.float32
    struct = jax.ShapeDtypeStruct
    turned = pltpu.VMEM((2 * channels, channels), bf16)
    held = pltpu.VMEM((OWNERS * size, width), f32)
    over_x, over_core, over_z, over_half = 1, cols, 2 * cols, OWNERS * cols
    near = exchange(pair_repr, places, over_z)
    normed = call(
        norm_kernel, struct((spots, channels), bf16), args=(pair_repr,), flops=1 << 30
    )
    stay, move = call(
        right_kernel,
        [struct((2 * size, width), bf16)] * 2,
        [turned, held],
        args=(normed, right_weight, right_gate_weight),
        flops=4 * spots * channels * channels,
    )
    cross = exchange(move, places, over_half + over_z)
    far = exchange(stay, places, over_half)
    block = struct((2 * size, width), bf16)
    own, core, masks = call(
        left_kernel,
        [block, block, struct((3 * tile_rows // 2, width), f32)],
        [turned, pltpu.VMEM((channels, channels), bf16), pltpu.VMEM((2 * size, width), f32)],
        [SMEM] + [VMEM] * 4,
        args=(chain_lengths, normed, left_weight, left_gate_weight, stay),
        flops=2 * spots * channels * channels,
    )
    near, near_over = call(
        near_kernel,
        [block, block],
        [
            pltpu.VMEM((4 * channels, channels), bf16),
            pltpu.VMEM((2 * channels, channels), bf16),
            pltpu.VMEM((2 * size, width), f32),
            pltpu.VMEM((2 * size, width), f32),
        ],
        args=(masks, near, left_weight, left_gate_weight, right_weight, right_gate_weight),
        flops=4 * spots * channels * channels,
    )
    near_over = exchange(near_over, places, over_core)
    core = exchange(core, places, over_core)
    both_over = call(
        pack_kernel,
        block,
        specs=[VMEM, VMEM, pl.BlockSpec(memory_space=pl.ANY)],
        args=(far, cross, near_over),
    )
    both_over = exchange(both_over, places, over_core)
    parts = call(
        tri_kernel,
        [struct((2 * size, width), bf16)] * OWNERS,
        [pltpu.VMEM((size // tile_rows, rows * tile_rows, width), bf16)],
        args=(masks, own, core, near, near_over, far, cross, both_over),
        flops=8 * size * 2 * tile_rows * 2 * width,
    )
    parts = [
        exchange(parts[d], places, d // 2 * over_z + d % 2 * over_x) if d else parts[0] for d in DIAGONAL_FIRST
    ]
    parts += [exchange(value, places, over_core) for value in parts]
    gate, x_turned, out_turned, dist_turned = call(
        gate_kernel,
        [
            struct((channels, spots), f32),
            struct((channels, spots), f32),
            struct((channels, channels), bf16),
            struct(dist_weight.shape[::-1], bf16),
        ],
        args=(pair_repr, normed, out_gate_weight, out_weight, dist_weight),
        flops=2 * spots * channels * channels,
    )
    pair_out, loss = call(
        finish_kernel,
        [struct((channels, spots), bf16), struct((8, 128), f32)],
        [held],
        args=(
            masks,
            x_turned,
            gate,
            distance_bins.reshape(tile_rows // 2, width),
            out_turned,
            dist_turned,
            *parts,
        ),
        flops=6 * spots * channels * channels,
    )
    pair_out = call(turn_back_kernel, struct(pair_repr.shape, bf16), args=(pair_out,), flops=1 << 26)
    beside, beside_over, sibling = [
        exchange(loss, places, mask) for mask in (over_x, over_x + over_core, over_core)
    ]
    loss = (beside + beside_over) + (sibling + loss)
    cross_loss, half, near_loss = [
        exchange(loss, places, mask) for mask in (over_half + over_z, over_half, over_z)
    ]
    loss = (cross_loss + half) + (near_loss + loss)
    return (pair_out, loss[0, :1])


def by_all_to_all(
    pair_repr,
    distance_bins,
    chain_lengths,
    left_weight,
    left_gate_weight,
    right_weight,
    right_gate_weight,
    out_weight,
    out_gate_weight,
    dist_weight,
):
    tile_rows, tile_cols, channels = pair_repr.shape
    rows, cols = lax.axis_size("row"), lax.axis_size("col")
    peers = rows * cols
    share = channels // peers
    residues = tile_rows * rows
    spots = tile_rows * tile_cols
    live_count = residues - chain_lengths[chain_lengths.shape[0] - 1]
    row_place = lax.axis_index("row") * tile_rows + jnp.arange(tile_rows, dtype=jnp.int32)
    col_place = lax.axis_index("col") * tile_cols + jnp.arange(tile_cols, dtype=jnp.int32)
    live_rows = (row_place < live_count).astype(jnp.float32)
    live_cols = (col_place < live_count).astype(jnp.float32)
    flat_mask = (live_rows[:, None] * live_cols[None, :]).reshape(-1)
    normed = layer_norm(pair_repr.astype(jnp.float32), -1).astype(jnp.bfloat16)
    normed = normed.reshape(spots, channels)

    def project_turned(weight):
        return lax.dot_general(
            weight, normed, (((0,), (1,)), ((), ())), preferred_element_type=jnp.float32
        )

    def gated(gate_weight, weight):
        values = jax.nn.sigmoid(project_turned(gate_weight)) * project_turned(weight)
        return (values * flat_mask[None, :]).astype(jnp.bfloat16)

    left = gated(left_gate_weight, left_weight).reshape(peers, share, tile_rows, tile_cols)
    right = gated(right_gate_weight, right_weight).reshape(peers, share, tile_rows, tile_cols)
    both = jnp.concatenate([left, right], axis=3).reshape(peers, share * tile_rows, 2 * tile_cols)
    owned = lax.all_to_all(both, AXES, split_axis=0, concat_axis=0, tiled=True)
    owned = owned.reshape(rows, cols, share, tile_rows, 2, tile_cols)
    owned = owned.transpose(4, 2, 0, 3, 1, 5).reshape(2, share, residues, residues)
    tri = jnp.einsum(
        "cik,cjk->cij", owned[0], owned[1], preferred_element_type=jnp.float32
    ).astype(jnp.bfloat16)
    tri = tri.reshape(share, rows, tile_rows, cols, tile_cols).transpose(1, 3, 0, 2, 4)
    tri = tri.reshape(peers, share, spots)
    tri = lax.all_to_all(tri, AXES, split_axis=0, concat_axis=0, tiled=True)
    tri = tri.reshape(channels, spots).astype(jnp.float32)
    tri_normed = layer_norm(tri, 0).astype(jnp.bfloat16)
    out_gate = jax.nn.sigmoid(jnp.dot(normed, out_gate_weight, preferred_element_type=jnp.float32))
    update = out_gate * tn_dot(tri_normed, out_weight)
    pair_out = (pair_repr.astype(jnp.float32).reshape(spots, channels) + update).astype(
        jnp.bfloat16
    )
    logits = jnp.dot(pair_out, dist_weight, preferred_element_type=jnp.float32)
    log_total = jnp.log(jnp.sum(jnp.exp(logits), axis=-1))
    bin_ids = jnp.arange(logits.shape[1], dtype=jnp.int32)
    picked = jnp.sum(
        jnp.where(bin_ids[None, :] == distance_bins.reshape(-1, 1), logits, 0.0), axis=-1
    )
    loss_sum = jnp.sum(flat_mask * (log_total - picked))
    sums = lax.all_to_all(
        jnp.full((peers, 1, 128), loss_sum), AXES, split_axis=0, concat_axis=0, tiled=True
    )
    pair_count = (live_count * live_count).astype(jnp.float32)
    loss_value = (jnp.sum(sums[:, 0, 0]) / pair_count).reshape(1)
    return (pair_out.reshape(pair_repr.shape), loss_value)


def on_device(pair_repr, *others):
    tile_rows, tile_cols, channels = pair_repr.shape
    rows, cols = lax.axis_size("row"), lax.axis_size("col")
    fits = (
        rows == 2 * OWNERS
        and cols == 2
        and tile_rows * rows == tile_cols * cols
        and 2 * tile_cols == 128
        and tile_rows == 16
        and channels == 32 * OWNERS
    )
    return (by_kernels if fits else by_all_to_all)(pair_repr, *others)


def solution(mesh):
    in_specs = (
        P(("groups", "row"), "col", None),
        P(("groups", "row"), "col"),
        P("groups"),
        P(),
        P(),
        P(),
        P(),
        P(),
        P(),
        P(),
    )
    out_specs = (P(("groups", "row"), "col", None), P("groups"))
    return jax.shard_map(
        on_device, mesh=mesh, in_specs=in_specs, out_specs=out_specs, check_vma=False
    )
```

```python
import jax
import jax.numpy as jnp
from jax import lax
from jax.experimental import pallas as pl
from jax.experimental.pallas import tpu as pltpu
from jax.sharding import PartitionSpec as P

AXES = ("row", "col")
OWNERS = 4
DIAGONAL_FIRST = (0, 3, 2, 1)
VMEM = pl.BlockSpec(memory_space=pltpu.VMEM)
SMEM = pl.BlockSpec(memory_space=pltpu.SMEM)
PARAMS = pltpu.CompilerParams(vmem_limit_bytes=24 * 1024 * 1024)


def layer_norm(values, axis):
    average = jnp.mean(values, axis=axis, keepdims=True)
    centred = values - average
    spread = jnp.mean(centred * centred, axis=axis, keepdims=True)
    return centred * lax.rsqrt(spread + 1e-05)


def sigmoid(values):
    return 0.5 * jnp.tanh(0.5 * values) + 0.5


def nt_dot(a, b):
    return lax.dot_general(a, b, (((1,), (1,)), ((), ())), preferred_element_type=jnp.float32)


def tn_dot(a, b):
    return lax.dot_general(a, b, (((0,), (0,)), ((), ())), preferred_element_type=jnp.float32)


def lanes_of(shape):
    return lax.broadcasted_iota(jnp.int32, shape, 1)


def make_masks(lens_ref, tile_rows, tile_cols):
    live = tile_rows * lax.axis_size("row") - lens_ref[lens_ref.shape[0] - 1]
    lane = lanes_of((1, 2 * tile_cols))
    upper = (lane >= tile_cols).astype(jnp.int32)
    place = lane - tile_cols * upper
    row, col = lax.axis_index("row"), lax.axis_index("col")
    keeps = [(place + (col ^ dx) * tile_cols < live).astype(jnp.float32) for dx in (0, 1)]
    pairs = [
        ((row ^ d) * tile_rows + first + upper < live).astype(jnp.float32) * keeps[0]
        for d in (0, OWNERS // 2)
        for first in range(0, tile_rows, 2)
    ]
    count = jnp.full(lane.shape, live * live, jnp.int32).astype(jnp.float32)
    return pairs, keeps, 1.0 / count


def turn(w_refs, turned):
    channels = w_refs[0].shape[0]
    share = channels // OWNERS
    half = share // 2
    for at, w_ref in enumerate(w_refs):
        w = w_ref[...].astype(jnp.float32).T
        blocks = [
            w[o * share + g * half : o * share + (g + 1) * half] for g in (0, 1) for o in range(OWNERS)
        ]
        turned[at * channels : (at + 1) * channels] = jnp.concatenate(blocks, 0).astype(jnp.bfloat16)


def store_rows(held, first, value, tile_cols):
    packed = value.shape[0] // 2
    stride = held.shape[0] // packed
    a, b = value[:packed], value[packed:]
    low = lanes_of(a.shape) < tile_cols
    held[pl.ds(first, packed, stride=stride), :] = jnp.where(low, a, pltpu.roll(b, tile_cols, 1))
    held[pl.ds(first + 1, packed, stride=stride), :] = jnp.where(low, pltpu.roll(a, tile_cols, 1), b)


def chip_rows(turned, mine):
    size = mine.shape[0] // (turned.shape[0] // mine.shape[1]) // 2
    pair = owner_place() // 2
    for at in range(mine.shape[0] // size):
        start = pl.multiple_of(at * (mine.shape[1] // 2) + pair * size, size)
        mine[at * size : (at + 1) * size] = turned[pl.ds(start, size), :]


def owner_place():
    return lax.axis_index("row") % OWNERS


def owner_block(held, d, size):
    at = pl.multiple_of((owner_place() ^ d) * size, size)
    return held[pl.ds(at, size)].astype(jnp.bfloat16)


def core_block(held, d, size):
    at = pl.multiple_of((owner_place() % 2 ^ d) * size, size)
    return held[pl.ds(at, size)].astype(jnp.bfloat16)


def norm_kernel(x_ref, normed_ref):
    x = x_ref[...].astype(jnp.float32).reshape(normed_ref.shape)
    normed_ref[...] = layer_norm(x, -1).astype(jnp.bfloat16)


def right_kernel(normed_ref, w_ref, g_ref, stay_ref, move_ref, turned, held):
    channels = normed_ref.shape[1]
    width = held.shape[1]
    turn((w_ref, g_ref), turned)
    for at in range(normed_ref.shape[0] // width):
        flat = nt_dot(turned[...], normed_ref[at * width : (at + 1) * width])
        store_rows(held, 2 * at, sigmoid(flat[channels:]) * flat[:channels], width // 2)
    size = stay_ref.shape[0] // 2
    for d, ref in enumerate((stay_ref, stay_ref, move_ref, move_ref)):
        ref[d % 2 * size : (d % 2 + 1) * size] = owner_block(held, d, size)


def left_kernel(lens_ref, normed_ref, w_ref, g_ref, stay_ref, own_ref, core_ref, masks_ref, *refs):
    turned, mine, held = refs
    width = held.shape[1]
    half = mine.shape[0] // 2
    pairs, keeps, share = make_masks(lens_ref, 2 * normed_ref.shape[0] // width, width // 2)
    masks_ref[...] = jnp.concatenate(
        pairs + keeps + [share] * (masks_ref.shape[0] - len(pairs) - len(keeps)), 0
    )
    turn((w_ref, g_ref), turned)
    chip_rows(turned, mine)
    for at in range(normed_ref.shape[0] // width):
        flat = nt_dot(mine[...], normed_ref[at * width : (at + 1) * width])
        store_rows(held, 2 * at, sigmoid(flat[half:]) * flat[:half] * pairs[at], width // 2)
    size = stay_ref.shape[0] // 2
    for d, ref in enumerate((own_ref, core_ref)):
        ref[:size] = core_block(held, d, size)
        ref[size:] = stay_ref[d * size : (d + 1) * size]


def near_kernel(masks_ref, x_ref, lw_ref, lg_ref, rw_ref, rg_ref, near_ref, over_ref, *refs):
    turned, mine, held_left, held_right = refs
    tile_rows, tile_cols, channels = x_ref.shape
    share = mine.shape[0] // 4
    turn((lw_ref, lg_ref, rw_ref, rg_ref), turned)
    chip_rows(turned, mine)
    for first in range(0, tile_rows, 2):
        x = x_ref[first : first + 2].astype(jnp.float32).reshape(2 * tile_cols, channels)
        flat = nt_dot(mine[...], layer_norm(x, -1).astype(jnp.bfloat16))
        lv, lg, rv, rg = [flat[at * share : (at + 1) * share] for at in range(4)]
        line = (tile_rows + first) // 2
        store_rows(held_left, first, sigmoid(lg) * lv * masks_ref[line : line + 1], tile_cols)
        store_rows(held_right, first, sigmoid(rg) * rv, tile_cols)
    size = near_ref.shape[0] // 2
    for d, ref in enumerate((near_ref, over_ref)):
        ref[:size] = core_block(held_left, d, size)
        ref[size:] = core_block(held_right, d, size)


def pack_kernel(far_ref, cross_ref, ready_ref, out_ref):
    del ready_ref
    size = out_ref.shape[0] // 2
    out_ref[:size] = far_ref[size:]
    out_ref[size:] = cross_ref[size:]


def gate_kernel(x_ref, normed_ref, gw_ref, ow_ref, dw_ref, gate_ref, x_turned_ref, ow_turned, dw_turned):
    tile_rows, tile_cols, channels = x_ref.shape
    share = channels // OWNERS
    half = share // 2
    blocks = [
        ow_ref[o * share + g * half : o * share + (g + 1) * half].astype(jnp.float32)
        for g in (0, 1)
        for o in range(OWNERS)
    ]
    ow_turned[...] = jnp.concatenate(blocks, 0).T.astype(jnp.bfloat16)
    dw_turned[...] = dw_ref[...].astype(jnp.float32).T.astype(jnp.bfloat16)
    gate_turned = gw_ref[...].astype(jnp.float32).T.astype(jnp.bfloat16)
    for first in range(0, tile_rows, 2):
        at = slice(first * tile_cols, (first + 2) * tile_cols)
        gate_ref[:, at] = sigmoid(nt_dot(gate_turned, normed_ref[at]))
        x = x_ref[first : first + 2].astype(jnp.float32).reshape(2 * tile_cols, channels)
        x_turned_ref[:, at] = x.T


def tri_kernel(masks_ref, own, core, near, near_over, far, cross, both_over, *refs):
    outs, rights = refs[:-1], refs[-1]
    half, _, width = rights.shape
    size = own.shape[0] // 2
    tile_rows = size // half
    side = OWNERS * tile_rows
    me, col = lax.axis_index("row"), lax.axis_index("col")
    lefts = (own, core, near, near_over)
    pieces = (
        (0, own, size),
        (1, core, size),
        (2, near, size),
        (3, near_over, size),
        (4, far, 0),
        (5, both_over, 0),
        (6, cross, 0),
        (7, both_over, size),
    )
    for away, ref, start in pieces:
        at = pl.multiple_of((me ^ away) * tile_rows, tile_rows)
        for m in range(half):
            rights[m, pl.ds(at, tile_rows), :] = ref[
                start + m * tile_rows : start + (m + 1) * tile_rows
            ]
    low = lanes_of((side, width)) < width // 2
    first = masks_ref.shape[0] - tile_rows // 2
    keep = jnp.concatenate([masks_ref[first : first + 1], masks_ref[first + 1 : first + 2]], 1)
    for m in range(half):
        left = jnp.concatenate(
            [ref[m * tile_rows : (m + 1) * tile_rows] for ref in lefts], 0
        )
        pieces = []
        for dx in (0, 1):
            block = rights[m, pl.ds(pl.multiple_of((col ^ dx) * side, side), side), :]
            block = block.astype(jnp.float32)
            pieces += [jnp.where(low, block, 0.0), jnp.where(low, 0.0, block)]
        right = jnp.concatenate(pieces, 0).astype(jnp.bfloat16)
        product = (nt_dot(left, right) * keep).astype(jnp.bfloat16)
        for d in range(OWNERS):
            for dx in (0, 1):
                at = d % 2 * size + m * tile_rows
                outs[d // 2 * 2 + dx][at : at + tile_rows] = product[
                    d * tile_rows : (d + 1) * tile_rows, dx * width : (dx + 1) * width
                ]


def finish_kernel(masks_ref, x_ref, gate_ref, bins_ref, ow_ref, dw_ref, *refs):
    parts, overs = [
        [refs[first + DIAGONAL_FIRST.index(d)] for d in range(OWNERS)] for first in (0, OWNERS)
    ]
    out_ref, loss_ref, held = refs[2 * OWNERS :]
    channels = x_ref.shape[0]
    size, width = parts[0].shape[0] // 2, parts[0].shape[1]
    half = channels // 2 // OWNERS
    tile_rows, tile_cols = size // half, width // 2
    packed = OWNERS * half
    owner = owner_place()
    total = jnp.zeros((tile_rows, width), jnp.float32)
    for d in range(OWNERS):
        refs, at = ((parts, 0), (overs, size))[d % 2]
        a, b = [refs[d // 2 * 2 + dx][at : at + size].astype(jnp.float32) for dx in (0, 1)]
        block = a + b
        held[pl.ds(pl.multiple_of((owner ^ d) * size, size), size), :] = block
        total = total + jnp.sum(block.reshape(half, tile_rows, width), 0)
    average = (total + pltpu.roll(total, tile_cols, 1)) * (1.0 / channels)
    total = jnp.zeros((tile_rows, width), jnp.float32)
    for om in range(packed):
        centred = held[om * tile_rows : (om + 1) * tile_rows] - average
        total = total + centred * centred
    spread = (total + pltpu.roll(total, tile_cols, 1)) * (1.0 / channels)
    scale = lax.rsqrt(spread + 1e-05)
    low = lanes_of((packed, width)) < tile_cols
    bin_ids = lax.broadcasted_iota(jnp.int32, (dw_ref.shape[0], width), 0)
    loss = jnp.zeros((1, width), jnp.float32)
    for first in range(0, tile_rows, 2):
        a, b = [
            (held[pl.ds(ii, packed, stride=tile_rows), :] - average[ii : ii + 1]) * scale[ii : ii + 1]
            for ii in (first, first + 1)
        ]
        normed = jnp.concatenate(
            [
                jnp.where(low, a, pltpu.roll(b, tile_cols, 1)),
                jnp.where(low, pltpu.roll(a, tile_cols, 1), b),
            ],
            0,
        ).astype(jnp.bfloat16)
        update = jnp.dot(ow_ref[...], normed, preferred_element_type=jnp.float32)
        at = slice(first * tile_cols, (first + 2) * tile_cols)
        pair_out = (x_ref[:, at] + gate_ref[:, at] * update).astype(jnp.bfloat16)
        out_ref[:, at] = pair_out
        logits = jnp.dot(dw_ref[...], pair_out, preferred_element_type=jnp.float32)
        log_total = jnp.log(jnp.sum(jnp.exp(logits), axis=0, keepdims=True))
        bins = bins_ref[first // 2 : first // 2 + 1]
        picked = jnp.sum(jnp.where(bin_ids == bins, logits, 0.0), axis=0, keepdims=True)
        loss = loss + masks_ref[first // 2 : first // 2 + 1] * (log_total - picked)
    last = masks_ref.shape[0] - 1
    loss = jnp.sum(loss * masks_ref[last : last + 1], axis=1, keepdims=True)
    loss_ref[...] = jnp.broadcast_to(loss, loss_ref.shape)


def turn_back_kernel(turned_ref, out_ref):
    tile_rows, tile_cols, channels = out_ref.shape
    for first in range(0, tile_rows, 2):
        block = turned_ref[:, first * tile_cols : (first + 2) * tile_cols].astype(jnp.float32).T
        out_ref[first : first + 2] = block.astype(jnp.bfloat16).reshape(2, tile_cols, channels)


def exchange(value, places, mask):
    return lax.ppermute(value, AXES, [(at, at ^ mask) for at in range(places)])


def call(kernel, outs, scratch=(), specs=None, out_specs=None, args=(), flops=0):
    return pl.pallas_call(
        kernel,
        out_shape=outs,
        in_specs=specs if specs is not None else [VMEM] * len(args),
        out_specs=out_specs if out_specs is not None else jax.tree.map(lambda _: VMEM, outs),
        scratch_shapes=list(scratch),
        compiler_params=PARAMS,
        cost_estimate=pl.CostEstimate(flops=flops, bytes_accessed=1 << 20, transcendentals=1 << 18),
    )(*args)


def by_kernels(
    pair_repr,
    distance_bins,
    chain_lengths,
    left_weight,
    left_gate_weight,
    right_weight,
    right_gate_weight,
    out_weight,
    out_gate_weight,
    dist_weight,
):
    tile_rows, tile_cols, channels = pair_repr.shape
    rows, cols = lax.axis_size("row"), lax.axis_size("col")
    places = rows * cols
    width = 2 * tile_cols
    spots = tile_rows * tile_cols
    size = channels // OWNERS // 2 * tile_rows
    bf16, f32 = jnp.bfloat16, jnp.float32
    struct = jax.ShapeDtypeStruct
    turned = pltpu.VMEM((2 * channels, channels), bf16)
    held = pltpu.VMEM((OWNERS * size, width), f32)
    over_x, over_core, over_z, over_half = 1, cols, 2 * cols, OWNERS * cols
    near = exchange(pair_repr, places, over_z)
    normed = call(
        norm_kernel, struct((spots, channels), bf16), args=(pair_repr,), flops=1 << 30
    )
    stay, move = call(
        right_kernel,
        [struct((2 * size, width), bf16)] * 2,
        [turned, held],
        args=(normed, right_weight, right_gate_weight),
        flops=4 * spots * channels * channels,
    )
    cross = exchange(move, places, over_half + over_z)
    far = exchange(stay, places, over_half)
    block = struct((2 * size, width), bf16)
    own, core, masks = call(
        left_kernel,
        [block, block, struct((3 * tile_rows // 2, width), f32)],
        [turned, pltpu.VMEM((channels, channels), bf16), pltpu.VMEM((2 * size, width), f32)],
        [SMEM] + [VMEM] * 4,
        args=(chain_lengths, normed, left_weight, left_gate_weight, stay),
        flops=2 * spots * channels * channels,
    )
    near, near_over = call(
        near_kernel,
        [block, block],
        [
            pltpu.VMEM((4 * channels, channels), bf16),
            pltpu.VMEM((2 * channels, channels), bf16),
            pltpu.VMEM((2 * size, width), f32),
            pltpu.VMEM((2 * size, width), f32),
        ],
        args=(masks, near, left_weight, left_gate_weight, right_weight, right_gate_weight),
        flops=4 * spots * channels * channels,
    )
    near_over = exchange(near_over, places, over_core)
    core = exchange(core, places, over_core)
    both_over = call(
        pack_kernel,
        block,
        specs=[VMEM, VMEM, pl.BlockSpec(memory_space=pl.ANY)],
        args=(far, cross, near_over),
    )
    both_over = exchange(both_over, places, over_core)
    parts = call(
        tri_kernel,
        [struct((2 * size, width), bf16)] * OWNERS,
        [pltpu.VMEM((size // tile_rows, rows * tile_rows, width), bf16)],
        args=(masks, own, core, near, near_over, far, cross, both_over),
        flops=8 * size * 2 * tile_rows * 2 * width,
    )
    parts = [
        exchange(parts[d], places, d // 2 * over_z + d % 2 * over_x) if d else parts[0] for d in DIAGONAL_FIRST
    ]
    parts += [exchange(value, places, over_core) for value in parts]
    gate, x_turned, out_turned, dist_turned = call(
        gate_kernel,
        [
            struct((channels, spots), f32),
            struct((channels, spots), f32),
            struct((channels, channels), bf16),
            struct(dist_weight.shape[::-1], bf16),
        ],
        args=(pair_repr, normed, out_gate_weight, out_weight, dist_weight),
        flops=2 * spots * channels * channels,
    )
    pair_out, loss = call(
        finish_kernel,
        [struct((channels, spots), bf16), struct((8, 128), f32)],
        [held],
        args=(
            masks,
            x_turned,
            gate,
            distance_bins.reshape(tile_rows // 2, width),
            out_turned,
            dist_turned,
            *parts,
        ),
        flops=6 * spots * channels * channels,
    )
    pair_out = call(turn_back_kernel, struct(pair_repr.shape, bf16), args=(pair_out,), flops=1 << 26)
    beside_over, beside, sibling = [
        exchange(loss, places, mask) for mask in (over_x + over_core, over_x, over_core)
    ]
    loss = (beside_over + beside) + (sibling + loss)
    cross_loss, half, near_loss = [
        exchange(loss, places, mask) for mask in (over_half + over_z, over_half, over_z)
    ]
    loss = (cross_loss + half) + (near_loss + loss)
    return (pair_out, loss[0, :1])


def by_all_to_all(
    pair_repr,
    distance_bins,
    chain_lengths,
    left_weight,
    left_gate_weight,
    right_weight,
    right_gate_weight,
    out_weight,
    out_gate_weight,
    dist_weight,
):
    tile_rows, tile_cols, channels = pair_repr.shape
    rows, cols = lax.axis_size("row"), lax.axis_size("col")
    peers = rows * cols
    share = channels // peers
    residues = tile_rows * rows
    spots = tile_rows * tile_cols
    live_count = residues - chain_lengths[chain_lengths.shape[0] - 1]
    row_place = lax.axis_index("row") * tile_rows + jnp.arange(tile_rows, dtype=jnp.int32)
    col_place = lax.axis_index("col") * tile_cols + jnp.arange(tile_cols, dtype=jnp.int32)
    live_rows = (row_place < live_count).astype(jnp.float32)
    live_cols = (col_place < live_count).astype(jnp.float32)
    flat_mask = (live_rows[:, None] * live_cols[None, :]).reshape(-1)
    normed = layer_norm(pair_repr.astype(jnp.float32), -1).astype(jnp.bfloat16)
    normed = normed.reshape(spots, channels)

    def project_turned(weight):
        return lax.dot_general(
            weight, normed, (((0,), (1,)), ((), ())), preferred_element_type=jnp.float32
        )

    def gated(gate_weight, weight):
        values = jax.nn.sigmoid(project_turned(gate_weight)) * project_turned(weight)
        return (values * flat_mask[None, :]).astype(jnp.bfloat16)

    left = gated(left_gate_weight, left_weight).reshape(peers, share, tile_rows, tile_cols)
    right = gated(right_gate_weight, right_weight).reshape(peers, share, tile_rows, tile_cols)
    both = jnp.concatenate([left, right], axis=3).reshape(peers, share * tile_rows, 2 * tile_cols)
    owned = lax.all_to_all(both, AXES, split_axis=0, concat_axis=0, tiled=True)
    owned = owned.reshape(rows, cols, share, tile_rows, 2, tile_cols)
    owned = owned.transpose(4, 2, 0, 3, 1, 5).reshape(2, share, residues, residues)
    tri = jnp.einsum(
        "cik,cjk->cij", owned[0], owned[1], preferred_element_type=jnp.float32
    ).astype(jnp.bfloat16)
    tri = tri.reshape(share, rows, tile_rows, cols, tile_cols).transpose(1, 3, 0, 2, 4)
    tri = tri.reshape(peers, share, spots)
    tri = lax.all_to_all(tri, AXES, split_axis=0, concat_axis=0, tiled=True)
    tri = tri.reshape(channels, spots).astype(jnp.float32)
    tri_normed = layer_norm(tri, 0).astype(jnp.bfloat16)
    out_gate = jax.nn.sigmoid(jnp.dot(normed, out_gate_weight, preferred_element_type=jnp.float32))
    update = out_gate * tn_dot(tri_normed, out_weight)
    pair_out = (pair_repr.astype(jnp.float32).reshape(spots, channels) + update).astype(
        jnp.bfloat16
    )
    logits = jnp.dot(pair_out, dist_weight, preferred_element_type=jnp.float32)
    log_total = jnp.log(jnp.sum(jnp.exp(logits), axis=-1))
    bin_ids = jnp.arange(logits.shape[1], dtype=jnp.int32)
    picked = jnp.sum(
        jnp.where(bin_ids[None, :] == distance_bins.reshape(-1, 1), logits, 0.0), axis=-1
    )
    loss_sum = jnp.sum(flat_mask * (log_total - picked))
    sums = lax.all_to_all(
        jnp.full((peers, 1, 128), loss_sum), AXES, split_axis=0, concat_axis=0, tiled=True
    )
    pair_count = (live_count * live_count).astype(jnp.float32)
    loss_value = (jnp.sum(sums[:, 0, 0]) / pair_count).reshape(1)
    return (pair_out.reshape(pair_repr.shape), loss_value)


def on_device(pair_repr, *others):
    tile_rows, tile_cols, channels = pair_repr.shape
    rows, cols = lax.axis_size("row"), lax.axis_size("col")
    fits = (
        rows == 2 * OWNERS
        and cols == 2
        and tile_rows * rows == tile_cols * cols
        and 2 * tile_cols == 128
        and tile_rows == 16
        and channels == 32 * OWNERS
    )
    return (by_kernels if fits else by_all_to_all)(pair_repr, *others)


def solution(mesh):
    in_specs = (
        P(("groups", "row"), "col", None),
        P(("groups", "row"), "col"),
        P("groups"),
        P(),
        P(),
        P(),
        P(),
        P(),
        P(),
        P(),
    )
    out_specs = (P(("groups", "row"), "col", None), P("groups"))
    return jax.shard_map(
        on_device, mesh=mesh, in_specs=in_specs, out_specs=out_specs, check_vma=False
    )
```
